32 devices in a mesh: tok: 16 (over z, y, core), head: 2 (over x).
Axes of the slice: x: 2, y: 2, z: 4, core: 2. Of those that a mesh axis runs over, the one named last changes fastest.
Arguments:
- hidden: bfloat16 [512, 2048], P('tok', 'head'), may hold values from -24 to 24
- attn_gain: float32 [2048], replicated, may hold values from 0.1 to 1.9
- w_query: bfloat16 [2048, 3072], P(None, 'head'), may hold values from -0.125 to 0.125
- w_latent: bfloat16 [2048, 576], P('head'), may hold values from -0.125 to 0.125
- w_key_up: bfloat16 [16, 128, 512], P('head'), may hold values from -0.5 to 0.5
- w_value_up: bfloat16 [16, 512, 128], P('head'), may hold values from -1 to 1
- w_out: bfloat16 [2048, 2048], P('head'), may hold values from -0.125 to 0.125
- latent_cache: bfloat16 [159744, 576], P(('tok', 'head')), may hold values from -6 to 6
- cache_lengths: int32 [512], P('tok'), may hold values from 144 to 2048, as said below
- request_slot: int32 [512], P('tok'), may hold values from 0 to 511, as said below
- ffn_gain: float32 [2048], P('head'), may hold values from 0.1 to 1.9
- w_router: bfloat16 [2048, 16], P('head'), may hold values from -0.25 to 0.25
- routes: int32 [512, 6], P('tok'), may hold values from 0 to 15, all different within a row; in each aligned block of 32 rows (0 to 31, 32 to 63, ...) at most 24 rows name the same one
- expert_gate: bfloat16 [16, 2048, 1408], P('tok', None, 'head'), may hold values from -0.125 to 0.125
- expert_up: bfloat16 [16, 2048, 1408], P('tok', None, 'head'), may hold values from -0.125 to 0.125
- expert_down: bfloat16 [16, 1408, 2048], P('tok', 'head'), may hold values from -0.15625 to 0.15625
Outputs:
- new_entry: bfloat16 [512, 576], P('tok')
- attended: bfloat16 [512, 2048], P('tok', 'head')
- expert_mix: bfloat16 [512, 2048], P('tok', 'head')
The draws below stay inside these ranges and needn't reach their ends.
Inputs may be any that keep to these rules, and one draw needn't show every extreme that they name: `request_slot`: a permutation of the 512 slots; slot s lies on owner s // 32, so every owner holds 32 slots; the requests of one device name at most 2 slots of one owner, and every device reaches that bound. `cache_lengths`: the caches of an owner's slots lie end to end in slot order at the start of that owner's 9984 rows of latent_cache; they fill at most 9984 rows, and some owner fills all of them. `routes`: each row names 6 different experts; in the rows of one device no expert is named more than 24 times.
All inputs are finite; a program needn't handle non-finite values.
Results may differ from the reference program's by a relative error of at most 0.028.
Values may be sent and summed in bfloat16 or wider, within the bound.
A program may use at most 128 MiB of HBM per device.

```python
import math
import jax
import jax.numpy as jnp
import numpy as np
from jax import lax

D = 2048
HEADS = 16
NOPE = 128
ROPE = 64
LATENT = 512
FF = 1408
TOPK = 6
REQ_DEV = 32
LONG_LEN = 2048
SHORT_MOST = 256
SHORT_LEAST = 144
EXPERTS = 16
REQUESTS = 512
CACHE_DEV = 9984
ROUTE_MOST = 24
N_TOK = 16


def shuffled(subkey):
    return jax.random.permutation(subkey, REQ_DEV)


def slot_plan(key):
    folded = jax.random.fold_in(key, 7)
    subkeys = jax.random.split(folded, 9)
    owners_count = REQUESTS // REQ_DEV
    member = jnp.arange(REQ_DEV, dtype=jnp.int32)
    shifts = jax.random.permutation(subkeys[0], owners_count).astype(jnp.int32)
    offsets = shifts[member % owners_count]
    layout = jax.random.permutation(subkeys[1], owners_count).astype(jnp.int32)
    order_in = jax.vmap(shuffled)(jax.random.split(subkeys[2], owners_count)).astype(jnp.int32)
    within = jax.vmap(shuffled)(jax.random.split(subkeys[3], owners_count)).astype(jnp.int32)
    senders = jnp.arange(owners_count, dtype=jnp.int32)[:, None]
    target = layout[(senders + offsets[order_in]) % owners_count]
    slot_index = within[target, order_in]
    request_slot = (target * REQ_DEV + slot_index).reshape(-1).astype(jnp.int32)
    owner_ids = jnp.arange(owners_count, dtype=jnp.int32)
    shorts = jax.random.randint(subkeys[4], (owners_count, REQ_DEV), SHORT_LEAST, SHORT_MOST + 1, dtype=jnp.int32)
    fullest = jax.random.randint(subkeys[5], (), 0, owners_count, dtype=jnp.int32)
    chosen = (jax.random.randint(subkeys[6], (owners_count,), 0, 2, dtype=jnp.int32) == 1) | (owner_ids == fullest)
    long_at = jax.random.randint(subkeys[7], (owners_count,), 0, REQ_DEV, dtype=jnp.int32)
    long_size = jax.random.randint(subkeys[8], (owners_count,), LONG_LEN - LONG_LEN // 8, LONG_LEN + 1, dtype=jnp.int32)
    long_size = jnp.where(owner_ids == fullest, LONG_LEN, long_size)
    shorts = jnp.where((owner_ids == fullest)[:, None], SHORT_MOST, shorts)
    is_long = chosen[:, None] & (member[None, :] == long_at[:, None])
    by_slot = jnp.where(is_long, long_size[:, None], shorts).reshape(-1).astype(jnp.int32)
    cache_lengths = by_slot[request_slot]
    return (request_slot, cache_lengths)


def draw_request_slot(key, part):
    return slot_plan(key)[0]


def draw_cache_lengths(key, part):
    return slot_plan(key)[1]


def draw_hidden(key, part):
    subkeys = jax.random.split(key, 3)
    columns = jnp.arange(D, dtype=jnp.float32)
    col_scale = 0.6 * 3.0 ** (0.5 * columns / D) * jnp.exp(jax.random.uniform(subkeys[1], (D,), jnp.float32, -0.3, 0.3))
    row_scale = jnp.exp(jax.random.uniform(subkeys[2], (REQUESTS, 1), jnp.float32, -0.4, 0.4))
    sample = jnp.clip(jax.random.normal(subkeys[0], (REQUESTS, D), jnp.float32), -6.0, 6.0)
    return jnp.clip(sample * row_scale * col_scale[None, :], -24.0, 24.0).astype(jnp.bfloat16)


def level_of(key, shape, cuts, least, high):
    gain, own = 1.0, jax.random.fold_in(key, 6)
    for dim, parts in cuts:
        heights = jnp.exp(jax.random.uniform(jax.random.fold_in(own, dim), (parts,), jnp.float32, least / len(cuts), high / len(cuts)))
        gain = gain * jnp.repeat(heights, shape[dim] // parts).reshape([-1 if axis == dim else 1 for axis in range(len(shape))])
    return gain


def shared_out(key, own, number, rows, count, top, limit, skew):
    sequence = jax.random.permutation(key, count)
    packed, ordinary = shares(count, rows * top, limit, skew, True), shares(count, rows * top, limit, skew, False)
    places = jnp.arange(count)

    def named(lengths, rotation):
        used = int((lengths > 0).sum())
        fixed = max(1, used // 4)
        passed = fixed + (places - fixed + rotation * (used - fixed)) % max(1, count - fixed)
        return jnp.zeros((count,), jnp.int32).at[sequence[jnp.where(places < fixed, places, passed)]].set(jnp.asarray(lengths, jnp.int32))

    lengths = jnp.where(number % 4 == 0, named(packed, number // 4), named(ordinary, number - number // 4 - 1))
    mixed = jax.random.permutation(jax.random.fold_in(own, 3), count)
    giver, sink = mixed[0:count // 2 * 2:2], mixed[1:count // 2 * 2:2]
    margin = jnp.minimum(lengths[giver] - 1, limit - lengths[sink]) // 2
    margin = jnp.where((giver == sequence[0]) | (sink == sequence[0]) | (lengths[sink] == 0), 0, jnp.maximum(margin, 0))
    passed = jax.random.randint(jax.random.fold_in(own, 4), (count // 2,), 0, 1 << 20) % (margin + 1)
    lengths = lengths.at[giver].add(-passed).at[sink].add(passed)
    members = jnp.searchsorted(jnp.cumsum(lengths), jnp.arange(rows * top), side="right").astype(jnp.int32)
    grid = members.reshape(top, rows).T
    grid = grid[jax.random.permutation(jax.random.fold_in(own, 1), rows)]
    rotation = jax.random.randint(jax.random.fold_in(own, 2), (rows, 1), 0, top)
    return jnp.take_along_axis(grid, (jnp.arange(top)[None, :] + rotation) % top, axis=1)


def shares(amount, total, reach, lean, full):
    loads = [(1 << 20) // math.isqrt(rank ** lean) + 1 for rank in range(1, amount + 1)]
    largest = reach if full else min(reach, max(-(-total // amount), total * loads[0] // sum(loads)))
    least = 1 if total - largest >= amount - 1 else 0
    counts, spare = [largest] + [least] * (amount - 1), total - largest - least * (amount - 1)
    while spare > 0:
        candidates = [i for i in range(1, amount) if counts[i] < largest] or [i for i in range(1, amount) if counts[i] < reach]
        whole, budget = sum([loads[i] for i in candidates]), spare
        for i in candidates:
            addition = min(reach - counts[i], max(1, budget * loads[i] // whole), spare)
            counts[i] = counts[i] + addition
            spare = spare - addition
    return np.array(counts)


def bell_draw(rng, dims, scale, reach, cuts=(), kind=jnp.bfloat16):
    array = jax.random.normal(rng, dims, jnp.float32) * scale
    if len(cuts) > 0:
        array = level_of(rng, dims, cuts, -0.22, 0.18) * array
    return jnp.clip(array, min=-reach, max=reach).astype(kind)


def setup_inputs(seed: int = 0) -> dict:
    arg_keys = jax.random.split(jax.random.key(seed), 17)
    hidden = draw_hidden(jax.random.fold_in(arg_keys[16], 71), 0)
    attn_gain = jnp.clip(1.0 + 0.18 * jax.random.normal(arg_keys[1], (D,), jnp.float32), 0.1, 1.9)
    w_query = bell_draw(arg_keys[2], (D, HEADS * (NOPE + ROPE)), D ** -0.5, 0.125, ((1, 2),))
    w_latent = bell_draw(arg_keys[3], (D, LATENT + ROPE), D ** -0.5, 0.125, ((0, 2),))
    w_key_up = bell_draw(arg_keys[4], (HEADS, NOPE, LATENT), NOPE ** -0.5, 0.5, ((0, 2),))
    w_value_up = bell_draw(arg_keys[5], (HEADS, LATENT, NOPE), (LATENT // 16) ** -0.5, 1.0, ((0, 2),))
    w_out = bell_draw(arg_keys[6], (HEADS * NOPE, D), (HEADS * NOPE) ** -0.5, 0.125, ((0, 2),))
    latent_cache = bell_draw(arg_keys[7], (N_TOK * CACHE_DEV, LATENT + ROPE), 1.0, 6.0, ((0, 32),))
    cache_lengths = draw_cache_lengths(jax.random.fold_in(arg_keys[16], 71), 0)
    request_slot = draw_request_slot(jax.random.fold_in(arg_keys[16], 71), 0)
    ffn_gain = jnp.clip(1.0 + 0.18 * jax.random.normal(arg_keys[10], (D,), jnp.float32), 0.1, 1.9)
    w_router = bell_draw(arg_keys[11], (D, EXPERTS), (D // 4) ** -0.5, 0.25, ((0, 2),))
    routes_keys = jax.random.split(jax.random.fold_in(arg_keys[12], 1), REQUESTS // REQ_DEV)
    routes_turns = jax.random.permutation(jax.random.fold_in(arg_keys[12], 3), REQUESTS // REQ_DEV)
    routes = jax.vmap(lambda own, number: shared_out(jax.random.fold_in(arg_keys[12], 2), own, number, REQ_DEV, EXPERTS, TOPK, ROUTE_MOST, 2))(routes_keys, routes_turns).reshape((REQUESTS, TOPK))
    expert_gate = bell_draw(arg_keys[13], (EXPERTS, D, FF), D ** -0.5, 0.125, ((0, 16), (2, 2)))
    expert_up = bell_draw(arg_keys[14], (EXPERTS, D, FF), D ** -0.5, 0.125, ((0, 16), (2, 2)))
    expert_down = bell_draw(arg_keys[15], (EXPERTS, FF, D), FF ** -0.5, 0.15625, ((0, 16), (1, 2)))
    return dict(hidden=hidden, attn_gain=attn_gain, w_query=w_query, w_latent=w_latent, w_key_up=w_key_up, w_value_up=w_value_up, w_out=w_out, latent_cache=latent_cache, cache_lengths=cache_lengths, request_slot=request_slot, ffn_gain=ffn_gain, w_router=w_router, routes=routes, expert_gate=expert_gate, expert_up=expert_up, expert_down=expert_down)


NORM_EPS = 1e-06

def rotate_pairs(values, places):
    halfway = values.shape[-1] // 2
    freqs = 10000.0 ** (-jnp.arange(halfway, dtype=jnp.float32) / halfway)
    angles = places.astype(jnp.float32).reshape(places.shape + (1,) * (values.ndim - 1)) * freqs
    cosine = jnp.cos(angles)
    sine = jnp.sin(angles)
    first_half = values[..., :halfway]
    second_half = values[..., halfway:]
    return jnp.concatenate([first_half * cosine - second_half * sine, first_half * sine + second_half * cosine], axis=-1)

def owner_attention(bundle):
    slot_probes, owner_rows, slot_lengths = bundle
    starts = jnp.cumsum(slot_lengths) - slot_lengths
    places = jnp.arange(owner_rows.shape[0], dtype=jnp.int32)
    inside = (places[None, :] >= starts[:, None]) & (places[None, :] < (starts + slot_lengths)[:, None])
    factor = (NOPE + ROPE) ** (-0.5)
    scores = factor * jnp.einsum('khc,pc->khp', slot_probes.astype(jnp.float32), owner_rows.astype(jnp.float32), precision=lax.Precision.HIGHEST)
    weights = jnp.where(inside[:, None, :], jnp.exp(scores), 0.0).astype(jnp.bfloat16)
    numerator = jnp.einsum('khp,pl->khl', weights.astype(jnp.float32), owner_rows[:, :LATENT].astype(jnp.float32), precision=lax.Precision.HIGHEST)
    denominator = lax.optimization_barrier(jnp.sum(weights.astype(jnp.float32), axis=2))
    return (numerator, denominator)

def reference(hidden, attn_gain, w_query, w_latent, w_key_up, w_value_up, w_out, latent_cache, cache_lengths, request_slot, ffn_gain, w_router, routes, expert_gate, expert_up, expert_down):
    owners_count = REQUESTS // REQ_DEV
    wide_hidden = hidden.astype(jnp.float32)
    inv_attn = lax.rsqrt(lax.optimization_barrier(jnp.mean(wide_hidden * wide_hidden, axis=1, keepdims=True)) + NORM_EPS)
    normed_attn = (wide_hidden * inv_attn * attn_gain).astype(jnp.bfloat16)
    queries = jnp.dot(normed_attn, w_query, preferred_element_type=jnp.float32).astype(jnp.bfloat16)
    queries = queries.reshape(REQUESTS, HEADS, NOPE + ROPE)
    compressed = jnp.dot(normed_attn, w_latent, preferred_element_type=jnp.float32)
    latent_new = compressed[:, :LATENT]
    latent_new = latent_new * lax.rsqrt(lax.optimization_barrier(jnp.mean(latent_new * latent_new, axis=1, keepdims=True)) + NORM_EPS)
    new_entry = jnp.concatenate([latent_new, rotate_pairs(compressed[:, LATENT:], cache_lengths)], axis=1).astype(jnp.bfloat16)
    absorbed = jnp.einsum('rhn,hnl->rhl', queries[:, :, :NOPE].astype(jnp.float32), w_key_up.astype(jnp.float32), precision=lax.Precision.HIGHEST).astype(jnp.bfloat16)
    turned = rotate_pairs(queries[:, :, NOPE:].astype(jnp.float32), cache_lengths).astype(jnp.bfloat16)
    probes = jnp.concatenate([absorbed, turned], axis=2)
    factor = (NOPE + ROPE) ** (-0.5)
    self_score = factor * jnp.einsum('rhc,rc->rh', probes.astype(jnp.float32), new_entry.astype(jnp.float32), precision=lax.Precision.HIGHEST)
    self_weight = jnp.exp(self_score).astype(jnp.bfloat16).astype(jnp.float32)
    inverse = jnp.zeros((REQUESTS,), jnp.int32).at[request_slot].set(jnp.arange(REQUESTS, dtype=jnp.int32))
    slot_probes = probes[inverse].reshape(owners_count, REQ_DEV, HEADS, LATENT + ROPE)
    slot_lengths = cache_lengths[inverse].reshape(owners_count, REQ_DEV)
    owner_rows = latent_cache.reshape(owners_count, CACHE_DEV, LATENT + ROPE)
    numerator, denominator = lax.map(owner_attention, (slot_probes, owner_rows, slot_lengths))
    numerator = numerator.reshape(REQUESTS, HEADS, LATENT)[request_slot]
    denominator = denominator.reshape(REQUESTS, HEADS)[request_slot]
    numerator = numerator + self_weight[:, :, None] * new_entry[:, None, :LATENT].astype(jnp.float32)
    denominator = denominator + self_weight
    mixed_latent = (numerator / denominator[:, :, None]).astype(jnp.bfloat16)
    head_out = jnp.einsum('rhl,hld->rhd', mixed_latent.astype(jnp.float32), w_value_up.astype(jnp.float32), precision=lax.Precision.HIGHEST).astype(jnp.bfloat16)
    head_out = head_out.reshape(REQUESTS, HEADS * NOPE)
    attended = (wide_hidden + jnp.dot(head_out, w_out, preferred_element_type=jnp.float32)).astype(jnp.bfloat16)
    attended_wide = attended.astype(jnp.float32)
    gained = (attended_wide * ffn_gain).astype(jnp.bfloat16)
    inv_ffn = lax.rsqrt(lax.optimization_barrier(jnp.mean(attended_wide * attended_wide, axis=1)) + NORM_EPS)
    logits = jnp.dot(gained, w_router, preferred_element_type=jnp.float32) * inv_ffn[:, None]
    picked = jnp.take_along_axis(logits, routes, axis=1)
    lifted = jnp.exp(picked)
    route_weight = lifted / lax.optimization_barrier(jnp.sum(lifted, axis=1, keepdims=True))
    normed_ffn = (attended_wide * ffn_gain * inv_ffn[:, None]).astype(jnp.bfloat16)
    padded_rows = jnp.concatenate([normed_ffn, jnp.zeros((1, D), jnp.bfloat16)], axis=0)
    row_limit = owners_count * ROUTE_MOST

    def one_expert(carried, expert_id):
        member = routes == expert_id
        weight_row = lax.optimization_barrier(jnp.sum(jnp.where(member, route_weight, 0.0), axis=1))
        taken = jnp.any(member, axis=1)
        picked_rows = jnp.nonzero(taken, size=row_limit, fill_value=REQUESTS)[0].astype(jnp.int32)
        expert_in = padded_rows[picked_rows]
        gate_value = jnp.dot(expert_in, expert_gate[expert_id], preferred_element_type=jnp.float32)
        up_value = jnp.dot(expert_in, expert_up[expert_id], preferred_element_type=jnp.float32)
        activity = (jax.nn.silu(gate_value) * up_value).astype(jnp.bfloat16)
        expert_row = jnp.dot(activity, expert_down[expert_id], preferred_element_type=jnp.float32).astype(jnp.bfloat16)
        weight_pad = jnp.concatenate([weight_row, jnp.zeros((1,), jnp.float32)])[picked_rows]
        carried = carried.at[picked_rows].add(weight_pad[:, None] * expert_row.astype(jnp.float32))
        return (carried, None)
    mixture, unused = lax.scan(one_expert, jnp.zeros((REQUESTS + 1, D), jnp.float32), jnp.arange(EXPERTS, dtype=jnp.int32))
    expert_mix = mixture[:REQUESTS].astype(jnp.bfloat16)
    return (new_entry, attended, expert_mix)
```

```python
import jax
import jax.numpy as jnp
from jax import lax
from jax.experimental import pallas as pl
from jax.experimental.pallas import tpu as pltpu
from jax.sharding import PartitionSpec as P

D = 2048
NOPE = 128
ROPE = 64
LATENT = 512


NORM_EPS = 1e-06


def rotate_pairs(values, places):
    halfway = values.shape[-1] // 2
    freqs = 10000.0 ** (-jnp.arange(halfway, dtype=jnp.float32) / halfway)
    angles = places.astype(jnp.float32).reshape(places.shape + (1,) * (values.ndim - 1)) * freqs
    cosine = jnp.cos(angles)
    sine = jnp.sin(angles)
    first_half = values[..., :halfway]
    second_half = values[..., halfway:]
    return jnp.concatenate(
        [first_half * cosine - second_half * sine, first_half * sine + second_half * cosine],
        axis=-1,
    )


def owner_attend(all_heads, owner_lengths, latent_cache, head_index, factor):
    slot_rows = all_heads.shape[0]
    total_heads = all_heads.shape[1]
    probe_width = all_heads.shape[2]
    key_rows = latent_cache.shape[0]
    starts = jnp.cumsum(owner_lengths) - owner_lengths
    places = head_index * key_rows + jnp.arange(key_rows, dtype=jnp.int32)
    inside = (places[None, :] >= starts[:, None]) & (
        places[None, :] < (starts + owner_lengths)[:, None]
    )
    scores = factor * jnp.einsum(
        "qc,pc->qp",
        all_heads.reshape(slot_rows * total_heads, probe_width),
        latent_cache,
        preferred_element_type=jnp.float32,
    )
    scores = scores.reshape(slot_rows, total_heads, key_rows)
    weights = jnp.where(inside[:, None, :], jnp.exp(scores), 0.0).astype(jnp.bfloat16)
    numerator = jnp.einsum(
        "khp,pl->khl", weights, latent_cache[:, :LATENT], preferred_element_type=jnp.float32
    )
    denominator = jnp.sum(weights.astype(jnp.float32), axis=2)
    return (numerator, denominator)


def body(
    hidden,
    attn_gain,
    w_query,
    w_latent,
    w_key_up,
    w_value_up,
    w_out,
    latent_cache,
    cache_lengths,
    request_slot,
    ffn_gain,
    w_router,
    routes,
    expert_gate,
    expert_up,
    expert_down,
):
    local_rows = hidden.shape[0]
    quarter_width = hidden.shape[1]
    local_heads = w_key_up.shape[0]
    peer_count = lax.axis_size("tok")
    head_index = lax.axis_index("head")
    tok_index = lax.axis_index("tok")
    row_ids = jnp.arange(local_rows, dtype=jnp.int32)
    gathered = lax.all_gather(hidden, "head", axis=1, tiled=True)
    widened = gathered.astype(jnp.float32)
    inv_attn = lax.rsqrt(jnp.mean(widened * widened, axis=1, keepdims=True) + NORM_EPS)
    normed_attn = (widened * inv_attn * attn_gain).astype(jnp.bfloat16)
    normed_part = lax.dynamic_slice_in_dim(
        normed_attn, head_index * quarter_width, quarter_width, 1
    )
    compressed = lax.psum(
        jnp.dot(normed_part, w_latent, preferred_element_type=jnp.float32), "head"
    )
    latent_new = compressed[:, :LATENT]
    latent_new = latent_new * lax.rsqrt(
        jnp.mean(latent_new * latent_new, axis=1, keepdims=True) + NORM_EPS
    )
    new_entry = jnp.concatenate(
        [latent_new, rotate_pairs(compressed[:, LATENT:], cache_lengths)], axis=1
    ).astype(jnp.bfloat16)
    queries = jnp.dot(normed_attn, w_query, preferred_element_type=jnp.float32).astype(jnp.bfloat16)
    queries = queries.reshape(local_rows, local_heads, NOPE + ROPE)
    absorbed = jnp.einsum(
        "bhn,hnl->bhl", queries[:, :, :NOPE], w_key_up, preferred_element_type=jnp.float32
    ).astype(jnp.bfloat16)
    turned = rotate_pairs(queries[:, :, NOPE:].astype(jnp.float32), cache_lengths).astype(
        jnp.bfloat16
    )
    probes = jnp.concatenate([absorbed, turned], axis=2)
    factor = (NOPE + ROPE) ** (-0.5)
    self_score = factor * jnp.einsum(
        "bhc,bc->bh", probes, new_entry, preferred_element_type=jnp.float32
    )
    self_weight = jnp.exp(self_score).astype(jnp.bfloat16).astype(jnp.float32)
    per_owner = max(1, local_rows // peer_count)
    buffer_rows = peer_count * per_owner
    buffer_ids = jnp.arange(buffer_rows, dtype=jnp.int32)
    dest_owner = request_slot // local_rows
    earlier_same = (dest_owner[None, :] == dest_owner[:, None]) & (
        row_ids[None, :] < row_ids[:, None]
    )
    send_place = dest_owner * per_owner + jnp.sum(earlier_same.astype(jnp.int32), axis=1)
    all_probes, all_slots, all_lengths = (
        lax.all_gather(probes, "tok", axis=0, tiled=True),
        lax.all_gather(request_slot, "tok", axis=0, tiled=True),
        lax.all_gather(cache_lengths, "tok", axis=0, tiled=True),
    )
    total_rows = all_slots.shape[0]
    slot_hit = all_slots[None, :] == (tok_index * local_rows + row_ids)[:, None]
    request_at = jnp.sum(
        jnp.where(slot_hit, jnp.arange(total_rows, dtype=jnp.int32)[None, :], 0), axis=1
    )
    owner_probes = all_probes[request_at]
    owner_lengths = all_lengths[request_at]
    owned_here = (
        (all_slots // local_rows == tok_index).astype(jnp.int32).reshape(peer_count, local_rows)
    )
    prior_count = (jnp.cumsum(owned_here, axis=1) - owned_here).reshape(total_rows)
    back_index = request_at // local_rows * per_owner + prior_count[request_at]
    all_heads = lax.all_gather(owner_probes, "head", axis=1, tiled=True)
    numerator, denominator = owner_attend(
        all_heads, owner_lengths, latent_cache, head_index, factor
    )
    group_num, group_den = (
        lax.psum_scatter(numerator, "head", scatter_dimension=1, tiled=True),
        lax.psum_scatter(denominator, "head", scatter_dimension=1, tiled=True),
    )
    at_place = buffer_ids[:, None] == back_index[None, :]
    slot_of_place = jnp.sum(jnp.where(at_place, row_ids[None, :], 0), axis=1) + local_rows * (
        1 - jnp.max(at_place.astype(jnp.int32), axis=1)
    )
    padded_num = jnp.concatenate(
        [group_num, jnp.zeros((1, local_heads, LATENT), jnp.float32)], axis=0
    )
    padded_den = jnp.concatenate([group_den, jnp.zeros((1, local_heads), jnp.float32)], axis=0)
    got_num, got_den = (
        lax.all_to_all(
            padded_num[slot_of_place].reshape(peer_count, per_owner, local_heads, LATENT),
            "tok",
            split_axis=0,
            concat_axis=0,
            tiled=True,
        ),
        lax.all_to_all(
            padded_den[slot_of_place].reshape(peer_count, per_owner, local_heads),
            "tok",
            split_axis=0,
            concat_axis=0,
            tiled=True,
        ),
    )
    back_num = got_num.reshape(buffer_rows, local_heads, LATENT)
    back_den = got_den.reshape(buffer_rows, local_heads)
    total_num = back_num[send_place] + self_weight[:, :, None] * new_entry[:, None, :LATENT].astype(
        jnp.float32
    )
    total_den = back_den[send_place] + self_weight
    mixed_latent = (total_num / total_den[:, :, None]).astype(jnp.bfloat16)
    head_out = jnp.einsum(
        "bhl,hld->bhd", mixed_latent, w_value_up, preferred_element_type=jnp.float32
    ).astype(jnp.bfloat16)
    head_out = head_out.reshape(local_rows, local_heads * NOPE)
    attn_piece = lax.psum_scatter(
        jnp.dot(head_out, w_out, preferred_element_type=jnp.float32),
        "head",
        scatter_dimension=1,
        tiled=True,
    )
    attended = (hidden.astype(jnp.float32) + attn_piece).astype(jnp.bfloat16)
    attended_wide = attended.astype(jnp.float32)
    gained = (attended_wide * ffn_gain).astype(jnp.bfloat16)
    squares, logit_part = lax.psum(
        (
            jnp.sum(attended_wide * attended_wide, axis=1),
            jnp.dot(gained, w_router, preferred_element_type=jnp.float32),
        ),
        "head",
    )
    inv_ffn = lax.rsqrt(squares / D + NORM_EPS)
    logits = logit_part * inv_ffn[:, None]
    normed_ffn = (attended_wide * ffn_gain * inv_ffn[:, None]).astype(jnp.bfloat16)
    expert_count = w_router.shape[1]
    route_count = routes.shape[1]
    expert_ids = jnp.arange(expert_count, dtype=jnp.int32)
    named = routes[:, :, None] == expert_ids[None, None, :]
    picked = jnp.sum(jnp.where(named, logits[:, None, :], 0.0), axis=2)
    lifted = jnp.exp(picked)
    route_weight = lifted / jnp.sum(lifted, axis=1, keepdims=True)
    struck = jnp.max(named.astype(jnp.int32), axis=1)
    earlier_hits = jnp.cumsum(struck, axis=0) - struck
    capacity = min(local_rows, max(2, 2 * local_rows * route_count // expert_count))
    route_place = routes * capacity + jnp.take_along_axis(earlier_hits, routes, axis=1)
    slot_total = expert_count * capacity
    slot_ids = jnp.arange(slot_total, dtype=jnp.int32)
    filled = route_place[None, :, :] == slot_ids[:, None, None]
    source_token = jnp.sum(
        jnp.where(filled, row_ids[None, :, None], 0), axis=(1, 2)
    ) + local_rows * (1 - jnp.max(filled.astype(jnp.int32), axis=(1, 2)))
    full_rows = lax.all_gather(normed_ffn, "head", axis=1, tiled=True)
    padded_rows = jnp.concatenate(
        [full_rows, jnp.zeros((1, full_rows.shape[1]), jnp.bfloat16)], axis=0
    )
    arrived = lax.all_to_all(
        padded_rows[source_token].reshape(expert_count, capacity, full_rows.shape[1]),
        "tok",
        split_axis=0,
        concat_axis=0,
        tiled=True,
    )
    expert_in = arrived.reshape(peer_count * capacity, full_rows.shape[1])
    gate_value = jnp.dot(expert_in, expert_gate[0], preferred_element_type=jnp.float32)
    up_value = jnp.dot(expert_in, expert_up[0], preferred_element_type=jnp.float32)
    activity = (jax.nn.silu(gate_value) * up_value).astype(jnp.bfloat16)
    expert_share = lax.psum_scatter(
        jnp.dot(activity, expert_down[0], preferred_element_type=jnp.float32).astype(jnp.bfloat16),
        "head",
        scatter_dimension=1,
        tiled=True,
    )
    returned = lax.all_to_all(
        expert_share.reshape(peer_count, capacity, quarter_width),
        "tok",
        split_axis=0,
        concat_axis=0,
        tiled=True,
    )
    chosen_rows = returned.reshape(slot_total, quarter_width)[route_place]
    expert_mix = jnp.sum(route_weight[:, :, None] * chosen_rows.astype(jnp.float32), axis=1).astype(
        jnp.bfloat16
    )
    return (new_entry, attended, expert_mix)


MESH_ID = pl.DeviceIdType.MESH
KEY_BLOCK = 384
WINDOW = 4
VMEM_LIMIT = 48 * 1024 * 1024


def meet(partners):
    barrier = pltpu.get_barrier_semaphore()
    for partner in partners:
        pl.semaphore_signal(barrier, inc=1, device_id=partner, device_id_type=MESH_ID)
    pl.semaphore_wait(barrier, len(partners))


def in_vmem(count):
    return [pl.BlockSpec(memory_space=pltpu.VMEM)] * count


def swap_pair(arrays, number):
    count = len(arrays)

    def kernel(*refs):
        ins, outs = refs[:count], refs[count : 2 * count]
        send_sem, recv_sem = refs[2 * count :]
        partner = (lax.axis_index("tok"), 1 - lax.axis_index("head"))
        meet([partner])
        copies = []
        for i in range(count):
            copy = pltpu.make_async_remote_copy(
                src_ref=ins[i],
                dst_ref=outs[i],
                send_sem=send_sem.at[i],
                recv_sem=recv_sem.at[i],
                device_id=partner,
                device_id_type=MESH_ID,
            )
            copy.start()
            copies.append(copy)
        for copy in copies:
            copy.wait()

    return pl.pallas_call(
        kernel,
        out_shape=[jax.ShapeDtypeStruct(a.shape, a.dtype) for a in arrays],
        in_specs=in_vmem(count),
        out_specs=in_vmem(count),
        scratch_shapes=[pltpu.SemaphoreType.DMA((count,)), pltpu.SemaphoreType.DMA((count,))],
        compiler_params=pltpu.CompilerParams(
            collective_id=number, has_side_effects=True, vmem_limit_bytes=VMEM_LIMIT
        ),
        name=f"swap_pair_{number}",
    )(*arrays)


def to_owners(blocks, number):
    peers = blocks.shape[0]

    def kernel(src, out, send_sem, recv_sem, own_sem):
        tok, head = lax.axis_index("tok"), lax.axis_index("head")
        others = [
            (lax.rem(tok + d, peers), head if e == 0 else 1 - head)
            for d in range(peers)
            for e in range(2)
            if d + e > 0
        ]
        meet(others)
        own = pltpu.make_async_copy(src.at[tok], out.at[head, tok], own_sem)
        own.start()
        sends = []
        for i, (there, side) in enumerate(others):
            copy = pltpu.make_async_remote_copy(
                src_ref=src.at[there],
                dst_ref=out.at[head, tok],
                send_sem=send_sem.at[i],
                recv_sem=recv_sem.at[head, tok],
                device_id=(there, side),
                device_id_type=MESH_ID,
            )
            copy.start()
            sends.append(copy)
        for there, side in others:
            pltpu.make_async_remote_copy(
                src_ref=src.at[there],
                dst_ref=out.at[side, there],
                send_sem=send_sem.at[0],
                recv_sem=recv_sem.at[side, there],
                device_id=(there, side),
                device_id_type=MESH_ID,
            ).wait_recv()
        for copy in sends:
            copy.wait_send()
        own.wait()

    return pl.pallas_call(
        kernel,
        out_shape=jax.ShapeDtypeStruct((2,) + blocks.shape, blocks.dtype),
        in_specs=in_vmem(1),
        out_specs=in_vmem(1)[0],
        scratch_shapes=[
            pltpu.SemaphoreType.DMA((2 * peers,)),
            pltpu.SemaphoreType.DMA((2, peers)),
            pltpu.SemaphoreType.DMA,
        ],
        compiler_params=pltpu.CompilerParams(
            collective_id=number, has_side_effects=True, vmem_limit_bytes=VMEM_LIMIT
        ),
        name="to_owners",
    )(blocks)


def gather_rows(block, peers, number):
    rows, width = block.shape
    half = rows // 2
    layers = peers // 4

    def kernel(src, out, send_sem, recv_sem, own_sem):
        tok, x = lax.axis_index("tok"), lax.axis_index("head")
        z, y, core = tok // 4, (tok // 2) % 2, tok % 2

        def place(z_, y_, core_):
            return z_ * 4 + y_ * 2 + core_

        across_x = (tok, 1 - x)
        across_y = (place(z, 1 - y, core), x)
        sibling = (place(z, y, 1 - core), x)
        along_z = [(place(lax.rem(z + d, layers), y, core), x) for d in range(1, layers)]
        meet([across_x, across_y, sibling] + along_z)

        def spot(z_, y_, core_, x_, h):
            start = pl.multiple_of(place(z_, y_, core_) * rows + h * half, half)
            return out.at[pl.ds(start, half), pl.ds(pl.multiple_of(x_ * width, 128), width)]

        def slot(z_, y_, core_, x_, h):
            return ((place(z_, y_, core_) * 2) + x_) * 2 + h

        sends = []

        def push(target, z_, y_, core_, x_, h, fresh=False):
            dst = spot(z_, y_, core_, x_, h)
            copy = pltpu.make_async_remote_copy(
                src_ref=src.at[pl.ds(h * half, half)] if fresh else dst,
                dst_ref=dst,
                send_sem=send_sem.at[len(sends)],
                recv_sem=recv_sem.at[slot(z_, y_, core_, x_, h)],
                device_id=target,
                device_id_type=MESH_ID,
            )
            copy.start()
            sends.append(copy)

        def land(z_, y_, core_, x_, h):
            dst = spot(z_, y_, core_, x_, h)
            pltpu.make_async_remote_copy(
                src_ref=dst,
                dst_ref=dst,
                send_sem=send_sem.at[0],
                recv_sem=recv_sem.at[slot(z_, y_, core_, x_, h)],
                device_id=sibling,
                device_id_type=MESH_ID,
            ).wait_recv()

        for target in along_z[:1] + along_z[2:] + along_z[1:2]:
            for h in range(2):
                push(target, z, y, core, x, h, True)
        for h in range(2):
            push(across_x, z, y, core, x, h, True)
            push(across_y, z, y, core, x, h, True)
            push(sibling, z, y, core, x, h, True)
        own = [
            pltpu.make_async_copy(
                src.at[pl.ds(h * half, half)], spot(z, y, core, x, h), own_sem.at[h]
            )
            for h in range(2)
        ]
        for copy in own:
            copy.start()
        turns = [0, 1, 3, 2][:layers]
        for d in turns:
            z_ = lax.rem(z + d, layers)
            if d > 0:
                for h in range(2):
                    land(z_, y, core, x, h)
                    push(across_x, z_, y, core, x, h)
                    push(across_y, z_, y, core, x, h)
                    push(sibling, z_, y, core, x, h)
            land(z_, 1 - y, core, x, 0)
            push(across_x, z_, 1 - y, core, x, 0)
            push(sibling, z_, 1 - y, core, x, 0)
            land(z_, y, core, 1 - x, 1)
            push(across_y, z_, y, core, 1 - x, 1)
            push(sibling, z_, y, core, 1 - x, 1)
            land(z_, 1 - y, core, x, 1)
            push(sibling, z_, 1 - y, core, x, 1)
            land(z_, y, core, 1 - x, 0)
            push(sibling, z_, y, core, 1 - x, 0)
        for d in turns:
            z_ = lax.rem(z + d, layers)
            for h in range(2):
                land(z_, 1 - y, core, 1 - x, h)
                push(sibling, z_, 1 - y, core, 1 - x, h)
        for d in turns:
            z_ = lax.rem(z + d, layers)
            for y_ in (y, 1 - y):
                for x_ in (x, 1 - x):
                    for h in range(2):
                        land(z_, y_, 1 - core, x_, h)
        for copy in sends:
            copy.wait_send()
        for copy in own:
            copy.wait()

    return pl.pallas_call(
        kernel,
        out_shape=jax.ShapeDtypeStruct((rows * peers, 2 * width), block.dtype),
        in_specs=in_vmem(1),
        out_specs=in_vmem(1)[0],
        scratch_shapes=[
            pltpu.SemaphoreType.DMA((128,)),
            pltpu.SemaphoreType.DMA((4 * peers,)),
            pltpu.SemaphoreType.DMA((2,)),
        ],
        compiler_params=pltpu.CompilerParams(
            collective_id=number, has_side_effects=True, vmem_limit_bytes=VMEM_LIMIT
        ),
        name="gather_rows",
    )(block)


def scatter_sums(parts, peers, number):
    layers = parts.shape[3]
    half, full = parts.shape[4:]
    width = full // 2

    def kernel(src, out, got_core, kept, got_first, mid, got_second, last, got_z, sends, recvs):
        tok, x = lax.axis_index("tok"), lax.axis_index("head")
        z, y, core = tok // 4, (tok // 2) % 2, tok % 2

        def place(z_, y_, core_):
            return z_ * 4 + y_ * 2 + core_

        across_x = (tok, 1 - x)
        across_y = (place(z, 1 - y, core), x)
        sibling = (place(z, y, 1 - core), x)
        along_z = [(place(lax.rem(z + d, layers), y, core), x) for d in range(1, layers)]
        meet([across_x, across_y, sibling] + along_z)

        def copy_to(target, source, dest, index):
            copy = pltpu.make_async_remote_copy(
                src_ref=source,
                dst_ref=dest,
                send_sem=sends.at[index],
                recv_sem=recvs.at[index],
                device_id=target,
                device_id_type=MESH_ID,
            )
            copy.start()
            return copy

        def columns(x_):
            return pl.ds(pl.multiple_of(x_ * width, 128), width)

        def total(first, second):
            return first.astype(jnp.float32) + second.astype(jnp.float32)

        cores = [[None, None], [None, None]]
        for g in range(2):
            for h in range(2):
                y_ = (1 - y) if g == 0 else y
                cores[h][g] = copy_to(
                    sibling, src.at[h, 1 - core, y_], got_core.at[h, y_], 2 * h + g
                )

        def fold_core(h, y_):
            @pl.loop(0, layers)
            def _(z_):
                kept[h, y_, z_] = total(src[h, core, y_, z_], got_core[h, y_, z_]).astype(
                    kept.dtype
                )

        cores[1][0].wait_recv()
        fold_core(1, 1 - y)
        first_y = copy_to(across_y, kept.at[1, 1 - y], got_first.at[1], 4)
        cores[0][0].wait_recv()
        fold_core(0, 1 - y)
        first_x = [
            copy_to(
                across_x,
                kept.at[0, 1 - y, slice(None), slice(None), columns(1 - x)],
                got_first.at[0, slice(None), slice(None), pl.ds(0, width)],
                5,
            )
        ]
        cores[0][1].wait_recv()
        fold_core(0, y)
        first_x.append(
            copy_to(
                across_x,
                kept.at[0, y, slice(None), slice(None), columns(1 - x)],
                got_first.at[0, slice(None), slice(None), pl.ds(width, width)],
                6,
            )
        )
        cores[1][1].wait_recv()
        fold_core(1, y)

        first_x[0].wait_recv()

        @pl.loop(0, layers)
        def _(z_):
            mid[0, z_] = total(
                kept[0, 1 - y, z_, :, columns(x)], got_first[0, z_, :, :width]
            ).astype(mid.dtype)

        second_y = copy_to(across_y, mid.at[0], got_second.at[0], 7)

        first_y.wait_recv()

        @pl.loop(0, layers)
        def _(z_):
            mid[1, z_] = total(
                kept[1, y, z_, :, columns(1 - x)], got_first[1, z_, :, columns(1 - x)]
            ).astype(mid.dtype)

        second_x = copy_to(across_x, mid.at[1], got_second.at[1], 8)
        first_x[1].wait_recv()

        zs = []

        def send_z(h):
            for d in range(1, layers):
                z_ = lax.rem(z + d, layers)
                zs.append(
                    copy_to(
                        along_z[d - 1], last.at[h, z_], got_z.at[h, d - 1], 9 + h * layers + d - 1
                    )
                )

        second_y.wait_recv()

        @pl.loop(0, layers)
        def _(z_):
            last[0, z_] = (
                total(kept[0, y, z_, :, columns(x)], got_first[0, z_, :, width:])
                + got_second[0, z_].astype(jnp.float32)
            ).astype(last.dtype)

        send_z(0)
        second_x.wait_recv()

        @pl.loop(0, layers)
        def _(z_):
            last[1, z_] = (
                total(kept[1, y, z_, :, columns(x)], got_first[1, z_, :, columns(x)])
                + got_second[1, z_].astype(jnp.float32)
            ).astype(last.dtype)

        send_z(1)
        for copy in zs:
            copy.wait_recv()
        for h in range(2):
            acc = last[h, z].astype(jnp.float32)
            for d in range(1, layers):
                acc = acc + got_z[h, d - 1].astype(jnp.float32)
            out[h] = acc.astype(out.dtype)
        for copy in cores[0] + cores[1] + first_x + [first_y, second_y, second_x] + zs:
            copy.wait_send()

    kind = parts.dtype
    return pl.pallas_call(
        kernel,
        out_shape=jax.ShapeDtypeStruct((2, half, width), kind),
        in_specs=in_vmem(1),
        out_specs=in_vmem(1)[0],
        scratch_shapes=[
            pltpu.VMEM((2, 2, layers, half, full), kind),
            pltpu.VMEM((2, 2, layers, half, full), kind),
            pltpu.VMEM((2, layers, half, full), kind),
            pltpu.VMEM((2, layers, half, width), kind),
            pltpu.VMEM((2, layers, half, width), kind),
            pltpu.VMEM((2, layers, half, width), kind),
            pltpu.VMEM((2, layers - 1, half, width), kind),
            pltpu.SemaphoreType.DMA((9 + 2 * layers,)),
            pltpu.SemaphoreType.DMA((9 + 2 * layers,)),
        ],
        compiler_params=pltpu.CompilerParams(
            collective_id=number, has_side_effects=True, vmem_limit_bytes=VMEM_LIMIT
        ),
        name="scatter_sums",
    )(parts)


def ragged_attend(queries, cache, ids, bounds, base, factor):
    slots, heads, width = queries.shape
    blocks = cache.shape[0] // KEY_BLOCK

    def kernel(ids_ref, bounds_ref, base_ref, q_ref, kv_ref, num_ref, den_ref):
        j = pl.program_id(0)

        @pl.when(j == 0)
        def _():
            num_ref[...] = jnp.zeros_like(num_ref)
            den_ref[...] = jnp.zeros_like(den_ref)

        kv = kv_ref[...]
        who = [ids_ref[j * WINDOW + w] for w in range(WINDOW)]
        some = jnp.concatenate([q_ref[r] for r in who], axis=0)
        scores = factor * lax.dot_general(
            some, kv, (((1,), (1,)), ((), ())), preferred_element_type=jnp.float32
        )
        places = (
            base_ref[0]
            + j * KEY_BLOCK
            + lax.broadcasted_iota(jnp.int32, (heads, KEY_BLOCK), 1)
        )
        inside = jnp.concatenate(
            [
                ((places >= bounds_ref[r]) & (places < bounds_ref[slots + r])).astype(jnp.int32)
                for r in who
            ],
            axis=0,
        )
        weights = jnp.where(inside > 0, jnp.exp(scores), 0.0).astype(jnp.bfloat16)
        num = jnp.dot(weights, kv[:, :LATENT], preferred_element_type=jnp.float32)
        den = jnp.sum(weights.astype(jnp.float32), axis=1, keepdims=True)
        for w, r in enumerate(who):
            rows = slice(w * heads, (w + 1) * heads)
            num_ref[r] += num[rows]
            den_ref[r] += jnp.broadcast_to(den[rows], (heads, 128))

    return pl.pallas_call(
        kernel,
        out_shape=[
            jax.ShapeDtypeStruct((slots, heads, LATENT), jnp.float32),
            jax.ShapeDtypeStruct((slots, heads, 128), jnp.float32),
        ],
        grid_spec=pltpu.PrefetchScalarGridSpec(
            num_scalar_prefetch=3,
            grid=(blocks,),
            in_specs=[
                pl.BlockSpec((slots, heads, width), lambda j, *_: (0, 0, 0)),
                pl.BlockSpec((KEY_BLOCK, width), lambda j, *_: (j, 0)),
            ],
            out_specs=[
                pl.BlockSpec((slots, heads, LATENT), lambda j, *_: (0, 0, 0)),
                pl.BlockSpec((slots, heads, 128), lambda j, *_: (0, 0, 0)),
            ],
        ),
        compiler_params=pltpu.CompilerParams(vmem_limit_bytes=VMEM_LIMIT),
        name="ragged_attend",
    )(ids, bounds, base, queries, cache)


def pick_rows(chosen, values):
    return jnp.dot(
        chosen.astype(jnp.bfloat16), values, preferred_element_type=jnp.float32
    ).astype(values.dtype)


def direct_body(
    hidden,
    attn_gain,
    w_query,
    w_latent,
    w_key_up,
    w_value_up,
    w_out,
    latent_cache,
    cache_lengths,
    request_slot,
    ffn_gain,
    w_router,
    routes,
    expert_gate,
    expert_up,
    expert_down,
):
    f32, bf16 = jnp.float32, jnp.bfloat16
    rows, part = hidden.shape
    peers = lax.axis_size("tok")
    each = rows // peers
    local_heads = w_key_up.shape[0]
    expert_count = w_router.shape[1]
    head = lax.axis_index("head")
    tok = lax.axis_index("tok")
    ids = jnp.arange(rows, dtype=jnp.int32)

    owner = request_slot // rows
    earlier = (owner[None, :] == owner[:, None]) & (ids[None, :] < ids[:, None])
    send_place = owner * each + jnp.sum(earlier.astype(jnp.int32), axis=1)
    placed = ids[:, None] == send_place[None, :]
    route_mask = jnp.max(
        (routes[:, :, None] == jnp.arange(expert_count, dtype=jnp.int32)).astype(jnp.int32), axis=1
    )
    meta = jnp.concatenate(
        [
            (request_slot % rows)[:, None],
            (cache_lengths // 64)[:, None],
            (cache_lengths % 64)[:, None],
            route_mask,
        ],
        axis=1,
    ).astype(bf16)
    meta = jnp.pad(meta, ((0, 0), (0, part - meta.shape[1])))
    sent = pick_rows(placed, jnp.concatenate([hidden, meta], axis=1))
    blocks = sent.reshape(peers, each, 2, part).transpose(0, 2, 1, 3)
    blocks = blocks.reshape(peers, 2 * each * part // 128, 128)
    arrived = to_owners(blocks, 0).reshape(2, peers, 2, each, part)
    wide = arrived[:, :, 0].reshape(2, rows, part)
    meta = arrived[0, :, 1].reshape(rows, part)[:, : 3 + expert_count].astype(jnp.int32)
    slot, lengths = meta[:, 0], meta[:, 1] * 64 + meta[:, 2]
    mask = meta[:, 3:]
    starts = jnp.sum(jnp.where(slot[None, :] < slot[:, None], lengths[None, :], 0), axis=1)
    full = jnp.concatenate([wide[0], wide[1]], axis=1).astype(f32)
    mine = lax.dynamic_index_in_dim(wide, head, 0, keepdims=False)

    inv_attn = lax.rsqrt(jnp.mean(full * full, axis=1, keepdims=True) + NORM_EPS)
    normed = (full * inv_attn * attn_gain).astype(bf16)
    normed_part = lax.dynamic_slice_in_dim(normed, head * part, part, 1)
    compressed = jnp.dot(normed_part, w_latent, preferred_element_type=f32)
    queries = jnp.dot(normed, w_query, preferred_element_type=f32).astype(bf16)
    queries = queries.reshape(rows, local_heads, NOPE + ROPE)
    absorbed = jnp.einsum(
        "bhn,hnl->bhl", queries[:, :, :NOPE], w_key_up, preferred_element_type=f32
    ).astype(bf16)
    turned = rotate_pairs(queries[:, :, NOPE:].astype(f32), lengths).astype(bf16)
    probes = jnp.concatenate([absorbed, turned], axis=2)
    far_probes, far_compressed = swap_pair([probes, compressed], 1)
    compressed = compressed + far_compressed
    latent_new = compressed[:, :LATENT]
    latent_new = latent_new * lax.rsqrt(
        jnp.mean(latent_new * latent_new, axis=1, keepdims=True) + NORM_EPS
    )
    new_entry = jnp.concatenate(
        [latent_new, rotate_pairs(compressed[:, LATENT:], lengths)], axis=1
    ).astype(bf16)
    factor = (NOPE + ROPE) ** (-0.5)
    self_score = factor * jnp.einsum(
        "bhc,bc->bh", probes, new_entry, preferred_element_type=f32
    )
    self_weight = jnp.exp(self_score).astype(bf16).astype(f32)

    key_rows = latent_cache.shape[0]
    block_starts = head * key_rows + jnp.arange(0, key_rows, KEY_BLOCK, dtype=jnp.int32)
    ends = starts + lengths
    first = jnp.sum((ends[None, :] <= block_starts[:, None]).astype(jnp.int32), axis=1)
    first = jnp.minimum(first, rows - WINDOW)
    window = first[:, None] + jnp.arange(WINDOW, dtype=jnp.int32)
    window_ids = jnp.sum(
        jnp.where(window[:, :, None] == slot[None, None, :], ids[None, None, :], 0), axis=2
    )
    numerator, denominator = ragged_attend(
        jnp.concatenate([probes, far_probes], axis=1),
        latent_cache,
        window_ids.reshape(-1).astype(jnp.int32),
        jnp.concatenate([starts, ends]).astype(jnp.int32),
        (head * key_rows).reshape(1).astype(jnp.int32),
        factor,
    )
    denominator = denominator[:, :, 0]
    far_num, far_den = swap_pair(
        [
            numerator[:, local_heads:].astype(bf16).reshape(rows * local_heads, LATENT),
            denominator[:, local_heads:].reshape(rows * local_heads // 128, 128),
        ],
        2,
    )
    total_num = (
        numerator[:, :local_heads]
        + far_num.reshape(rows, local_heads, LATENT).astype(f32)
        + self_weight[:, :, None] * new_entry[:, None, :LATENT].astype(f32)
    )
    total_den = denominator[:, :local_heads] + far_den.reshape(rows, local_heads) + self_weight
    mixed = (total_num / total_den[:, :, None]).astype(bf16)
    head_out = jnp.einsum("bhl,hld->bhd", mixed, w_value_up, preferred_element_type=f32)
    head_out = head_out.astype(bf16).reshape(rows, local_heads * NOPE)
    piece = jnp.dot(head_out, w_out, preferred_element_type=f32)
    kept = lax.dynamic_slice_in_dim(piece, head * part, part, 1)
    given = lax.dynamic_slice_in_dim(piece, (1 - head) * part, part, 1)
    (far_piece,) = swap_pair([given], 3)
    attended = (mine.astype(f32) + (kept + far_piece)).astype(bf16)

    attended_wide = attended.astype(f32)
    gained = (attended_wide * ffn_gain).astype(bf16)
    squares = jnp.sum(attended_wide * attended_wide, axis=1, keepdims=True)
    logit_part = jnp.dot(gained, w_router, preferred_element_type=f32)
    notes = jnp.concatenate([squares, logit_part], axis=1)
    high = notes.astype(bf16)
    low = (notes - high.astype(f32)).astype(bf16)
    notes = jnp.concatenate([high, low, mask.astype(bf16)], axis=1)
    notes = jnp.pad(notes, ((0, 0), (0, 128 - notes.shape[1])))
    gathered = gather_rows(jnp.concatenate([gained, notes], axis=1), peers, 4)

    back = jnp.concatenate([attended, new_entry], axis=1).reshape(peers, each, -1)
    back = lax.all_to_all(back, "tok", split_axis=0, concat_axis=0, tiled=True)
    back = pick_rows(placed.T, back.reshape(rows, -1))

    span = part + 128
    tokens = jnp.concatenate([gathered[:, :part], gathered[:, span : span + part]], axis=1)
    marks = gathered[:, part:span].astype(f32), gathered[:, span + part :].astype(f32)
    count = 1 + expert_count
    sums = sum(m[:, :count] + m[:, count : 2 * count] for m in marks)
    inv_ffn = lax.rsqrt(sums[:, :1] / (2 * part) + NORM_EPS)
    lifted = jnp.exp(sums[:, 1:] * inv_ffn) * marks[0][:, 2 * count : 2 * count + expert_count]
    here = (jnp.arange(expert_count, dtype=jnp.int32) == tok).astype(f32)
    weight = jnp.sum(lifted * here, axis=1) / jnp.sum(lifted, axis=1)
    gate_value = jnp.dot(tokens, expert_gate[0], preferred_element_type=f32) * inv_ffn
    up_value = jnp.dot(tokens, expert_up[0], preferred_element_type=f32) * inv_ffn
    activity = (jax.nn.silu(gate_value) * up_value).astype(bf16)
    every = jnp.arange(rows * peers, dtype=jnp.int32)
    half = rows // 2
    layers = peers // 4
    h_, c_, y_, z_ = (
        every // (half * peers),
        every // (half * peers // 2) % 2,
        every // (half * layers) % 2,
        every // half % layers,
    )
    device = z_ * 4 + y_ * 2 + c_
    inner = h_ * half + every % half
    source = inner // each * rows + device * each + inner % each
    moved = source[:, None] == every[None, :]
    activity = pick_rows(moved, activity)
    weight = jnp.sum(jnp.where(moved, weight[None, :], 0.0), axis=1)
    terms = jnp.dot(activity, expert_down[0], preferred_element_type=f32) * weight[:, None]
    terms = terms.astype(bf16).reshape(2, 2, 2, layers, half, 2 * part)
    summed = scatter_sums(terms, peers, 5).reshape(rows, part)
    expert_mix = pick_rows(placed.T, summed)
    return (back[:, part:], back[:, :part], expert_mix)


def solution(mesh):
    in_specs = (
        P("tok", "head"),
        P(),
        P(None, "head"),
        P("head", None),
        P("head", None, None),
        P("head", None, None),
        P("head", None),
        P(("tok", "head"), None),
        P("tok"),
        P("tok"),
        P("head"),
        P("head", None),
        P("tok", None),
        P("tok", None, "head"),
        P("tok", None, "head"),
        P("tok", "head", None),
    )
    out_specs = (P("tok", None), P("tok", "head"), P("tok", "head"))
    chosen = direct_body if (mesh.shape["tok"], mesh.shape["head"]) == (16, 2) else body
    return jax.shard_map(chosen, mesh=mesh, in_specs=in_specs, out_specs=out_specs, check_vma=False)
```

```python
import jax
import jax.numpy as jnp
from jax import lax
from jax.experimental import pallas as pl
from jax.experimental.pallas import tpu as pltpu
from jax.sharding import PartitionSpec as P

D = 2048
NOPE = 128
ROPE = 64
LATENT = 512


NORM_EPS = 1e-06


def rotate_pairs(values, places):
    halfway = values.shape[-1] // 2
    freqs = 10000.0 ** (-jnp.arange(halfway, dtype=jnp.float32) / halfway)
    angles = places.astype(jnp.float32).reshape(places.shape + (1,) * (values.ndim - 1)) * freqs
    cosine = jnp.cos(angles)
    sine = jnp.sin(angles)
    first_half = values[..., :halfway]
    second_half = values[..., halfway:]
    return jnp.concatenate(
        [first_half * cosine - second_half * sine, first_half * sine + second_half * cosine],
        axis=-1,
    )


def owner_attend(all_heads, owner_lengths, latent_cache, head_index, factor):
    slot_rows = all_heads.shape[0]
    total_heads = all_heads.shape[1]
    probe_width = all_heads.shape[2]
    key_rows = latent_cache.shape[0]
    starts = jnp.cumsum(owner_lengths) - owner_lengths
    places = head_index * key_rows + jnp.arange(key_rows, dtype=jnp.int32)
    inside = (places[None, :] >= starts[:, None]) & (
        places[None, :] < (starts + owner_lengths)[:, None]
    )
    scores = factor * jnp.einsum(
        "qc,pc->qp",
        all_heads.reshape(slot_rows * total_heads, probe_width),
        latent_cache,
        preferred_element_type=jnp.float32,
    )
    scores = scores.reshape(slot_rows, total_heads, key_rows)
    weights = jnp.where(inside[:, None, :], jnp.exp(scores), 0.0).astype(jnp.bfloat16)
    numerator = jnp.einsum(
        "khp,pl->khl", weights, latent_cache[:, :LATENT], preferred_element_type=jnp.float32
    )
    denominator = jnp.sum(weights.astype(jnp.float32), axis=2)
    return (numerator, denominator)


def body(
    hidden,
    attn_gain,
    w_query,
    w_latent,
    w_key_up,
    w_value_up,
    w_out,
    latent_cache,
    cache_lengths,
    request_slot,
    ffn_gain,
    w_router,
    routes,
    expert_gate,
    expert_up,
    expert_down,
):
    local_rows = hidden.shape[0]
    quarter_width = hidden.shape[1]
    local_heads = w_key_up.shape[0]
    peer_count = lax.axis_size("tok")
    head_index = lax.axis_index("head")
    tok_index = lax.axis_index("tok")
    row_ids = jnp.arange(local_rows, dtype=jnp.int32)
    gathered = lax.all_gather(hidden, "head", axis=1, tiled=True)
    widened = gathered.astype(jnp.float32)
    inv_attn = lax.rsqrt(jnp.mean(widened * widened, axis=1, keepdims=True) + NORM_EPS)
    normed_attn = (widened * inv_attn * attn_gain).astype(jnp.bfloat16)
    normed_part = lax.dynamic_slice_in_dim(
        normed_attn, head_index * quarter_width, quarter_width, 1
    )
    compressed = lax.psum(
        jnp.dot(normed_part, w_latent, preferred_element_type=jnp.float32), "head"
    )
    latent_new = compressed[:, :LATENT]
    latent_new = latent_new * lax.rsqrt(
        jnp.mean(latent_new * latent_new, axis=1, keepdims=True) + NORM_EPS
    )
    new_entry = jnp.concatenate(
        [latent_new, rotate_pairs(compressed[:, LATENT:], cache_lengths)], axis=1
    ).astype(jnp.bfloat16)
    queries = jnp.dot(normed_attn, w_query, preferred_element_type=jnp.float32).astype(jnp.bfloat16)
    queries = queries.reshape(local_rows, local_heads, NOPE + ROPE)
    absorbed = jnp.einsum(
        "bhn,hnl->bhl", queries[:, :, :NOPE], w_key_up, preferred_element_type=jnp.float32
    ).astype(jnp.bfloat16)
    turned = rotate_pairs(queries[:, :, NOPE:].astype(jnp.float32), cache_lengths).astype(
        jnp.bfloat16
    )
    probes = jnp.concatenate([absorbed, turned], axis=2)
    factor = (NOPE + ROPE) ** (-0.5)
    self_score = factor * jnp.einsum(
        "bhc,bc->bh", probes, new_entry, preferred_element_type=jnp.float32
    )
    self_weight = jnp.exp(self_score).astype(jnp.bfloat16).astype(jnp.float32)
    per_owner = max(1, local_rows // peer_count)
    buffer_rows = peer_count * per_owner
    buffer_ids = jnp.arange(buffer_rows, dtype=jnp.int32)
    dest_owner = request_slot // local_rows
    earlier_same = (dest_owner[None, :] == dest_owner[:, None]) & (
        row_ids[None, :] < row_ids[:, None]
    )
    send_place = dest_owner * per_owner + jnp.sum(earlier_same.astype(jnp.int32), axis=1)
    all_probes, all_slots, all_lengths = (
        lax.all_gather(probes, "tok", axis=0, tiled=True),
        lax.all_gather(request_slot, "tok", axis=0, tiled=True),
        lax.all_gather(cache_lengths, "tok", axis=0, tiled=True),
    )
    total_rows = all_slots.shape[0]
    slot_hit = all_slots[None, :] == (tok_index * local_rows + row_ids)[:, None]
    request_at = jnp.sum(
        jnp.where(slot_hit, jnp.arange(total_rows, dtype=jnp.int32)[None, :], 0), axis=1
    )
    owner_probes = all_probes[request_at]
    owner_lengths = all_lengths[request_at]
    owned_here = (
        (all_slots // local_rows == tok_index).astype(jnp.int32).reshape(peer_count, local_rows)
    )
    prior_count = (jnp.cumsum(owned_here, axis=1) - owned_here).reshape(total_rows)
    back_index = request_at // local_rows * per_owner + prior_count[request_at]
    all_heads = lax.all_gather(owner_probes, "head", axis=1, tiled=True)
    numerator, denominator = owner_attend(
        all_heads, owner_lengths, latent_cache, head_index, factor
    )
    group_num, group_den = (
        lax.psum_scatter(numerator, "head", scatter_dimension=1, tiled=True),
        lax.psum_scatter(denominator, "head", scatter_dimension=1, tiled=True),
    )
    at_place = buffer_ids[:, None] == back_index[None, :]
    slot_of_place = jnp.sum(jnp.where(at_place, row_ids[None, :], 0), axis=1) + local_rows * (
        1 - jnp.max(at_place.astype(jnp.int32), axis=1)
    )
    padded_num = jnp.concatenate(
        [group_num, jnp.zeros((1, local_heads, LATENT), jnp.float32)], axis=0
    )
    padded_den = jnp.concatenate([group_den, jnp.zeros((1, local_heads), jnp.float32)], axis=0)
    got_num, got_den = (
        lax.all_to_all(
            padded_num[slot_of_place].reshape(peer_count, per_owner, local_heads, LATENT),
            "tok",
            split_axis=0,
            concat_axis=0,
            tiled=True,
        ),
        lax.all_to_all(
            padded_den[slot_of_place].reshape(peer_count, per_owner, local_heads),
            "tok",
            split_axis=0,
            concat_axis=0,
            tiled=True,
        ),
    )
    back_num = got_num.reshape(buffer_rows, local_heads, LATENT)
    back_den = got_den.reshape(buffer_rows, local_heads)
    total_num = back_num[send_place] + self_weight[:, :, None] * new_entry[:, None, :LATENT].astype(
        jnp.float32
    )
    total_den = back_den[send_place] + self_weight
    mixed_latent = (total_num / total_den[:, :, None]).astype(jnp.bfloat16)
    head_out = jnp.einsum(
        "bhl,hld->bhd", mixed_latent, w_value_up, preferred_element_type=jnp.float32
    ).astype(jnp.bfloat16)
    head_out = head_out.reshape(local_rows, local_heads * NOPE)
    attn_piece = lax.psum_scatter(
        jnp.dot(head_out, w_out, preferred_element_type=jnp.float32),
        "head",
        scatter_dimension=1,
        tiled=True,
    )
    attended = (hidden.astype(jnp.float32) + attn_piece).astype(jnp.bfloat16)
    attended_wide = attended.astype(jnp.float32)
    gained = (attended_wide * ffn_gain).astype(jnp.bfloat16)
    squares, logit_part = lax.psum(
        (
            jnp.sum(attended_wide * attended_wide, axis=1),
            jnp.dot(gained, w_router, preferred_element_type=jnp.float32),
        ),
        "head",
    )
    inv_ffn = lax.rsqrt(squares / D + NORM_EPS)
    logits = logit_part * inv_ffn[:, None]
    normed_ffn = (attended_wide * ffn_gain * inv_ffn[:, None]).astype(jnp.bfloat16)
    expert_count = w_router.shape[1]
    route_count = routes.shape[1]
    expert_ids = jnp.arange(expert_count, dtype=jnp.int32)
    named = routes[:, :, None] == expert_ids[None, None, :]
    picked = jnp.sum(jnp.where(named, logits[:, None, :], 0.0), axis=2)
    lifted = jnp.exp(picked)
    route_weight = lifted / jnp.sum(lifted, axis=1, keepdims=True)
    struck = jnp.max(named.astype(jnp.int32), axis=1)
    earlier_hits = jnp.cumsum(struck, axis=0) - struck
    capacity = min(local_rows, max(2, 2 * local_rows * route_count // expert_count))
    route_place = routes * capacity + jnp.take_along_axis(earlier_hits, routes, axis=1)
    slot_total = expert_count * capacity
    slot_ids = jnp.arange(slot_total, dtype=jnp.int32)
    filled = route_place[None, :, :] == slot_ids[:, None, None]
    source_token = jnp.sum(
        jnp.where(filled, row_ids[None, :, None], 0), axis=(1, 2)
    ) + local_rows * (1 - jnp.max(filled.astype(jnp.int32), axis=(1, 2)))
    full_rows = lax.all_gather(normed_ffn, "head", axis=1, tiled=True)
    padded_rows = jnp.concatenate(
        [full_rows, jnp.zeros((1, full_rows.shape[1]), jnp.bfloat16)], axis=0
    )
    arrived = lax.all_to_all(
        padded_rows[source_token].reshape(expert_count, capacity, full_rows.shape[1]),
        "tok",
        split_axis=0,
        concat_axis=0,
        tiled=True,
    )
    expert_in = arrived.reshape(peer_count * capacity, full_rows.shape[1])
    gate_value = jnp.dot(expert_in, expert_gate[0], preferred_element_type=jnp.float32)
    up_value = jnp.dot(expert_in, expert_up[0], preferred_element_type=jnp.float32)
    activity = (jax.nn.silu(gate_value) * up_value).astype(jnp.bfloat16)
    expert_share = lax.psum_scatter(
        jnp.dot(activity, expert_down[0], preferred_element_type=jnp.float32).astype(jnp.bfloat16),
        "head",
        scatter_dimension=1,
        tiled=True,
    )
    returned = lax.all_to_all(
        expert_share.reshape(peer_count, capacity, quarter_width),
        "tok",
        split_axis=0,
        concat_axis=0,
        tiled=True,
    )
    chosen_rows = returned.reshape(slot_total, quarter_width)[route_place]
    expert_mix = jnp.sum(route_weight[:, :, None] * chosen_rows.astype(jnp.float32), axis=1).astype(
        jnp.bfloat16
    )
    return (new_entry, attended, expert_mix)


MESH_ID = pl.DeviceIdType.MESH
KEY_BLOCK = 1664
KEY_CUTS = (0, 384, 768, 1152, 1536, 1664)
WINDOW = 4
VMEM_LIMIT = 48 * 1024 * 1024


def meet(partners):
    barrier = pltpu.get_barrier_semaphore()
    for partner in partners:
        pl.semaphore_signal(barrier, inc=1, device_id=partner, device_id_type=MESH_ID)
    pl.semaphore_wait(barrier, len(partners))


def in_vmem(count):
    return [pl.BlockSpec(memory_space=pltpu.VMEM)] * count


def swap_pair(arrays, number):
    count = len(arrays)

    def kernel(*refs):
        ins, outs = refs[:count], refs[count : 2 * count]
        send_sem, recv_sem = refs[2 * count :]
        partner = (lax.axis_index("tok"), 1 - lax.axis_index("head"))
        meet([partner])
        copies = []
        for i in range(count):
            copy = pltpu.make_async_remote_copy(
                src_ref=ins[i],
                dst_ref=outs[i],
                send_sem=send_sem.at[i],
                recv_sem=recv_sem.at[i],
                device_id=partner,
                device_id_type=MESH_ID,
            )
            copy.start()
            copies.append(copy)
        for copy in copies:
            copy.wait()

    return pl.pallas_call(
        kernel,
        out_shape=[jax.ShapeDtypeStruct(a.shape, a.dtype) for a in arrays],
        in_specs=in_vmem(count),
        out_specs=in_vmem(count),
        scratch_shapes=[pltpu.SemaphoreType.DMA((count,)), pltpu.SemaphoreType.DMA((count,))],
        compiler_params=pltpu.CompilerParams(
            collective_id=number, has_side_effects=True, vmem_limit_bytes=VMEM_LIMIT
        ),
        name=f"swap_pair_{number}",
    )(*arrays)


def to_owners(blocks, notes, number):
    peers = blocks.shape[0]

    def kernel(src, src_notes, out, out_notes, send_sem, recv_sem, pass_sem, note_sem, own_sem):
        tok, head = lax.axis_index("tok"), lax.axis_index("head")
        partner = (tok, 1 - head)
        others = [lax.rem(tok + d, peers) for d in range(1, peers)]
        meet([partner] + [(there, head) for there in others])

        def remote(source, dest, first, second, target):
            return pltpu.make_async_remote_copy(
                src_ref=source,
                dst_ref=dest,
                send_sem=first,
                recv_sem=second,
                device_id=target,
                device_id_type=MESH_ID,
            )

        sends = []
        for i, there in enumerate(others):
            sends.append(
                remote(
                    src.at[there],
                    out.at[head, tok],
                    send_sem.at[i],
                    recv_sem.at[head, tok],
                    (there, head),
                )
            )
            sends[-1].start()
        sends.append(
            remote(
                src.at[tok], out.at[head, tok], pass_sem.at[0], recv_sem.at[head, tok], partner
            )
        )
        sends[-1].start()
        for i, there in enumerate(others):
            sends.append(
                remote(
                    src_notes.at[there],
                    out_notes.at[tok],
                    send_sem.at[peers + i],
                    note_sem.at[tok],
                    (there, head),
                )
            )
            sends[-1].start()
        own = [
            pltpu.make_async_copy(src.at[tok], out.at[head, tok], own_sem.at[0]),
            pltpu.make_async_copy(src_notes.at[tok], out_notes.at[tok], own_sem.at[1]),
        ]
        for copy in own:
            copy.start()
        for i, there in enumerate(others):
            spot = out.at[head, there]
            remote(spot, spot, send_sem.at[0], recv_sem.at[head, there], partner).wait_recv()
            sends.append(
                remote(spot, spot, pass_sem.at[1 + i], recv_sem.at[head, there], partner)
            )
            sends[-1].start()
        for there in [tok] + others:
            spot = out.at[1 - head, there]
            remote(spot, spot, send_sem.at[0], recv_sem.at[1 - head, there], partner).wait_recv()
        for there in others:
            spot = out_notes.at[there]
            remote(spot, spot, send_sem.at[0], note_sem.at[there], partner).wait_recv()
        for copy in sends:
            copy.wait_send()
        for copy in own:
            copy.wait()

    return pl.pallas_call(
        kernel,
        out_shape=[
            jax.ShapeDtypeStruct((2,) + blocks.shape, blocks.dtype),
            jax.ShapeDtypeStruct(notes.shape, notes.dtype),
        ],
        in_specs=in_vmem(2),
        out_specs=in_vmem(2),
        scratch_shapes=[
            pltpu.SemaphoreType.DMA((2 * peers,)),
            pltpu.SemaphoreType.DMA((2, peers)),
            pltpu.SemaphoreType.DMA((peers,)),
            pltpu.SemaphoreType.DMA((peers,)),
            pltpu.SemaphoreType.DMA((2,)),
        ],
        compiler_params=pltpu.CompilerParams(
            collective_id=number, has_side_effects=True, vmem_limit_bytes=VMEM_LIMIT
        ),
        name="to_owners",
    )(blocks, notes)


def gather_rows(block, peers, number):
    rows, width = block.shape
    half = rows // 2
    layers = peers // 4

    def kernel(src, out, send_sem, recv_sem, own_sem):
        tok, x = lax.axis_index("tok"), lax.axis_index("head")
        z, y, core = tok // 4, (tok // 2) % 2, tok % 2

        def place(z_, y_, core_):
            return z_ * 4 + y_ * 2 + core_

        across_x = (tok, 1 - x)
        across_y = (place(z, 1 - y, core), x)
        sibling = (place(z, y, 1 - core), x)
        along_z = [(place(lax.rem(z + d, layers), y, core), x) for d in range(1, layers)]
        meet([across_x, across_y, sibling] + along_z)

        def spot(z_, y_, core_, x_, h):
            start = place(z_, y_, core_) * rows + (h or 0) * half
            size = rows if h is None else half
            return out.at[
                pl.ds(pl.multiple_of(start, half), size),
                pl.ds(pl.multiple_of(x_ * width, 128), width),
            ]

        def slot(z_, y_, core_, x_, h):
            return (place(z_, y_, core_) * 2 + x_) * 2 + (h or 0)

        sends = []

        def push(target, z_, y_, core_, x_, h, fresh=False):
            dst = spot(z_, y_, core_, x_, h)
            copy = pltpu.make_async_remote_copy(
                src_ref=src if fresh else dst,
                dst_ref=dst,
                send_sem=send_sem.at[len(sends)],
                recv_sem=recv_sem.at[slot(z_, y_, core_, x_, h)],
                device_id=target,
                device_id_type=MESH_ID,
            )
            copy.start()
            sends.append(copy)

        def land(z_, y_, core_, x_, h):
            dst = spot(z_, y_, core_, x_, h)
            pltpu.make_async_remote_copy(
                src_ref=dst,
                dst_ref=dst,
                send_sem=send_sem.at[0],
                recv_sem=recv_sem.at[slot(z_, y_, core_, x_, h)],
                device_id=sibling,
                device_id_type=MESH_ID,
            ).wait_recv()

        turns = [1, 3, 2][: layers - 1]
        for d in turns:
            push(along_z[d - 1], z, y, core, x, None, True)
        for target in (across_x, across_y, sibling):
            push(target, z, y, core, x, None, True)
        own = pltpu.make_async_copy(src, spot(z, y, core, x, None), own_sem)
        own.start()

        def second(z_):
            land(z_, 1 - y, core, x, None)
            push(across_x, z_, 1 - y, core, x, 0)
            land(z_, y, core, 1 - x, None)
            push(across_y, z_, y, core, 1 - x, 1)
            push(sibling, z_, 1 - y, core, x, None)
            push(sibling, z_, y, core, 1 - x, None)

        def third(z_):
            land(z_, 1 - y, core, 1 - x, 0)
            land(z_, 1 - y, core, 1 - x, 1)
            push(sibling, z_, 1 - y, core, 1 - x, None)

        for d in turns:
            z_ = lax.rem(z + d, layers)
            land(z_, y, core, x, None)
            for target in (across_x, across_y, sibling):
                push(target, z_, y, core, x, None)
            if d == turns[0]:
                second(z)
        for d in turns:
            second(lax.rem(z + d, layers))
        for d in [0] + turns:
            third(lax.rem(z + d, layers))
        for d in [0] + turns:
            z_ = lax.rem(z + d, layers)
            for y_ in (y, 1 - y):
                for x_ in (x, 1 - x):
                    land(z_, y_, 1 - core, x_, None)
        for copy in sends:
            copy.wait_send()
        own.wait()

    return pl.pallas_call(
        kernel,
        out_shape=jax.ShapeDtypeStruct((rows * peers, 2 * width), block.dtype),
        in_specs=in_vmem(1),
        out_specs=in_vmem(1)[0],
        scratch_shapes=[
            pltpu.SemaphoreType.DMA((64,)),
            pltpu.SemaphoreType.DMA((4 * peers,)),
            pltpu.SemaphoreType.DMA,
        ],
        compiler_params=pltpu.CompilerParams(
            collective_id=number, has_side_effects=True, vmem_limit_bytes=VMEM_LIMIT
        ),
        name="gather_rows",
    )(block)


def scatter_sums(parts, back, peers, number):
    layers = parts.shape[3]
    half, full = parts.shape[4:]
    width = full // 2

    def kernel(
        src, back_src, out, back_out, got_core, kept, got_first, mid, got_second, last, got_z,
        sends, recvs, back_sends, back_recvs, own_sem,
    ):
        tok, x = lax.axis_index("tok"), lax.axis_index("head")
        z, y, core = tok // 4, (tok // 2) % 2, tok % 2

        def place(z_, y_, core_):
            return z_ * 4 + y_ * 2 + core_

        across_x = (tok, 1 - x)
        across_y = (place(z, 1 - y, core), x)
        sibling = (place(z, y, 1 - core), x)
        along_z = [(place(lax.rem(z + d, layers), y, core), x) for d in range(1, layers)]
        others = [lax.rem(tok + d, peers) for d in range(1, peers)]
        meet([across_x] + [(there, x) for there in others])

        def copy_to(target, source, dest, index):
            copy = pltpu.make_async_remote_copy(
                src_ref=source,
                dst_ref=dest,
                send_sem=sends.at[index],
                recv_sem=recvs.at[index],
                device_id=target,
                device_id_type=MESH_ID,
            )
            copy.start()
            return copy

        def columns(x_):
            return pl.ds(pl.multiple_of(x_ * width, 128), width)

        def total(first, second):
            return first.astype(jnp.float32) + second.astype(jnp.float32)

        cores = [[None, None], [None, None]]
        for g in range(2):
            for h in range(2):
                y_ = (1 - y) if g == 0 else y
                cores[h][g] = copy_to(
                    sibling, src.at[h, 1 - core, y_], got_core.at[h, y_], 2 * h + g
                )

        backs = []
        for i, there in enumerate(others):
            copy = pltpu.make_async_remote_copy(
                src_ref=back_src.at[there],
                dst_ref=back_out.at[tok],
                send_sem=back_sends.at[i],
                recv_sem=back_recvs.at[tok],
                device_id=(there, x),
                device_id_type=MESH_ID,
            )
            copy.start()
            backs.append(copy)
        own = pltpu.make_async_copy(back_src.at[tok], back_out.at[tok], own_sem)
        own.start()

        def fold_core(h, y_):
            @pl.loop(0, layers)
            def _(z_):
                kept[h, y_, z_] = total(src[h, core, y_, z_], got_core[h, y_, z_]).astype(
                    kept.dtype
                )

        cores[1][0].wait_recv()
        fold_core(1, 1 - y)
        first_y = copy_to(across_y, kept.at[1, 1 - y], got_first.at[1], 4)
        cores[0][0].wait_recv()
        fold_core(0, 1 - y)
        first_x = [
            copy_to(
                across_x,
                kept.at[0, 1 - y, slice(None), slice(None), columns(1 - x)],
                got_first.at[0, slice(None), slice(None), pl.ds(0, width)],
                5,
            )
        ]
        cores[0][1].wait_recv()
        fold_core(0, y)
        first_x.append(
            copy_to(
                across_x,
                kept.at[0, y, slice(None), slice(None), columns(1 - x)],
                got_first.at[0, slice(None), slice(None), pl.ds(width, width)],
                6,
            )
        )
        cores[1][1].wait_recv()
        fold_core(1, y)

        first_x[0].wait_recv()

        @pl.loop(0, layers)
        def _(z_):
            mid[0, z_] = total(
                kept[0, 1 - y, z_, :, columns(x)], got_first[0, z_, :, :width]
            ).astype(mid.dtype)

        second_y = copy_to(across_y, mid.at[0], got_second.at[0], 7)

        first_y.wait_recv()

        @pl.loop(0, layers)
        def _(z_):
            mid[1, z_] = total(
                kept[1, y, z_, :, columns(1 - x)], got_first[1, z_, :, columns(1 - x)]
            ).astype(mid.dtype)

        second_x = copy_to(across_x, mid.at[1], got_second.at[1], 8)
        first_x[1].wait_recv()

        zs = []

        def send_z(h):
            for d in range(1, layers):
                z_ = lax.rem(z + d, layers)
                zs.append(
                    copy_to(
                        along_z[d - 1], last.at[h, z_], got_z.at[h, d - 1], 9 + h * layers + d - 1
                    )
                )

        second_y.wait_recv()

        @pl.loop(0, layers)
        def _(z_):
            last[0, z_] = (
                total(kept[0, y, z_, :, columns(x)], got_first[0, z_, :, width:])
                + got_second[0, z_].astype(jnp.float32)
            ).astype(last.dtype)

        send_z(0)
        second_x.wait_recv()

        @pl.loop(0, layers)
        def _(z_):
            last[1, z_] = (
                total(kept[1, y, z_, :, columns(x)], got_first[1, z_, :, columns(x)])
                + got_second[1, z_].astype(jnp.float32)
            ).astype(last.dtype)

        send_z(1)
        for copy in zs:
            copy.wait_recv()
        for h in range(2):
            acc = last[h, z].astype(jnp.float32)
            for d in range(1, layers):
                acc = acc + got_z[h, d - 1].astype(jnp.float32)
            out[h] = acc.astype(out.dtype)
        for there in others:
            spot = back_out.at[there]
            pltpu.make_async_remote_copy(
                src_ref=spot,
                dst_ref=spot,
                send_sem=back_sends.at[0],
                recv_sem=back_recvs.at[there],
                device_id=sibling,
                device_id_type=MESH_ID,
            ).wait_recv()
        for copy in backs:
            copy.wait_send()
        own.wait()
        for copy in cores[0] + cores[1] + first_x + [first_y, second_y, second_x] + zs:
            copy.wait_send()

    kind = parts.dtype
    return pl.pallas_call(
        kernel,
        out_shape=[
            jax.ShapeDtypeStruct((2, half, width), kind),
            jax.ShapeDtypeStruct(back.shape, back.dtype),
        ],
        in_specs=in_vmem(2),
        out_specs=in_vmem(2),
        scratch_shapes=[
            pltpu.VMEM((2, 2, layers, half, full), kind),
            pltpu.VMEM((2, 2, layers, half, full), kind),
            pltpu.VMEM((2, layers, half, full), kind),
            pltpu.VMEM((2, layers, half, width), kind),
            pltpu.VMEM((2, layers, half, width), kind),
            pltpu.VMEM((2, layers, half, width), kind),
            pltpu.VMEM((2, layers - 1, half, width), kind),
            pltpu.SemaphoreType.DMA((9 + 2 * layers,)),
            pltpu.SemaphoreType.DMA((9 + 2 * layers,)),
            pltpu.SemaphoreType.DMA((peers,)),
            pltpu.SemaphoreType.DMA((peers,)),
            pltpu.SemaphoreType.DMA,
        ],
        compiler_params=pltpu.CompilerParams(
            collective_id=number, has_side_effects=True, vmem_limit_bytes=VMEM_LIMIT
        ),
        name="scatter_sums",
    )(parts, back)


def ragged_attend(queries, cache, ids, bounds, base, factor):
    slots, heads, width = queries.shape
    blocks = cache.shape[1] // KEY_BLOCK
    cuts = list(zip(KEY_CUTS[:-1], KEY_CUTS[1:]))

    def kernel(ids_ref, bounds_ref, base_ref, q_ref, kv_ref, num_ref, den_ref):
        j = pl.program_id(0)

        @pl.when(j == 0)
        def _():
            num_ref[...] = jnp.zeros_like(num_ref)
            den_ref[...] = jnp.zeros_like(den_ref)

        found = []
        for i, (low, high) in enumerate(cuts):
            size = high - low
            kv = kv_ref[:, low:high]
            who = [ids_ref[(j * len(cuts) + i) * WINDOW + w] for w in range(WINDOW)]
            some = jnp.concatenate([q_ref[r] for r in who], axis=0)
            scores = factor * jnp.dot(some, kv, preferred_element_type=jnp.float32)
            places = (
                base_ref[0]
                + j * KEY_BLOCK
                + low
                + lax.broadcasted_iota(jnp.int32, (heads, size), 1)
            )
            lifted = jnp.exp(scores)
            weights = jnp.concatenate(
                [
                    jnp.where(
                        (places >= bounds_ref[r]) & (places < bounds_ref[slots + r]),
                        lifted[w * heads : (w + 1) * heads],
                        0.0,
                    )
                    for w, r in enumerate(who)
                ],
                axis=0,
            ).astype(jnp.bfloat16)
            num = lax.dot_general(
                weights,
                kv[:LATENT],
                (((1,), (1,)), ((), ())),
                preferred_element_type=jnp.float32,
            )
            wide = weights.astype(jnp.float32)
            den = sum(wide[:, k : k + 128] for k in range(0, size, 128))
            found.append((who, num, den))
        for who, num, den in found:
            for w, r in enumerate(who):
                rows = slice(w * heads, (w + 1) * heads)
                num_ref[r] += num[rows]
                den_ref[r] += den[rows]

    return pl.pallas_call(
        kernel,
        out_shape=[
            jax.ShapeDtypeStruct((slots, heads, LATENT), jnp.float32),
            jax.ShapeDtypeStruct((slots, heads, 128), jnp.float32),
        ],
        grid_spec=pltpu.PrefetchScalarGridSpec(
            num_scalar_prefetch=3,
            grid=(blocks,),
            in_specs=[
                pl.BlockSpec((slots, heads, width), lambda j, *_: (0, 0, 0)),
                pl.BlockSpec((width, KEY_BLOCK), lambda j, *_: (0, j)),
            ],
            out_specs=[
                pl.BlockSpec((slots, heads, LATENT), lambda j, *_: (0, 0, 0)),
                pl.BlockSpec((slots, heads, 128), lambda j, *_: (0, 0, 0)),
            ],
        ),
        compiler_params=pltpu.CompilerParams(vmem_limit_bytes=VMEM_LIMIT),
        name="ragged_attend",
    )(ids, bounds, base, queries, cache)


def pick_rows(chosen, values):
    return jnp.dot(
        chosen.astype(jnp.bfloat16), values, preferred_element_type=jnp.float32
    ).astype(values.dtype)


def direct_body(
    hidden,
    attn_gain,
    w_query,
    w_latent,
    w_key_up,
    w_value_up,
    w_out,
    latent_cache,
    cache_lengths,
    request_slot,
    ffn_gain,
    w_router,
    routes,
    expert_gate,
    expert_up,
    expert_down,
):
    f32, bf16 = jnp.float32, jnp.bfloat16
    rows, part = hidden.shape
    peers = lax.axis_size("tok")
    each = rows // peers
    local_heads = w_key_up.shape[0]
    expert_count = w_router.shape[1]
    head = lax.axis_index("head")
    tok = lax.axis_index("tok")
    ids = jnp.arange(rows, dtype=jnp.int32)

    owner = request_slot // rows
    earlier = (owner[None, :] == owner[:, None]) & (ids[None, :] < ids[:, None])
    send_place = owner * each + jnp.sum(earlier.astype(jnp.int32), axis=1)
    placed = ids[:, None] == send_place[None, :]
    route_mask = jnp.max(
        (routes[:, :, None] == jnp.arange(expert_count, dtype=jnp.int32)).astype(jnp.int32), axis=1
    )
    meta = jnp.concatenate(
        [
            (request_slot % rows)[:, None],
            (cache_lengths // 64)[:, None],
            (cache_lengths % 64)[:, None],
            route_mask,
        ],
        axis=1,
    ).astype(bf16)
    meta = jnp.pad(meta, ((0, 0), (0, 128 // each - meta.shape[1])))
    sent_meta = jnp.dot(placed.astype(bf16), meta, preferred_element_type=f32)
    blocks = pick_rows(placed, hidden).reshape(peers, each * part // 128, 128)
    wide, meta = to_owners(
        blocks, sent_meta.astype(jnp.int32).reshape(peers, 1, 128), 0
    )
    wide = wide.reshape(2, rows, part)
    meta = meta.reshape(rows, 128 // each)[:, : 3 + expert_count]
    slot, lengths = meta[:, 0], meta[:, 1] * 64 + meta[:, 2]
    mask = meta[:, 3:]
    starts = jnp.sum(jnp.where(slot[None, :] < slot[:, None], lengths[None, :], 0), axis=1)
    full = jnp.concatenate([wide[0], wide[1]], axis=1).astype(f32)
    mine = lax.dynamic_index_in_dim(wide, head, 0, keepdims=False)

    inv_attn = lax.rsqrt(jnp.mean(full * full, axis=1, keepdims=True) + NORM_EPS)
    normed = (full * inv_attn * attn_gain).astype(bf16)
    normed_part = lax.dynamic_slice_in_dim(normed, head * part, part, 1)
    compressed = jnp.dot(normed_part, w_latent, preferred_element_type=f32)
    queries = jnp.dot(normed, w_query, preferred_element_type=f32).astype(bf16)
    queries = queries.reshape(rows, local_heads, NOPE + ROPE)
    absorbed = jnp.einsum(
        "bhn,hnl->bhl", queries[:, :, :NOPE], w_key_up, preferred_element_type=f32
    ).astype(bf16)
    turned = rotate_pairs(queries[:, :, NOPE:].astype(f32), lengths).astype(bf16)
    probes = jnp.concatenate([absorbed, turned], axis=2)
    far_probes, far_compressed = swap_pair([probes, compressed], 1)
    compressed = compressed + far_compressed
    latent_new = compressed[:, :LATENT]
    latent_new = latent_new * lax.rsqrt(
        jnp.mean(latent_new * latent_new, axis=1, keepdims=True) + NORM_EPS
    )
    new_entry = jnp.concatenate(
        [latent_new, rotate_pairs(compressed[:, LATENT:], lengths)], axis=1
    ).astype(bf16)
    factor = (NOPE + ROPE) ** (-0.5)
    self_score = factor * jnp.einsum(
        "bhc,bc->bh", probes, new_entry, preferred_element_type=f32
    )
    self_weight = jnp.exp(self_score).astype(bf16).astype(f32)

    key_rows = latent_cache.shape[0]
    block_starts = (
        head * key_rows
        + jnp.arange(0, key_rows, KEY_BLOCK, dtype=jnp.int32)[:, None]
        + jnp.array(KEY_CUTS[:-1], jnp.int32)
    ).reshape(-1)
    ends = starts + lengths
    first = jnp.sum((ends[None, :] <= block_starts[:, None]).astype(jnp.int32), axis=1)
    first = jnp.minimum(first, rows - WINDOW)
    window = first[:, None] + jnp.arange(WINDOW, dtype=jnp.int32)
    window_ids = jnp.sum(
        jnp.where(window[:, :, None] == slot[None, None, :], ids[None, None, :], 0), axis=2
    )
    numerator, denominator = ragged_attend(
        jnp.concatenate([probes, far_probes], axis=1),
        latent_cache.T,
        window_ids.reshape(-1).astype(jnp.int32),
        jnp.concatenate([starts, ends]).astype(jnp.int32),
        (head * key_rows).reshape(1).astype(jnp.int32),
        factor,
    )
    denominator = jnp.sum(denominator, axis=2)
    far_num, far_den = swap_pair(
        [
            numerator[:, local_heads:].astype(bf16).reshape(rows * local_heads, LATENT),
            denominator[:, local_heads:].reshape(rows * local_heads // 128, 128),
        ],
        2,
    )
    total_num = (
        numerator[:, :local_heads]
        + far_num.reshape(rows, local_heads, LATENT).astype(f32)
        + self_weight[:, :, None] * new_entry[:, None, :LATENT].astype(f32)
    )
    total_den = denominator[:, :local_heads] + far_den.reshape(rows, local_heads) + self_weight
    mixed = (total_num / total_den[:, :, None]).astype(bf16)
    head_out = jnp.einsum("bhl,hld->bhd", mixed, w_value_up, preferred_element_type=f32)
    head_out = head_out.astype(bf16).reshape(rows, local_heads * NOPE)
    piece = jnp.dot(head_out, w_out, preferred_element_type=f32)
    kept = lax.dynamic_slice_in_dim(piece, head * part, part, 1)
    given = lax.dynamic_slice_in_dim(piece, (1 - head) * part, part, 1)
    (far_piece,) = swap_pair([given], 3)
    attended = (mine.astype(f32) + (kept + far_piece)).astype(bf16)

    attended_wide = attended.astype(f32)
    gained = (attended_wide * ffn_gain).astype(bf16)
    squares = jnp.sum(attended_wide * attended_wide, axis=1, keepdims=True)
    logit_part = jnp.dot(gained, w_router, preferred_element_type=f32)
    notes = jnp.concatenate([squares, logit_part], axis=1)
    high = notes.astype(bf16)
    low = (notes - high.astype(f32)).astype(bf16)
    notes = jnp.concatenate([high, low, mask.astype(bf16)], axis=1)
    notes = jnp.pad(notes, ((0, 0), (0, 128 - notes.shape[1])))
    gathered = gather_rows(jnp.concatenate([gained, notes], axis=1), peers, 4)

    span = part + 128
    tokens = jnp.concatenate([gathered[:, :part], gathered[:, span : span + part]], axis=1)
    marks = gathered[:, part:span].astype(f32), gathered[:, span + part :].astype(f32)
    count = 1 + expert_count
    sums = sum(m[:, :count] + m[:, count : 2 * count] for m in marks)
    inv_ffn = lax.rsqrt(sums[:, :1] / (2 * part) + NORM_EPS)
    lifted = jnp.exp(sums[:, 1:] * inv_ffn) * marks[0][:, 2 * count : 2 * count + expert_count]
    here = (jnp.arange(expert_count, dtype=jnp.int32) == tok).astype(f32)
    weight = jnp.sum(lifted * here, axis=1) / jnp.sum(lifted, axis=1)
    gate_value = jnp.dot(tokens, expert_gate[0], preferred_element_type=f32) * inv_ffn
    up_value = jnp.dot(tokens, expert_up[0], preferred_element_type=f32) * inv_ffn
    activity = (jax.nn.silu(gate_value) * up_value).astype(bf16)
    every = jnp.arange(rows * peers, dtype=jnp.int32)
    half = rows // 2
    layers = peers // 4
    h_, c_, y_, z_ = (
        every // (half * peers),
        every // (half * peers // 2) % 2,
        every // (half * layers) % 2,
        every // half % layers,
    )
    device = z_ * 4 + y_ * 2 + c_
    inner = h_ * half + every % half
    source = inner // each * rows + device * each + inner % each
    moved = source[:, None] == every[None, :]
    activity = pick_rows(moved, activity)
    weight = jnp.sum(jnp.where(moved, weight[None, :], 0.0), axis=1)
    terms = jnp.dot(activity, expert_down[0], preferred_element_type=f32) * weight[:, None]
    terms = terms.astype(bf16).reshape(2, 2, 2, layers, half, 2 * part)
    back = jnp.concatenate([attended, new_entry], axis=1)
    back = jnp.pad(back, ((0, 0), (0, 2 * part - back.shape[1])))
    summed, back = scatter_sums(terms, back.reshape(peers, each * 2 * part // 128, 128), peers, 5)
    mixed_back = jnp.concatenate([back.reshape(rows, 2 * part), summed.reshape(rows, part)], axis=1)
    final = pick_rows(placed.T, mixed_back)
    return (
        final[:, part : part + LATENT + ROPE],
        final[:, :part],
        final[:, 2 * part :],
    )


def solution(mesh):
    in_specs = (
        P("tok", "head"),
        P(),
        P(None, "head"),
        P("head", None),
        P("head", None, None),
        P("head", None, None),
        P("head", None),
        P(("tok", "head"), None),
        P("tok"),
        P("tok"),
        P("head"),
        P("head", None),
        P("tok", None),
        P("tok", None, "head"),
        P("tok", None, "head"),
        P("tok", "head", None),
    )
    out_specs = (P("tok", None), P("tok", "head"), P("tok", "head"))
    chosen = direct_body if (mesh.shape["tok"], mesh.shape["head"]) == (16, 2) else body
    return jax.shard_map(chosen, mesh=mesh, in_specs=in_specs, out_specs=out_specs, check_vma=False)
```

```python
import jax
import jax.numpy as jnp
from jax import lax
from jax.experimental import pallas as pl
from jax.experimental.pallas import tpu as pltpu
from jax.sharding import PartitionSpec as P

D = 2048
NOPE = 128
ROPE = 64
LATENT = 512


NORM_EPS = 1e-06


def rotate_pairs(values, places):
    halfway = values.shape[-1] // 2
    freqs = 10000.0 ** (-jnp.arange(halfway, dtype=jnp.float32) / halfway)
    angles = places.astype(jnp.float32).reshape(places.shape + (1,) * (values.ndim - 1)) * freqs
    cosine = jnp.cos(angles)
    sine = jnp.sin(angles)
    first_half = values[..., :halfway]
    second_half = values[..., halfway:]
    return jnp.concatenate(
        [first_half * cosine - second_half * sine, first_half * sine + second_half * cosine],
        axis=-1,
    )


def owner_attend(all_heads, owner_lengths, latent_cache, head_index, factor):
    slot_rows = all_heads.shape[0]
    total_heads = all_heads.shape[1]
    probe_width = all_heads.shape[2]
    key_rows = latent_cache.shape[0]
    starts = jnp.cumsum(owner_lengths) - owner_lengths
    places = head_index * key_rows + jnp.arange(key_rows, dtype=jnp.int32)
    inside = (places[None, :] >= starts[:, None]) & (
        places[None, :] < (starts + owner_lengths)[:, None]
    )
    scores = factor * jnp.einsum(
        "qc,pc->qp",
        all_heads.reshape(slot_rows * total_heads, probe_width),
        latent_cache,
        preferred_element_type=jnp.float32,
    )
    scores = scores.reshape(slot_rows, total_heads, key_rows)
    weights = jnp.where(inside[:, None, :], jnp.exp(scores), 0.0).astype(jnp.bfloat16)
    numerator = jnp.einsum(
        "khp,pl->khl", weights, latent_cache[:, :LATENT], preferred_element_type=jnp.float32
    )
    denominator = jnp.sum(weights.astype(jnp.float32), axis=2)
    return (numerator, denominator)


def body(
    hidden,
    attn_gain,
    w_query,
    w_latent,
    w_key_up,
    w_value_up,
    w_out,
    latent_cache,
    cache_lengths,
    request_slot,
    ffn_gain,
    w_router,
    routes,
    expert_gate,
    expert_up,
    expert_down,
):
    local_rows = hidden.shape[0]
    quarter_width = hidden.shape[1]
    local_heads = w_key_up.shape[0]
    peer_count = lax.axis_size("tok")
    head_index = lax.axis_index("head")
    tok_index = lax.axis_index("tok")
    row_ids = jnp.arange(local_rows, dtype=jnp.int32)
    gathered = lax.all_gather(hidden, "head", axis=1, tiled=True)
    widened = gathered.astype(jnp.float32)
    inv_attn = lax.rsqrt(jnp.mean(widened * widened, axis=1, keepdims=True) + NORM_EPS)
    normed_attn = (widened * inv_attn * attn_gain).astype(jnp.bfloat16)
    normed_part = lax.dynamic_slice_in_dim(
        normed_attn, head_index * quarter_width, quarter_width, 1
    )
    compressed = lax.psum(
        jnp.dot(normed_part, w_latent, preferred_element_type=jnp.float32), "head"
    )
    latent_new = compressed[:, :LATENT]
    latent_new = latent_new * lax.rsqrt(
        jnp.mean(latent_new * latent_new, axis=1, keepdims=True) + NORM_EPS
    )
    new_entry = jnp.concatenate(
        [latent_new, rotate_pairs(compressed[:, LATENT:], cache_lengths)], axis=1
    ).astype(jnp.bfloat16)
    queries = jnp.dot(normed_attn, w_query, preferred_element_type=jnp.float32).astype(jnp.bfloat16)
    queries = queries.reshape(local_rows, local_heads, NOPE + ROPE)
    absorbed = jnp.einsum(
        "bhn,hnl->bhl", queries[:, :, :NOPE], w_key_up, preferred_element_type=jnp.float32
    ).astype(jnp.bfloat16)
    turned = rotate_pairs(queries[:, :, NOPE:].astype(jnp.float32), cache_lengths).astype(
        jnp.bfloat16
    )
    probes = jnp.concatenate([absorbed, turned], axis=2)
    factor = (NOPE + ROPE) ** (-0.5)
    self_score = factor * jnp.einsum(
        "bhc,bc->bh", probes, new_entry, preferred_element_type=jnp.float32
    )
    self_weight = jnp.exp(self_score).astype(jnp.bfloat16).astype(jnp.float32)
    per_owner = max(1, local_rows // peer_count)
    buffer_rows = peer_count * per_owner
    buffer_ids = jnp.arange(buffer_rows, dtype=jnp.int32)
    dest_owner = request_slot // local_rows
    earlier_same = (dest_owner[None, :] == dest_owner[:, None]) & (
        row_ids[None, :] < row_ids[:, None]
    )
    send_place = dest_owner * per_owner + jnp.sum(earlier_same.astype(jnp.int32), axis=1)
    all_probes, all_slots, all_lengths = (
        lax.all_gather(probes, "tok", axis=0, tiled=True),
        lax.all_gather(request_slot, "tok", axis=0, tiled=True),
        lax.all_gather(cache_lengths, "tok", axis=0, tiled=True),
    )
    total_rows = all_slots.shape[0]
    slot_hit = all_slots[None, :] == (tok_index * local_rows + row_ids)[:, None]
    request_at = jnp.sum(
        jnp.where(slot_hit, jnp.arange(total_rows, dtype=jnp.int32)[None, :], 0), axis=1
    )
    owner_probes = all_probes[request_at]
    owner_lengths = all_lengths[request_at]
    owned_here = (
        (all_slots // local_rows == tok_index).astype(jnp.int32).reshape(peer_count, local_rows)
    )
    prior_count = (jnp.cumsum(owned_here, axis=1) - owned_here).reshape(total_rows)
    back_index = request_at // local_rows * per_owner + prior_count[request_at]
    all_heads = lax.all_gather(owner_probes, "head", axis=1, tiled=True)
    numerator, denominator = owner_attend(
        all_heads, owner_lengths, latent_cache, head_index, factor
    )
    group_num, group_den = (
        lax.psum_scatter(numerator, "head", scatter_dimension=1, tiled=True),
        lax.psum_scatter(denominator, "head", scatter_dimension=1, tiled=True),
    )
    at_place = buffer_ids[:, None] == back_index[None, :]
    slot_of_place = jnp.sum(jnp.where(at_place, row_ids[None, :], 0), axis=1) + local_rows * (
        1 - jnp.max(at_place.astype(jnp.int32), axis=1)
    )
    padded_num = jnp.concatenate(
        [group_num, jnp.zeros((1, local_heads, LATENT), jnp.float32)], axis=0
    )
    padded_den = jnp.concatenate([group_den, jnp.zeros((1, local_heads), jnp.float32)], axis=0)
    got_num, got_den = (
        lax.all_to_all(
            padded_num[slot_of_place].reshape(peer_count, per_owner, local_heads, LATENT),
            "tok",
            split_axis=0,
            concat_axis=0,
            tiled=True,
        ),
        lax.all_to_all(
            padded_den[slot_of_place].reshape(peer_count, per_owner, local_heads),
            "tok",
            split_axis=0,
            concat_axis=0,
            tiled=True,
        ),
    )
    back_num = got_num.reshape(buffer_rows, local_heads, LATENT)
    back_den = got_den.reshape(buffer_rows, local_heads)
    total_num = back_num[send_place] + self_weight[:, :, None] * new_entry[:, None, :LATENT].astype(
        jnp.float32
    )
    total_den = back_den[send_place] + self_weight
    mixed_latent = (total_num / total_den[:, :, None]).astype(jnp.bfloat16)
    head_out = jnp.einsum(
        "bhl,hld->bhd", mixed_latent, w_value_up, preferred_element_type=jnp.float32
    ).astype(jnp.bfloat16)
    head_out = head_out.reshape(local_rows, local_heads * NOPE)
    attn_piece = lax.psum_scatter(
        jnp.dot(head_out, w_out, preferred_element_type=jnp.float32),
        "head",
        scatter_dimension=1,
        tiled=True,
    )
    attended = (hidden.astype(jnp.float32) + attn_piece).astype(jnp.bfloat16)
    attended_wide = attended.astype(jnp.float32)
    gained = (attended_wide * ffn_gain).astype(jnp.bfloat16)
    squares, logit_part = lax.psum(
        (
            jnp.sum(attended_wide * attended_wide, axis=1),
            jnp.dot(gained, w_router, preferred_element_type=jnp.float32),
        ),
        "head",
    )
    inv_ffn = lax.rsqrt(squares / D + NORM_EPS)
    logits = logit_part * inv_ffn[:, None]
    normed_ffn = (attended_wide * ffn_gain * inv_ffn[:, None]).astype(jnp.bfloat16)
    expert_count = w_router.shape[1]
    route_count = routes.shape[1]
    expert_ids = jnp.arange(expert_count, dtype=jnp.int32)
    named = routes[:, :, None] == expert_ids[None, None, :]
    picked = jnp.sum(jnp.where(named, logits[:, None, :], 0.0), axis=2)
    lifted = jnp.exp(picked)
    route_weight = lifted / jnp.sum(lifted, axis=1, keepdims=True)
    struck = jnp.max(named.astype(jnp.int32), axis=1)
    earlier_hits = jnp.cumsum(struck, axis=0) - struck
    capacity = min(local_rows, max(2, 2 * local_rows * route_count // expert_count))
    route_place = routes * capacity + jnp.take_along_axis(earlier_hits, routes, axis=1)
    slot_total = expert_count * capacity
    slot_ids = jnp.arange(slot_total, dtype=jnp.int32)
    filled = route_place[None, :, :] == slot_ids[:, None, None]
    source_token = jnp.sum(
        jnp.where(filled, row_ids[None, :, None], 0), axis=(1, 2)
    ) + local_rows * (1 - jnp.max(filled.astype(jnp.int32), axis=(1, 2)))
    full_rows = lax.all_gather(normed_ffn, "head", axis=1, tiled=True)
    padded_rows = jnp.concatenate(
        [full_rows, jnp.zeros((1, full_rows.shape[1]), jnp.bfloat16)], axis=0
    )
    arrived = lax.all_to_all(
        padded_rows[source_token].reshape(expert_count, capacity, full_rows.shape[1]),
        "tok",
        split_axis=0,
        concat_axis=0,
        tiled=True,
    )
    expert_in = arrived.reshape(peer_count * capacity, full_rows.shape[1])
    gate_value = jnp.dot(expert_in, expert_gate[0], preferred_element_type=jnp.float32)
    up_value = jnp.dot(expert_in, expert_up[0], preferred_element_type=jnp.float32)
    activity = (jax.nn.silu(gate_value) * up_value).astype(jnp.bfloat16)
    expert_share = lax.psum_scatter(
        jnp.dot(activity, expert_down[0], preferred_element_type=jnp.float32).astype(jnp.bfloat16),
        "head",
        scatter_dimension=1,
        tiled=True,
    )
    returned = lax.all_to_all(
        expert_share.reshape(peer_count, capacity, quarter_width),
        "tok",
        split_axis=0,
        concat_axis=0,
        tiled=True,
    )
    chosen_rows = returned.reshape(slot_total, quarter_width)[route_place]
    expert_mix = jnp.sum(route_weight[:, :, None] * chosen_rows.astype(jnp.float32), axis=1).astype(
        jnp.bfloat16
    )
    return (new_entry, attended, expert_mix)


MESH_ID = pl.DeviceIdType.MESH
KEY_BLOCK = 1664
KEY_CUTS = (0, 384, 768, 1152, 1536, 1664)
WINDOW = 4
VMEM_LIMIT = 48 * 1024 * 1024


def meet(partners):
    barrier = pltpu.get_barrier_semaphore()
    for partner in partners:
        pl.semaphore_signal(barrier, inc=1, device_id=partner, device_id_type=MESH_ID)
    pl.semaphore_wait(barrier, len(partners))


def in_vmem(count):
    return [pl.BlockSpec(memory_space=pltpu.VMEM)] * count


def swap_pair(arrays, number):
    count = len(arrays)

    def kernel(*refs):
        ins, outs = refs[:count], refs[count : 2 * count]
        send_sem, recv_sem = refs[2 * count :]
        partner = (lax.axis_index("tok"), 1 - lax.axis_index("head"))
        meet([partner])
        copies = []
        for i in range(count):
            copy = pltpu.make_async_remote_copy(
                src_ref=ins[i],
                dst_ref=outs[i],
                send_sem=send_sem.at[i],
                recv_sem=recv_sem.at[i],
                device_id=partner,
                device_id_type=MESH_ID,
            )
            copy.start()
            copies.append(copy)
        for copy in copies:
            copy.wait()

    return pl.pallas_call(
        kernel,
        out_shape=[jax.ShapeDtypeStruct(a.shape, a.dtype) for a in arrays],
        in_specs=in_vmem(count),
        out_specs=in_vmem(count),
        scratch_shapes=[pltpu.SemaphoreType.DMA((count,)), pltpu.SemaphoreType.DMA((count,))],
        compiler_params=pltpu.CompilerParams(
            collective_id=number, has_side_effects=True, vmem_limit_bytes=VMEM_LIMIT
        ),
        name=f"swap_pair_{number}",
    )(*arrays)


def to_owners(blocks, notes, number):
    peers = blocks.shape[0]

    def kernel(src, src_notes, out, out_notes, send_sem, recv_sem, pass_sem, note_sem, own_sem):
        tok, head = lax.axis_index("tok"), lax.axis_index("head")
        partner = (tok, 1 - head)
        others = [lax.rem(tok + d, peers) for d in range(1, peers)]
        meet([partner] + [(there, head) for there in others])

        def remote(source, dest, first, second, target):
            return pltpu.make_async_remote_copy(
                src_ref=source,
                dst_ref=dest,
                send_sem=first,
                recv_sem=second,
                device_id=target,
                device_id_type=MESH_ID,
            )

        sends = []
        for i, there in enumerate(others):
            sends.append(
                remote(
                    src.at[there],
                    out.at[head, tok],
                    send_sem.at[i],
                    recv_sem.at[head, tok],
                    (there, head),
                )
            )
            sends[-1].start()
        sends.append(
            remote(
                src.at[tok], out.at[head, tok], pass_sem.at[0], recv_sem.at[head, tok], partner
            )
        )
        sends[-1].start()
        for i, there in enumerate(others):
            sends.append(
                remote(
                    src_notes.at[there],
                    out_notes.at[tok],
                    send_sem.at[peers + i],
                    note_sem.at[tok],
                    (there, head),
                )
            )
            sends[-1].start()
        own = [
            pltpu.make_async_copy(src.at[tok], out.at[head, tok], own_sem.at[0]),
            pltpu.make_async_copy(src_notes.at[tok], out_notes.at[tok], own_sem.at[1]),
        ]
        for copy in own:
            copy.start()
        for i, there in enumerate(others):
            spot = out.at[head, there]
            remote(spot, spot, send_sem.at[0], recv_sem.at[head, there], partner).wait_recv()
            sends.append(
                remote(spot, spot, pass_sem.at[1 + i], recv_sem.at[head, there], partner)
            )
            sends[-1].start()
        for there in [tok] + others:
            spot = out.at[1 - head, there]
            remote(spot, spot, send_sem.at[0], recv_sem.at[1 - head, there], partner).wait_recv()
        for there in others:
            spot = out_notes.at[there]
            remote(spot, spot, send_sem.at[0], note_sem.at[there], partner).wait_recv()
        for copy in sends:
            copy.wait_send()
        for copy in own:
            copy.wait()

    return pl.pallas_call(
        kernel,
        out_shape=[
            jax.ShapeDtypeStruct((2,) + blocks.shape, blocks.dtype),
            jax.ShapeDtypeStruct(notes.shape, notes.dtype),
        ],
        in_specs=in_vmem(2),
        out_specs=in_vmem(2),
        scratch_shapes=[
            pltpu.SemaphoreType.DMA((2 * peers,)),
            pltpu.SemaphoreType.DMA((2, peers)),
            pltpu.SemaphoreType.DMA((peers,)),
            pltpu.SemaphoreType.DMA((peers,)),
            pltpu.SemaphoreType.DMA((2,)),
        ],
        compiler_params=pltpu.CompilerParams(
            collective_id=number, has_side_effects=True, vmem_limit_bytes=VMEM_LIMIT
        ),
        name="to_owners",
    )(blocks, notes)


def gather_experts(block, gate, up, down, order, select, peers, number):
    rows, width = block.shape
    half = rows // 2
    layers = peers // 4
    part = width - 128
    units, full = gate.shape
    some = rows * peers // 2

    def kernel(
        src, gate_any, up_any, down_any, order_ref, select_ref, terms, out,
        gate_ref, up_ref, down_ref, send_sem, recv_sem, own_sem, weight_sem,
    ):
        tok, x = lax.axis_index("tok"), lax.axis_index("head")
        z, y, core = tok // 4, (tok // 2) % 2, tok % 2

        def place(z_, y_, core_):
            return z_ * 4 + y_ * 2 + core_

        across_x = (tok, 1 - x)
        across_y = (place(z, 1 - y, core), x)
        sibling = (place(z, y, 1 - core), x)
        along_z = [(place(lax.rem(z + d, layers), y, core), x) for d in range(1, layers)]
        meet([across_x, across_y, sibling] + along_z)

        def spot(z_, y_, core_, x_, h):
            start = place(z_, y_, core_) * rows + (h or 0) * half
            size = rows if h is None else half
            return out.at[
                pl.ds(pl.multiple_of(start, half), size),
                pl.ds(pl.multiple_of(x_ * width, 128), width),
            ]

        def slot(z_, y_, core_, x_, h):
            return (place(z_, y_, core_) * 2 + x_) * 2 + (h or 0)

        sends = []

        def push(target, z_, y_, core_, x_, h, fresh=False):
            dst = spot(z_, y_, core_, x_, h)
            copy = pltpu.make_async_remote_copy(
                src_ref=src if fresh else dst,
                dst_ref=dst,
                send_sem=send_sem.at[len(sends)],
                recv_sem=recv_sem.at[slot(z_, y_, core_, x_, h)],
                device_id=target,
                device_id_type=MESH_ID,
            )
            copy.start()
            sends.append(copy)

        def land(z_, y_, core_, x_, h):
            dst = spot(z_, y_, core_, x_, h)
            pltpu.make_async_remote_copy(
                src_ref=dst,
                dst_ref=dst,
                send_sem=send_sem.at[0],
                recv_sem=recv_sem.at[slot(z_, y_, core_, x_, h)],
                device_id=sibling,
                device_id_type=MESH_ID,
            ).wait_recv()

        turns = [1, 3, 2][: layers - 1]
        for d in turns:
            push(along_z[d - 1], z, y, core, x, None, True)
        for target in (across_x, across_y, sibling):
            push(target, z, y, core, x, None, True)
        own = pltpu.make_async_copy(src, spot(z, y, core, x, None), own_sem)
        own.start()
        weights = [
            pltpu.make_async_copy(a, b, weight_sem.at[i])
            for i, (a, b) in enumerate(
                [(gate_any, gate_ref), (up_any, up_ref), (down_any, down_ref)]
            )
        ]
        for copy in weights:
            copy.start()

        def second(z_):
            land(z_, 1 - y, core, x, None)
            push(across_x, z_, 1 - y, core, x, 0)
            land(z_, y, core, 1 - x, None)
            push(across_y, z_, y, core, 1 - x, 1)
            push(sibling, z_, 1 - y, core, x, None)
            push(sibling, z_, y, core, 1 - x, None)

        def third(z_):
            land(z_, 1 - y, core, 1 - x, 0)
            land(z_, 1 - y, core, 1 - x, 1)
            push(sibling, z_, 1 - y, core, 1 - x, None)

        for d in turns:
            z_ = lax.rem(z + d, layers)
            land(z_, y, core, x, None)
            for target in (across_x, across_y, sibling):
                push(target, z_, y, core, x, None)
            if d == turns[0]:
                second(z)
        near = z + 1 - 2 * (z % 2)
        pairs = [(z, near), (lax.rem(z + 2, layers), lax.rem(near + 2, layers))]
        second(near)
        for z_ in pairs[1]:
            second(z_)

        def across(a, b):
            return lax.dot_general(
                a, b, (((1,), (1,)), ((), ())), preferred_element_type=jnp.float32
            )

        def product(a, b):
            return jnp.dot(a, b, preferred_element_type=jnp.float32)

        def expert(group):
            at = pl.ds(pl.multiple_of(group * some, some), some)
            left, right = out[at, part:width], out[at, width + part :]
            logits = product(left, select_ref[:, :128]) + product(right, select_ref[:, :128])
            named = product(left, select_ref[:, 128:256])
            squares = product(left, select_ref[:, 256:]) + product(right, select_ref[:, 256:])
            inv_ffn = lax.rsqrt(squares / full + NORM_EPS)
            lifted = jnp.where(named > 0.5, jnp.exp(logits * inv_ffn), 0.0)
            lane = lax.broadcasted_iota(jnp.int32, (some, 128), 1)
            mine = jnp.sum(jnp.where(lane == tok, lifted, 0.0), axis=1, keepdims=True)
            weight = mine / jnp.sum(lifted, axis=1, keepdims=True)
            inv_ffn = inv_ffn[:, :1]
            first, last = out[at, :part], out[at, width : width + part]
            gate_value = across(first, gate_ref[:, :part]) + across(last, gate_ref[:, part:])
            gate_value = gate_value * inv_ffn
            up_value = across(first, up_ref[:, :part]) + across(last, up_ref[:, part:])
            up_value = up_value * (inv_ffn * weight)
            activity = gate_value / (1.0 + jnp.exp(-gate_value)) * up_value
            moved = product(order_ref[...], activity.astype(out.dtype)).astype(out.dtype)
            for k in range(0, full, 512):
                piece = product(moved, down_ref[:, k : k + 512]).astype(terms.dtype)
                terms[group, :, :, k : k + 512] = piece.reshape(peers, half, 512)

        for g, pair in enumerate(pairs):
            for z_ in pair:
                third(z_)
            for z_ in pair:
                for y_ in (y, 1 - y):
                    for x_ in (x, 1 - x):
                        land(z_, y_, 1 - core, x_, None)
            if g == 0:
                own.wait()
                for copy in weights:
                    copy.wait()
            expert(pair[0] // 2)
        for copy in sends:
            copy.wait_send()

    return pl.pallas_call(
        kernel,
        out_shape=jax.ShapeDtypeStruct((2, peers, half, full), block.dtype),
        in_specs=in_vmem(1) + [pl.BlockSpec(memory_space=pl.ANY)] * 3 + in_vmem(2),
        out_specs=in_vmem(1)[0],
        scratch_shapes=[
            pltpu.VMEM((rows * peers, 2 * width), block.dtype),
            pltpu.VMEM((units, full), block.dtype),
            pltpu.VMEM((units, full), block.dtype),
            pltpu.VMEM((units, full), block.dtype),
            pltpu.SemaphoreType.DMA((64,)),
            pltpu.SemaphoreType.DMA((4 * peers,)),
            pltpu.SemaphoreType.DMA,
            pltpu.SemaphoreType.DMA((3,)),
        ],
        compiler_params=pltpu.CompilerParams(
            collective_id=number, has_side_effects=True, vmem_limit_bytes=VMEM_LIMIT
        ),
        name="gather_experts",
    )(block, gate, up, down, order, select)


def scatter_sums(parts, back, peers, number):
    layers = parts.shape[3]
    half, full = parts.shape[4:]
    width = full // 2

    def kernel(
        src, back_src, out, back_out, got_core, kept, got_first, mid, got_second, last, got_z,
        sends, recvs, back_sends, back_recvs, own_sem,
    ):
        tok, x = lax.axis_index("tok"), lax.axis_index("head")
        z, y, core = tok // 4, (tok // 2) % 2, tok % 2

        def place(z_, y_, core_):
            return z_ * 4 + y_ * 2 + core_

        across_x = (tok, 1 - x)
        across_y = (place(z, 1 - y, core), x)
        sibling = (place(z, y, 1 - core), x)
        along_z = [(place(lax.rem(z + d, layers), y, core), x) for d in range(1, layers)]
        others = [lax.rem(tok + d, peers) for d in range(1, peers)]
        meet([across_x] + [(there, x) for there in others])

        def copy_to(target, source, dest, index):
            copy = pltpu.make_async_remote_copy(
                src_ref=source,
                dst_ref=dest,
                send_sem=sends.at[index],
                recv_sem=recvs.at[index],
                device_id=target,
                device_id_type=MESH_ID,
            )
            copy.start()
            return copy

        def columns(x_):
            return pl.ds(pl.multiple_of(x_ * width, 128), width)

        def total(first, second):
            return first.astype(jnp.float32) + second.astype(jnp.float32)

        cores = [[None, None], [None, None]]
        for g in range(2):
            for h in range(2):
                y_ = (1 - y) if g == 0 else y
                cores[h][g] = copy_to(
                    sibling, src.at[h, 1 - core, y_], got_core.at[h, y_], 2 * h + g
                )

        backs = []
        for i, there in enumerate(others):
            copy = pltpu.make_async_remote_copy(
                src_ref=back_src.at[there],
                dst_ref=back_out.at[tok],
                send_sem=back_sends.at[i],
                recv_sem=back_recvs.at[tok],
                device_id=(there, x),
                device_id_type=MESH_ID,
            )
            copy.start()
            backs.append(copy)
        own = pltpu.make_async_copy(back_src.at[tok], back_out.at[tok], own_sem)
        own.start()

        def fold_core(h, y_):
            @pl.loop(0, layers)
            def _(z_):
                kept[h, y_, z_] = total(src[h, core, y_, z_], got_core[h, y_, z_]).astype(
                    kept.dtype
                )

        cores[1][0].wait_recv()
        fold_core(1, 1 - y)
        first_y = copy_to(across_y, kept.at[1, 1 - y], got_first.at[1], 4)
        cores[0][0].wait_recv()
        fold_core(0, 1 - y)
        first_x = [
            copy_to(
                across_x,
                kept.at[0, 1 - y, slice(None), slice(None), columns(1 - x)],
                got_first.at[0, slice(None), slice(None), pl.ds(0, width)],
                5,
            )
        ]
        cores[0][1].wait_recv()
        fold_core(0, y)
        first_x.append(
            copy_to(
                across_x,
                kept.at[0, y, slice(None), slice(None), columns(1 - x)],
                got_first.at[0, slice(None), slice(None), pl.ds(width, width)],
                6,
            )
        )
        cores[1][1].wait_recv()
        fold_core(1, y)

        first_x[0].wait_recv()

        @pl.loop(0, layers)
        def _(z_):
            mid[0, z_] = total(
                kept[0, 1 - y, z_, :, columns(x)], got_first[0, z_, :, :width]
            ).astype(mid.dtype)

        second_y = copy_to(across_y, mid.at[0], got_second.at[0], 7)

        first_y.wait_recv()

        @pl.loop(0, layers)
        def _(z_):
            mid[1, z_] = total(
                kept[1, y, z_, :, columns(1 - x)], got_first[1, z_, :, columns(1 - x)]
            ).astype(mid.dtype)

        second_x = copy_to(across_x, mid.at[1], got_second.at[1], 8)
        first_x[1].wait_recv()

        zs = []

        def send_z(h):
            for d in range(1, layers):
                z_ = lax.rem(z + d, layers)
                zs.append(
                    copy_to(
                        along_z[d - 1], last.at[h, z_], got_z.at[h, d - 1], 9 + h * layers + d - 1
                    )
                )

        second_y.wait_recv()

        @pl.loop(0, layers)
        def _(z_):
            last[0, z_] = (
                total(kept[0, y, z_, :, columns(x)], got_first[0, z_, :, width:])
                + got_second[0, z_].astype(jnp.float32)
            ).astype(last.dtype)

        send_z(0)
        second_x.wait_recv()

        @pl.loop(0, layers)
        def _(z_):
            last[1, z_] = (
                total(kept[1, y, z_, :, columns(x)], got_first[1, z_, :, columns(x)])
                + got_second[1, z_].astype(jnp.float32)
            ).astype(last.dtype)

        send_z(1)
        for copy in zs:
            copy.wait_recv()
        for h in range(2):
            acc = last[h, z].astype(jnp.float32)
            for d in range(1, layers):
                acc = acc + got_z[h, d - 1].astype(jnp.float32)
            out[h] = acc.astype(out.dtype)
        for there in others:
            spot = back_out.at[there]
            pltpu.make_async_remote_copy(
                src_ref=spot,
                dst_ref=spot,
                send_sem=back_sends.at[0],
                recv_sem=back_recvs.at[there],
                device_id=sibling,
                device_id_type=MESH_ID,
            ).wait_recv()
        for copy in backs:
            copy.wait_send()
        own.wait()
        for copy in cores[0] + cores[1] + first_x + [first_y, second_y, second_x] + zs:
            copy.wait_send()

    kind = parts.dtype
    return pl.pallas_call(
        kernel,
        out_shape=[
            jax.ShapeDtypeStruct((2, half, width), kind),
            jax.ShapeDtypeStruct(back.shape, back.dtype),
        ],
        in_specs=in_vmem(2),
        out_specs=in_vmem(2),
        scratch_shapes=[
            pltpu.VMEM((2, 2, layers, half, full), kind),
            pltpu.VMEM((2, 2, layers, half, full), kind),
            pltpu.VMEM((2, layers, half, full), kind),
            pltpu.VMEM((2, layers, half, width), kind),
            pltpu.VMEM((2, layers, half, width), kind),
            pltpu.VMEM((2, layers, half, width), kind),
            pltpu.VMEM((2, layers - 1, half, width), kind),
            pltpu.SemaphoreType.DMA((9 + 2 * layers,)),
            pltpu.SemaphoreType.DMA((9 + 2 * layers,)),
            pltpu.SemaphoreType.DMA((peers,)),
            pltpu.SemaphoreType.DMA((peers,)),
            pltpu.SemaphoreType.DMA,
        ],
        compiler_params=pltpu.CompilerParams(
            collective_id=number, has_side_effects=True, vmem_limit_bytes=VMEM_LIMIT
        ),
        name="scatter_sums",
    )(parts, back)


def ragged_attend(queries, cache, ids, bounds, base, factor):
    slots, heads, width = queries.shape
    blocks = cache.shape[1] // KEY_BLOCK
    cuts = list(zip(KEY_CUTS[:-1], KEY_CUTS[1:]))

    def kernel(ids_ref, bounds_ref, base_ref, q_ref, kv_ref, num_ref, den_ref):
        j = pl.program_id(0)

        @pl.when(j == 0)
        def _():
            num_ref[...] = jnp.zeros_like(num_ref)
            den_ref[...] = jnp.zeros_like(den_ref)

        found = []
        for i, (low, high) in enumerate(cuts):
            size = high - low
            kv = kv_ref[:, low:high]
            who = [ids_ref[(j * len(cuts) + i) * WINDOW + w] for w in range(WINDOW)]
            some = jnp.concatenate([q_ref[r] for r in who], axis=0)
            scores = factor * jnp.dot(some, kv, preferred_element_type=jnp.float32)
            places = (
                base_ref[0]
                + j * KEY_BLOCK
                + low
                + lax.broadcasted_iota(jnp.int32, (heads, size), 1)
            )
            lifted = jnp.exp(scores)
            weights = jnp.concatenate(
                [
                    jnp.where(
                        (places >= bounds_ref[r]) & (places < bounds_ref[slots + r]),
                        lifted[w * heads : (w + 1) * heads],
                        0.0,
                    )
                    for w, r in enumerate(who)
                ],
                axis=0,
            ).astype(jnp.bfloat16)
            num = lax.dot_general(
                weights,
                kv[:LATENT],
                (((1,), (1,)), ((), ())),
                preferred_element_type=jnp.float32,
            )
            wide = weights.astype(jnp.float32)
            den = sum(wide[:, k : k + 128] for k in range(0, size, 128))
            found.append((who, num, den))
        for who, num, den in found:
            for w, r in enumerate(who):
                rows = slice(w * heads, (w + 1) * heads)
                num_ref[r] += num[rows]
                den_ref[r] += den[rows]

    return pl.pallas_call(
        kernel,
        out_shape=[
            jax.ShapeDtypeStruct((slots, heads, LATENT), jnp.float32),
            jax.ShapeDtypeStruct((slots, heads, 128), jnp.float32),
        ],
        grid_spec=pltpu.PrefetchScalarGridSpec(
            num_scalar_prefetch=3,
            grid=(blocks,),
            in_specs=[
                pl.BlockSpec((slots, heads, width), lambda j, *_: (0, 0, 0)),
                pl.BlockSpec((width, KEY_BLOCK), lambda j, *_: (0, j)),
            ],
            out_specs=[
                pl.BlockSpec((slots, heads, LATENT), lambda j, *_: (0, 0, 0)),
                pl.BlockSpec((slots, heads, 128), lambda j, *_: (0, 0, 0)),
            ],
        ),
        compiler_params=pltpu.CompilerParams(vmem_limit_bytes=VMEM_LIMIT),
        name="ragged_attend",
    )(ids, bounds, base, queries, cache)


def pick_rows(chosen, values):
    return jnp.dot(
        chosen.astype(jnp.bfloat16), values, preferred_element_type=jnp.float32
    ).astype(values.dtype)


def direct_body(
    hidden,
    attn_gain,
    w_query,
    w_latent,
    w_key_up,
    w_value_up,
    w_out,
    latent_cache,
    cache_lengths,
    request_slot,
    ffn_gain,
    w_router,
    routes,
    expert_gate,
    expert_up,
    expert_down,
):
    f32, bf16 = jnp.float32, jnp.bfloat16
    rows, part = hidden.shape
    peers = lax.axis_size("tok")
    each = rows // peers
    local_heads = w_key_up.shape[0]
    expert_count = w_router.shape[1]
    head = lax.axis_index("head")
    tok = lax.axis_index("tok")
    ids = jnp.arange(rows, dtype=jnp.int32)

    owner = request_slot // rows
    earlier = (owner[None, :] == owner[:, None]) & (ids[None, :] < ids[:, None])
    send_place = owner * each + jnp.sum(earlier.astype(jnp.int32), axis=1)
    placed = ids[:, None] == send_place[None, :]
    route_mask = jnp.max(
        (routes[:, :, None] == jnp.arange(expert_count, dtype=jnp.int32)).astype(jnp.int32), axis=1
    )
    meta = jnp.concatenate(
        [
            (request_slot % rows)[:, None],
            (cache_lengths // 64)[:, None],
            (cache_lengths % 64)[:, None],
            route_mask,
        ],
        axis=1,
    ).astype(bf16)
    meta = jnp.pad(meta, ((0, 0), (0, 128 // each - meta.shape[1])))
    sent_meta = jnp.dot(placed.astype(bf16), meta, preferred_element_type=f32)
    blocks = pick_rows(placed, hidden).reshape(peers, each * part // 128, 128)
    wide, meta = to_owners(
        blocks, sent_meta.astype(jnp.int32).reshape(peers, 1, 128), 0
    )
    wide = wide.reshape(2, rows, part)
    meta = meta.reshape(rows, 128 // each)[:, : 3 + expert_count]
    slot, lengths = meta[:, 0], meta[:, 1] * 64 + meta[:, 2]
    mask = meta[:, 3:]
    starts = jnp.sum(jnp.where(slot[None, :] < slot[:, None], lengths[None, :], 0), axis=1)
    full = jnp.concatenate([wide[0], wide[1]], axis=1).astype(f32)
    mine = lax.dynamic_index_in_dim(wide, head, 0, keepdims=False)

    inv_attn = lax.rsqrt(jnp.mean(full * full, axis=1, keepdims=True) + NORM_EPS)
    normed = (full * inv_attn * attn_gain).astype(bf16)
    normed_part = lax.dynamic_slice_in_dim(normed, head * part, part, 1)
    compressed = jnp.dot(normed_part, w_latent, preferred_element_type=f32)
    queries = jnp.dot(normed, w_query, preferred_element_type=f32).astype(bf16)
    queries = queries.reshape(rows, local_heads, NOPE + ROPE)
    absorbed = jnp.einsum(
        "bhn,hnl->bhl", queries[:, :, :NOPE], w_key_up, preferred_element_type=f32
    ).astype(bf16)
    turned = rotate_pairs(queries[:, :, NOPE:].astype(f32), lengths).astype(bf16)
    probes = jnp.concatenate([absorbed, turned], axis=2)
    far_probes, far_compressed = swap_pair([probes, compressed], 1)
    compressed = compressed + far_compressed
    latent_new = compressed[:, :LATENT]
    latent_new = latent_new * lax.rsqrt(
        jnp.mean(latent_new * latent_new, axis=1, keepdims=True) + NORM_EPS
    )
    new_entry = jnp.concatenate(
        [latent_new, rotate_pairs(compressed[:, LATENT:], lengths)], axis=1
    ).astype(bf16)
    factor = (NOPE + ROPE) ** (-0.5)
    self_score = factor * jnp.einsum(
        "bhc,bc->bh", probes, new_entry, preferred_element_type=f32
    )
    self_weight = jnp.exp(self_score).astype(bf16).astype(f32)

    key_rows = latent_cache.shape[0]
    block_starts = (
        head * key_rows
        + jnp.arange(0, key_rows, KEY_BLOCK, dtype=jnp.int32)[:, None]
        + jnp.array(KEY_CUTS[:-1], jnp.int32)
    ).reshape(-1)
    ends = starts + lengths
    first = jnp.sum((ends[None, :] <= block_starts[:, None]).astype(jnp.int32), axis=1)
    first = jnp.minimum(first, rows - WINDOW)
    window = first[:, None] + jnp.arange(WINDOW, dtype=jnp.int32)
    window_ids = jnp.sum(
        jnp.where(window[:, :, None] == slot[None, None, :], ids[None, None, :], 0), axis=2
    )
    numerator, denominator = ragged_attend(
        jnp.concatenate([probes, far_probes], axis=1),
        latent_cache.T,
        window_ids.reshape(-1).astype(jnp.int32),
        jnp.concatenate([starts, ends]).astype(jnp.int32),
        (head * key_rows).reshape(1).astype(jnp.int32),
        factor,
    )
    denominator = jnp.sum(denominator, axis=2)
    far_num, far_den = swap_pair(
        [
            numerator[:, local_heads:].astype(bf16).reshape(rows * local_heads, LATENT),
            denominator[:, local_heads:].reshape(rows * local_heads // 128, 128),
        ],
        2,
    )
    total_num = (
        numerator[:, :local_heads]
        + far_num.reshape(rows, local_heads, LATENT).astype(f32)
        + self_weight[:, :, None] * new_entry[:, None, :LATENT].astype(f32)
    )
    total_den = denominator[:, :local_heads] + far_den.reshape(rows, local_heads) + self_weight
    mixed = (total_num / total_den[:, :, None]).astype(bf16)
    head_out = jnp.einsum("bhl,hld->bhd", mixed, w_value_up, preferred_element_type=f32)
    head_out = head_out.astype(bf16).reshape(rows, local_heads * NOPE)
    piece = jnp.dot(head_out, w_out, preferred_element_type=f32)
    kept = lax.dynamic_slice_in_dim(piece, head * part, part, 1)
    given = lax.dynamic_slice_in_dim(piece, (1 - head) * part, part, 1)
    (far_piece,) = swap_pair([given], 3)
    attended = (mine.astype(f32) + (kept + far_piece)).astype(bf16)

    attended_wide = attended.astype(f32)
    gained = (attended_wide * ffn_gain).astype(bf16)
    squares = jnp.sum(attended_wide * attended_wide, axis=1, keepdims=True)
    logit_part = jnp.dot(gained, w_router, preferred_element_type=f32)
    notes = jnp.concatenate([squares, logit_part], axis=1)
    high = notes.astype(bf16)
    low = (notes - high.astype(f32)).astype(bf16)
    notes = jnp.concatenate([high, low, mask.astype(bf16)], axis=1)
    notes = jnp.pad(notes, ((0, 0), (0, 128 - notes.shape[1])))
    half = rows // 2
    layers = peers // 4
    every = jnp.arange(half * peers, dtype=jnp.int32)
    c_, y_, z_ = (
        every // (half * peers // 2),
        every // (half * layers) % 2,
        every // half % layers,
    )
    inner = every % half
    source = inner // each * rows + (z_ * 4 + y_ * 2 + c_) * each + inner % each
    order = (source[:, None] == every[None, :]).astype(bf16)
    count = 1 + expert_count
    line = jnp.arange(128, dtype=jnp.int32)[:, None]
    lane = jnp.arange(128, dtype=jnp.int32)[None, :]
    held = lane < expert_count
    select = jnp.concatenate(
        [
            held & ((line == 1 + lane) | (line == count + 1 + lane)),
            held & (line == 2 * count + lane),
            ((line == 0) | (line == count)) & (lane >= 0),
        ],
        axis=1,
    ).astype(bf16)
    terms = gather_experts(
        jnp.concatenate([gained, notes], axis=1),
        expert_gate[0].T,
        expert_up[0].T,
        expert_down[0],
        order,
        select,
        peers,
        4,
    ).reshape(2, 2, 2, layers, half, 2 * part)
    back = jnp.concatenate([attended, new_entry], axis=1)
    back = jnp.pad(back, ((0, 0), (0, 2 * part - back.shape[1])))
    summed, back = scatter_sums(terms, back.reshape(peers, each * 2 * part // 128, 128), peers, 5)
    mixed_back = jnp.concatenate([back.reshape(rows, 2 * part), summed.reshape(rows, part)], axis=1)
    final = pick_rows(placed.T, mixed_back)
    return (
        final[:, part : part + LATENT + ROPE],
        final[:, :part],
        final[:, 2 * part :],
    )


def solution(mesh):
    in_specs = (
        P("tok", "head"),
        P(),
        P(None, "head"),
        P("head", None),
        P("head", None, None),
        P("head", None, None),
        P("head", None),
        P(("tok", "head"), None),
        P("tok"),
        P("tok"),
        P("head"),
        P("head", None),
        P("tok", None),
        P("tok", None, "head"),
        P("tok", None, "head"),
        P("tok", "head", None),
    )
    out_specs = (P("tok", None), P("tok", "head"), P("tok", "head"))
    chosen = direct_body if (mesh.shape["tok"], mesh.shape["head"]) == (16, 2) else body
    return jax.shard_map(chosen, mesh=mesh, in_specs=in_specs, out_specs=out_specs, check_vma=False)
```

```python
import jax
import jax.numpy as jnp
from jax import lax
from jax.experimental import pallas as pl
from jax.experimental.pallas import tpu as pltpu
from jax.sharding import PartitionSpec as P

D = 2048
NOPE = 128
ROPE = 64
LATENT = 512


NORM_EPS = 1e-06


def rotate_pairs(values, places):
    halfway = values.shape[-1] // 2
    freqs = 10000.0 ** (-jnp.arange(halfway, dtype=jnp.float32) / halfway)
    angles = places.astype(jnp.float32).reshape(places.shape + (1,) * (values.ndim - 1)) * freqs
    cosine = jnp.cos(angles)
    sine = jnp.sin(angles)
    first_half = values[..., :halfway]
    second_half = values[..., halfway:]
    return jnp.concatenate(
        [first_half * cosine - second_half * sine, first_half * sine + second_half * cosine],
        axis=-1,
    )


def owner_attend(all_heads, owner_lengths, latent_cache, head_index, factor):
    slot_rows = all_heads.shape[0]
    total_heads = all_heads.shape[1]
    probe_width = all_heads.shape[2]
    key_rows = latent_cache.shape[0]
    starts = jnp.cumsum(owner_lengths) - owner_lengths
    places = head_index * key_rows + jnp.arange(key_rows, dtype=jnp.int32)
    inside = (places[None, :] >= starts[:, None]) & (
        places[None, :] < (starts + owner_lengths)[:, None]
    )
    scores = factor * jnp.einsum(
        "qc,pc->qp",
        all_heads.reshape(slot_rows * total_heads, probe_width),
        latent_cache,
        preferred_element_type=jnp.float32,
    )
    scores = scores.reshape(slot_rows, total_heads, key_rows)
    weights = jnp.where(inside[:, None, :], jnp.exp(scores), 0.0).astype(jnp.bfloat16)
    numerator = jnp.einsum(
        "khp,pl->khl", weights, latent_cache[:, :LATENT], preferred_element_type=jnp.float32
    )
    denominator = jnp.sum(weights.astype(jnp.float32), axis=2)
    return (numerator, denominator)


def body(
    hidden,
    attn_gain,
    w_query,
    w_latent,
    w_key_up,
    w_value_up,
    w_out,
    latent_cache,
    cache_lengths,
    request_slot,
    ffn_gain,
    w_router,
    routes,
    expert_gate,
    expert_up,
    expert_down,
):
    local_rows = hidden.shape[0]
    quarter_width = hidden.shape[1]
    local_heads = w_key_up.shape[0]
    peer_count = lax.axis_size("tok")
    head_index = lax.axis_index("head")
    tok_index = lax.axis_index("tok")
    row_ids = jnp.arange(local_rows, dtype=jnp.int32)
    gathered = lax.all_gather(hidden, "head", axis=1, tiled=True)
    widened = gathered.astype(jnp.float32)
    inv_attn = lax.rsqrt(jnp.mean(widened * widened, axis=1, keepdims=True) + NORM_EPS)
    normed_attn = (widened * inv_attn * attn_gain).astype(jnp.bfloat16)
    normed_part = lax.dynamic_slice_in_dim(
        normed_attn, head_index * quarter_width, quarter_width, 1
    )
    compressed = lax.psum(
        jnp.dot(normed_part, w_latent, preferred_element_type=jnp.float32), "head"
    )
    latent_new = compressed[:, :LATENT]
    latent_new = latent_new * lax.rsqrt(
        jnp.mean(latent_new * latent_new, axis=1, keepdims=True) + NORM_EPS
    )
    new_entry = jnp.concatenate(
        [latent_new, rotate_pairs(compressed[:, LATENT:], cache_lengths)], axis=1
    ).astype(jnp.bfloat16)
    queries = jnp.dot(normed_attn, w_query, preferred_element_type=jnp.float32).astype(jnp.bfloat16)
    queries = queries.reshape(local_rows, local_heads, NOPE + ROPE)
    absorbed = jnp.einsum(
        "bhn,hnl->bhl", queries[:, :, :NOPE], w_key_up, preferred_element_type=jnp.float32
    ).astype(jnp.bfloat16)
    turned = rotate_pairs(queries[:, :, NOPE:].astype(jnp.float32), cache_lengths).astype(
        jnp.bfloat16
    )
    probes = jnp.concatenate([absorbed, turned], axis=2)
    factor = (NOPE + ROPE) ** (-0.5)
    self_score = factor * jnp.einsum(
        "bhc,bc->bh", probes, new_entry, preferred_element_type=jnp.float32
    )
    self_weight = jnp.exp(self_score).astype(jnp.bfloat16).astype(jnp.float32)
    per_owner = max(1, local_rows // peer_count)
    buffer_rows = peer_count * per_owner
    buffer_ids = jnp.arange(buffer_rows, dtype=jnp.int32)
    dest_owner = request_slot // local_rows
    earlier_same = (dest_owner[None, :] == dest_owner[:, None]) & (
        row_ids[None, :] < row_ids[:, None]
    )
    send_place = dest_owner * per_owner + jnp.sum(earlier_same.astype(jnp.int32), axis=1)
    all_probes, all_slots, all_lengths = (
        lax.all_gather(probes, "tok", axis=0, tiled=True),
        lax.all_gather(request_slot, "tok", axis=0, tiled=True),
        lax.all_gather(cache_lengths, "tok", axis=0, tiled=True),
    )
    total_rows = all_slots.shape[0]
    slot_hit = all_slots[None, :] == (tok_index * local_rows + row_ids)[:, None]
    request_at = jnp.sum(
        jnp.where(slot_hit, jnp.arange(total_rows, dtype=jnp.int32)[None, :], 0), axis=1
    )
    owner_probes = all_probes[request_at]
    owner_lengths = all_lengths[request_at]
    owned_here = (
        (all_slots // local_rows == tok_index).astype(jnp.int32).reshape(peer_count, local_rows)
    )
    prior_count = (jnp.cumsum(owned_here, axis=1) - owned_here).reshape(total_rows)
    back_index = request_at // local_rows * per_owner + prior_count[request_at]
    all_heads = lax.all_gather(owner_probes, "head", axis=1, tiled=True)
    numerator, denominator = owner_attend(
        all_heads, owner_lengths, latent_cache, head_index, factor
    )
    group_num, group_den = (
        lax.psum_scatter(numerator, "head", scatter_dimension=1, tiled=True),
        lax.psum_scatter(denominator, "head", scatter_dimension=1, tiled=True),
    )
    at_place = buffer_ids[:, None] == back_index[None, :]
    slot_of_place = jnp.sum(jnp.where(at_place, row_ids[None, :], 0), axis=1) + local_rows * (
        1 - jnp.max(at_place.astype(jnp.int32), axis=1)
    )
    padded_num = jnp.concatenate(
        [group_num, jnp.zeros((1, local_heads, LATENT), jnp.float32)], axis=0
    )
    padded_den = jnp.concatenate([group_den, jnp.zeros((1, local_heads), jnp.float32)], axis=0)
    got_num, got_den = (
        lax.all_to_all(
            padded_num[slot_of_place].reshape(peer_count, per_owner, local_heads, LATENT),
            "tok",
            split_axis=0,
            concat_axis=0,
            tiled=True,
        ),
        lax.all_to_all(
            padded_den[slot_of_place].reshape(peer_count, per_owner, local_heads),
            "tok",
            split_axis=0,
            concat_axis=0,
            tiled=True,
        ),
    )
    back_num = got_num.reshape(buffer_rows, local_heads, LATENT)
    back_den = got_den.reshape(buffer_rows, local_heads)
    total_num = back_num[send_place] + self_weight[:, :, None] * new_entry[:, None, :LATENT].astype(
        jnp.float32
    )
    total_den = back_den[send_place] + self_weight
    mixed_latent = (total_num / total_den[:, :, None]).astype(jnp.bfloat16)
    head_out = jnp.einsum(
        "bhl,hld->bhd", mixed_latent, w_value_up, preferred_element_type=jnp.float32
    ).astype(jnp.bfloat16)
    head_out = head_out.reshape(local_rows, local_heads * NOPE)
    attn_piece = lax.psum_scatter(
        jnp.dot(head_out, w_out, preferred_element_type=jnp.float32),
        "head",
        scatter_dimension=1,
        tiled=True,
    )
    attended = (hidden.astype(jnp.float32) + attn_piece).astype(jnp.bfloat16)
    attended_wide = attended.astype(jnp.float32)
    gained = (attended_wide * ffn_gain).astype(jnp.bfloat16)
    squares, logit_part = lax.psum(
        (
            jnp.sum(attended_wide * attended_wide, axis=1),
            jnp.dot(gained, w_router, preferred_element_type=jnp.float32),
        ),
        "head",
    )
    inv_ffn = lax.rsqrt(squares / D + NORM_EPS)
    logits = logit_part * inv_ffn[:, None]
    normed_ffn = (attended_wide * ffn_gain * inv_ffn[:, None]).astype(jnp.bfloat16)
    expert_count = w_router.shape[1]
    route_count = routes.shape[1]
    expert_ids = jnp.arange(expert_count, dtype=jnp.int32)
    named = routes[:, :, None] == expert_ids[None, None, :]
    picked = jnp.sum(jnp.where(named, logits[:, None, :], 0.0), axis=2)
    lifted = jnp.exp(picked)
    route_weight = lifted / jnp.sum(lifted, axis=1, keepdims=True)
    struck = jnp.max(named.astype(jnp.int32), axis=1)
    earlier_hits = jnp.cumsum(struck, axis=0) - struck
    capacity = min(local_rows, max(2, 2 * local_rows * route_count // expert_count))
    route_place = routes * capacity + jnp.take_along_axis(earlier_hits, routes, axis=1)
    slot_total = expert_count * capacity
    slot_ids = jnp.arange(slot_total, dtype=jnp.int32)
    filled = route_place[None, :, :] == slot_ids[:, None, None]
    source_token = jnp.sum(
        jnp.where(filled, row_ids[None, :, None], 0), axis=(1, 2)
    ) + local_rows * (1 - jnp.max(filled.astype(jnp.int32), axis=(1, 2)))
    full_rows = lax.all_gather(normed_ffn, "head", axis=1, tiled=True)
    padded_rows = jnp.concatenate(
        [full_rows, jnp.zeros((1, full_rows.shape[1]), jnp.bfloat16)], axis=0
    )
    arrived = lax.all_to_all(
        padded_rows[source_token].reshape(expert_count, capacity, full_rows.shape[1]),
        "tok",
        split_axis=0,
        concat_axis=0,
        tiled=True,
    )
    expert_in = arrived.reshape(peer_count * capacity, full_rows.shape[1])
    gate_value = jnp.dot(expert_in, expert_gate[0], preferred_element_type=jnp.float32)
    up_value = jnp.dot(expert_in, expert_up[0], preferred_element_type=jnp.float32)
    activity = (jax.nn.silu(gate_value) * up_value).astype(jnp.bfloat16)
    expert_share = lax.psum_scatter(
        jnp.dot(activity, expert_down[0], preferred_element_type=jnp.float32).astype(jnp.bfloat16),
        "head",
        scatter_dimension=1,
        tiled=True,
    )
    returned = lax.all_to_all(
        expert_share.reshape(peer_count, capacity, quarter_width),
        "tok",
        split_axis=0,
        concat_axis=0,
        tiled=True,
    )
    chosen_rows = returned.reshape(slot_total, quarter_width)[route_place]
    expert_mix = jnp.sum(route_weight[:, :, None] * chosen_rows.astype(jnp.float32), axis=1).astype(
        jnp.bfloat16
    )
    return (new_entry, attended, expert_mix)


MESH_ID = pl.DeviceIdType.MESH
KEY_BLOCK = 1664
KEY_CUTS = (0, 384, 768, 1152, 1536, 1664)
WINDOW = 4
VMEM_LIMIT = 48 * 1024 * 1024


def meet(partners):
    barrier = pltpu.get_barrier_semaphore()
    for partner in partners:
        pl.semaphore_signal(barrier, inc=1, device_id=partner, device_id_type=MESH_ID)
    pl.semaphore_wait(barrier, len(partners))


def in_vmem(count):
    return [pl.BlockSpec(memory_space=pltpu.VMEM)] * count


def swap_pair(arrays, number):
    count = len(arrays)

    def kernel(*refs):
        ins, outs = refs[:count], refs[count : 2 * count]
        send_sem, recv_sem = refs[2 * count :]
        partner = (lax.axis_index("tok"), 1 - lax.axis_index("head"))
        meet([partner])
        copies = []
        for i in range(count):
            copy = pltpu.make_async_remote_copy(
                src_ref=ins[i],
                dst_ref=outs[i],
                send_sem=send_sem.at[i],
                recv_sem=recv_sem.at[i],
                device_id=partner,
                device_id_type=MESH_ID,
            )
            copy.start()
            copies.append(copy)
        for copy in copies:
            copy.wait()

    return pl.pallas_call(
        kernel,
        out_shape=[jax.ShapeDtypeStruct(a.shape, a.dtype) for a in arrays],
        in_specs=in_vmem(count),
        out_specs=in_vmem(count),
        scratch_shapes=[pltpu.SemaphoreType.DMA((count,)), pltpu.SemaphoreType.DMA((count,))],
        compiler_params=pltpu.CompilerParams(
            collective_id=number, has_side_effects=True, vmem_limit_bytes=VMEM_LIMIT
        ),
        name=f"swap_pair_{number}",
    )(*arrays)


def to_owners(blocks, notes, number):
    peers = blocks.shape[0]

    def kernel(src, src_notes, out, out_notes, send_sem, recv_sem, pass_sem, note_sem, own_sem):
        tok, head = lax.axis_index("tok"), lax.axis_index("head")
        partner = (tok, 1 - head)
        others = [lax.rem(tok + d, peers) for d in range(1, peers)]
        meet([partner] + [(there, head) for there in others])

        def remote(source, dest, first, second, target):
            return pltpu.make_async_remote_copy(
                src_ref=source,
                dst_ref=dest,
                send_sem=first,
                recv_sem=second,
                device_id=target,
                device_id_type=MESH_ID,
            )

        sends = []
        for i, there in enumerate(others):
            sends.append(
                remote(
                    src.at[there],
                    out.at[head, tok],
                    send_sem.at[i],
                    recv_sem.at[head, tok],
                    (there, head),
                )
            )
            sends[-1].start()
        sends.append(
            remote(
                src.at[tok], out.at[head, tok], pass_sem.at[0], recv_sem.at[head, tok], partner
            )
        )
        sends[-1].start()
        for i, there in enumerate(others):
            sends.append(
                remote(
                    src_notes.at[there],
                    out_notes.at[tok],
                    send_sem.at[peers + i],
                    note_sem.at[tok],
                    (there, head),
                )
            )
            sends[-1].start()
        own = [
            pltpu.make_async_copy(src.at[tok], out.at[head, tok], own_sem.at[0]),
            pltpu.make_async_copy(src_notes.at[tok], out_notes.at[tok], own_sem.at[1]),
        ]
        for copy in own:
            copy.start()
        for i, there in enumerate(others):
            spot = out.at[head, there]
            remote(spot, spot, send_sem.at[0], recv_sem.at[head, there], partner).wait_recv()
            sends.append(
                remote(spot, spot, pass_sem.at[1 + i], recv_sem.at[head, there], partner)
            )
            sends[-1].start()
        for there in [tok] + others:
            spot = out.at[1 - head, there]
            remote(spot, spot, send_sem.at[0], recv_sem.at[1 - head, there], partner).wait_recv()
        for there in others:
            spot = out_notes.at[there]
            remote(spot, spot, send_sem.at[0], note_sem.at[there], partner).wait_recv()
        for copy in sends:
            copy.wait_send()
        for copy in own:
            copy.wait()

    return pl.pallas_call(
        kernel,
        out_shape=[
            jax.ShapeDtypeStruct((2,) + blocks.shape, blocks.dtype),
            jax.ShapeDtypeStruct(notes.shape, notes.dtype),
        ],
        in_specs=in_vmem(2),
        out_specs=in_vmem(2),
        scratch_shapes=[
            pltpu.SemaphoreType.DMA((2 * peers,)),
            pltpu.SemaphoreType.DMA((2, peers)),
            pltpu.SemaphoreType.DMA((peers,)),
            pltpu.SemaphoreType.DMA((peers,)),
            pltpu.SemaphoreType.DMA((2,)),
        ],
        compiler_params=pltpu.CompilerParams(
            collective_id=number, has_side_effects=True, vmem_limit_bytes=VMEM_LIMIT
        ),
        name="to_owners",
    )(blocks, notes)


def route_and_sum(block, gate, up, down, order, select, back, peers, number):
    rows, width = block.shape
    half = rows // 2
    layers = peers // 4
    part = width - 128
    units, full = gate.shape
    some = rows * peers // 2

    def kernel(
        src, gate_any, up_any, down_any, order_ref, select_ref, back_src, result, back_out,
        out, gate_ref, up_ref, down_ref, terms, got_core, kept, got_first, mid, got_second,
        last, got_z, send_sem, recv_sem, own_sem, weight_sem, sum_sends, sum_recvs,
        back_sends, back_recvs,
    ):
        tok, x = lax.axis_index("tok"), lax.axis_index("head")
        z, y, core = tok // 4, (tok // 2) % 2, tok % 2

        def place(z_, y_, core_):
            return z_ * 4 + y_ * 2 + core_

        across_x = (tok, 1 - x)
        across_y = (place(z, 1 - y, core), x)
        sibling = (place(z, y, 1 - core), x)
        along_z = [(place(lax.rem(z + d, layers), y, core), x) for d in range(1, layers)]
        others = [lax.rem(tok + d, peers) for d in range(1, peers)]
        meet([across_x] + [(there, x) for there in others])

        def spot(z_, y_, core_, x_, h):
            start = place(z_, y_, core_) * rows + (h or 0) * half
            size = rows if h is None else half
            return out.at[
                pl.ds(pl.multiple_of(start, half), size),
                pl.ds(pl.multiple_of(x_ * width, 128), width),
            ]

        def slot(z_, y_, core_, x_, h):
            return (place(z_, y_, core_) * 2 + x_) * 2 + (h or 0)

        sends = []

        def push(target, z_, y_, core_, x_, h, fresh=False):
            dst = spot(z_, y_, core_, x_, h)
            copy = pltpu.make_async_remote_copy(
                src_ref=src if fresh else dst,
                dst_ref=dst,
                send_sem=send_sem.at[len(sends)],
                recv_sem=recv_sem.at[slot(z_, y_, core_, x_, h)],
                device_id=target,
                device_id_type=MESH_ID,
            )
            copy.start()
            sends.append(copy)

        def land(z_, y_, core_, x_, h):
            dst = spot(z_, y_, core_, x_, h)
            pltpu.make_async_remote_copy(
                src_ref=dst,
                dst_ref=dst,
                send_sem=send_sem.at[0],
                recv_sem=recv_sem.at[slot(z_, y_, core_, x_, h)],
                device_id=sibling,
                device_id_type=MESH_ID,
            ).wait_recv()

        turns = [1, 3, 2][: layers - 1]
        for d in turns:
            push(along_z[d - 1], z, y, core, x, None, True)
        for target in (across_x, across_y, sibling):
            push(target, z, y, core, x, None, True)
        own = pltpu.make_async_copy(src, spot(z, y, core, x, None), own_sem.at[0])
        own.start()
        weights = [
            pltpu.make_async_copy(a, b, weight_sem.at[i])
            for i, (a, b) in enumerate(
                [(gate_any, gate_ref), (up_any, up_ref), (down_any, down_ref)]
            )
        ]
        for copy in weights:
            copy.start()

        def second(z_):
            land(z_, 1 - y, core, x, None)
            push(across_x, z_, 1 - y, core, x, 0)
            land(z_, y, core, 1 - x, None)
            push(across_y, z_, y, core, 1 - x, 1)
            push(sibling, z_, 1 - y, core, x, None)
            push(sibling, z_, y, core, 1 - x, None)

        def third(z_):
            land(z_, 1 - y, core, 1 - x, 0)
            land(z_, 1 - y, core, 1 - x, 1)
            push(sibling, z_, 1 - y, core, 1 - x, None)

        for d in turns:
            z_ = lax.rem(z + d, layers)
            land(z_, y, core, x, None)
            for target in (across_x, across_y, sibling):
                push(target, z_, y, core, x, None)
            if d == turns[0]:
                second(z)
        near = z + 1 - 2 * (z % 2)
        pairs = [(z, near), (lax.rem(z + 2, layers), lax.rem(near + 2, layers))]
        second(near)
        for z_ in pairs[1]:
            second(z_)

        backs = []
        for i, there in enumerate(others):
            copy = pltpu.make_async_remote_copy(
                src_ref=back_src.at[there],
                dst_ref=back_out.at[tok],
                send_sem=back_sends.at[i],
                recv_sem=back_recvs.at[tok],
                device_id=(there, x),
                device_id_type=MESH_ID,
            )
            copy.start()
            backs.append(copy)
        own_back = pltpu.make_async_copy(back_src.at[tok], back_out.at[tok], own_sem.at[1])
        own_back.start()

        def across(a, b):
            return lax.dot_general(
                a, b, (((1,), (1,)), ((), ())), preferred_element_type=jnp.float32
            )

        def product(a, b):
            return jnp.dot(a, b, preferred_element_type=jnp.float32)

        def expert(a, group):
            at = pl.ds(pl.multiple_of(group * some, some), some)
            left, right = out[at, part:width], out[at, width + part :]
            logits = product(left, select_ref[:, :128]) + product(right, select_ref[:, :128])
            named = product(left, select_ref[:, 128:256])
            squares = product(left, select_ref[:, 256:]) + product(right, select_ref[:, 256:])
            inv_ffn = lax.rsqrt(squares / full + NORM_EPS)
            lifted = jnp.where(named > 0.5, jnp.exp(logits * inv_ffn), 0.0)
            lane = lax.broadcasted_iota(jnp.int32, (some, 128), 1)
            mine = jnp.sum(jnp.where(lane == tok, lifted, 0.0), axis=1, keepdims=True)
            weight = mine / jnp.sum(lifted, axis=1, keepdims=True)
            inv_ffn = inv_ffn[:, :1]
            first, last = out[at, :part], out[at, width : width + part]
            gate_value = across(first, gate_ref[:, :part]) + across(last, gate_ref[:, part:])
            gate_value = gate_value * inv_ffn
            up_value = across(first, up_ref[:, :part]) + across(last, up_ref[:, part:])
            up_value = up_value * (inv_ffn * weight)
            activity = gate_value / (1.0 + jnp.exp(-gate_value)) * up_value
            moved = product(order_ref[...], activity.astype(out.dtype)).astype(out.dtype)
            for k in range(0, full, 512):
                piece = product(moved, down_ref[:, k : k + 512]).astype(terms.dtype)
                terms[a, :, :, k : k + 512] = piece.reshape(peers, half, 512)

        def copy_to(target, source, dest, index, landing=None):
            copy = pltpu.make_async_remote_copy(
                src_ref=source,
                dst_ref=dest,
                send_sem=sum_sends.at[index],
                recv_sem=sum_recvs.at[index if landing is None else landing],
                device_id=target,
                device_id_type=MESH_ID,
            )
            copy.start()
            return copy

        def columns(x_):
            return pl.ds(pl.multiple_of(x_ * part, 128), part)

        def total(first, second):
            return first.astype(jnp.float32) + second.astype(jnp.float32)

        def hand_over(a):
            return [
                copy_to(
                    sibling,
                    terms.at[a, pl.ds(((1 - core) * 2 + y_) * layers, layers)],
                    got_core.at[a, y_],
                    2 * a + g,
                )
                for g, y_ in enumerate((1 - y, y))
            ]

        def fold_core(a, y_):
            @pl.loop(0, layers)
            def _(z_):
                kept[a, y_, z_] = total(
                    terms[a, (core * 2 + y_) * layers + z_], got_core[a, y_, z_]
                ).astype(kept.dtype)

        def bring(pair):
            for z_ in pair:
                third(z_)
            for z_ in pair:
                for y_ in (y, 1 - y):
                    for x_ in (x, 1 - x):
                        land(z_, y_, 1 - core, x_, None)

        bring(pairs[0])
        own.wait()
        for copy in weights:
            copy.wait()
        expert(0, z // 2)
        cores = [hand_over(0)]
        bring(pairs[1])
        first_x = []
        for g, y_ in enumerate((1 - y, y)):
            cores[0][g].wait_recv()
            fold_core(0, y_)
            first_x.append(
                copy_to(
                    across_x,
                    kept.at[0, y_, slice(None), slice(None), columns(1 - x)],
                    got_first.at[0, slice(None), slice(None), pl.ds(g * part, part)],
                    5 + g,
                )
            )
        expert(1, 1 - z // 2)
        cores.append(hand_over(1))
        cores[1][0].wait_recv()
        fold_core(1, 1 - y)
        first_y = copy_to(across_y, kept.at[1, 1 - y], got_first.at[1], 4)
        first_x[0].wait_recv()

        @pl.loop(0, layers)
        def _(z_):
            mid[0, z_] = total(
                kept[0, 1 - y, z_, :, columns(x)], got_first[0, z_, :, :part]
            ).astype(mid.dtype)

        second_y = copy_to(across_y, mid.at[0], got_second.at[0], 7)
        cores[1][1].wait_recv()
        fold_core(1, y)
        first_x[1].wait_recv()
        zs = []

        def send_z(a):
            group = (z // 2) if a == 0 else (1 - z // 2)
            for d in range(1, layers):
                z_ = lax.rem(z + d, layers)
                zs.append(
                    copy_to(
                        along_z[d - 1],
                        last.at[a, z_],
                        got_z.at[group, d - 1],
                        9 + a * layers + d - 1,
                        9 + group * layers + d - 1,
                    )
                )

        first_y.wait_recv()

        @pl.loop(0, layers)
        def _(z_):
            mid[1, z_] = total(
                kept[1, y, z_, :, columns(1 - x)], got_first[1, z_, :, columns(1 - x)]
            ).astype(mid.dtype)

        second_x = copy_to(across_x, mid.at[1], got_second.at[1], 8)
        second_y.wait_recv()

        @pl.loop(0, layers)
        def _(z_):
            last[0, z_] = (
                total(kept[0, y, z_, :, columns(x)], got_first[0, z_, :, part:])
                + got_second[0, z_].astype(jnp.float32)
            ).astype(last.dtype)

        send_z(0)
        second_x.wait_recv()

        @pl.loop(0, layers)
        def _(z_):
            last[1, z_] = (
                total(kept[1, y, z_, :, columns(x)], got_first[1, z_, :, columns(x)])
                + got_second[1, z_].astype(jnp.float32)
            ).astype(last.dtype)

        send_z(1)
        for copy in zs:
            copy.wait_recv()
        for a in range(2):
            group = (z // 2) if a == 0 else (1 - z // 2)
            acc = last[a, z].astype(jnp.float32)
            for d in range(1, layers):
                acc = acc + got_z[group, d - 1].astype(jnp.float32)
            result[group] = acc.astype(result.dtype)
        for there in others:
            spot_back = back_out.at[there]
            pltpu.make_async_remote_copy(
                src_ref=spot_back,
                dst_ref=spot_back,
                send_sem=back_sends.at[0],
                recv_sem=back_recvs.at[there],
                device_id=sibling,
                device_id_type=MESH_ID,
            ).wait_recv()
        own_back.wait()
        for copy in (
            sends + backs + cores[0] + cores[1] + first_x + [first_y, second_y, second_x] + zs
        ):
            copy.wait_send()

    kind = block.dtype
    return pl.pallas_call(
        kernel,
        out_shape=[
            jax.ShapeDtypeStruct((2, half, part), kind),
            jax.ShapeDtypeStruct(back.shape, kind),
        ],
        in_specs=in_vmem(1) + [pl.BlockSpec(memory_space=pl.ANY)] * 3 + in_vmem(3),
        out_specs=in_vmem(2),
        scratch_shapes=[
            pltpu.VMEM((rows * peers, 2 * width), block.dtype),
            pltpu.VMEM((units, full), block.dtype),
            pltpu.VMEM((units, full), block.dtype),
            pltpu.VMEM((units, full), block.dtype),
            pltpu.VMEM((2, peers, half, full), kind),
            pltpu.VMEM((2, 2, layers, half, full), kind),
            pltpu.VMEM((2, 2, layers, half, full), kind),
            pltpu.VMEM((2, layers, half, full), kind),
            pltpu.VMEM((2, layers, half, part), kind),
            pltpu.VMEM((2, layers, half, part), kind),
            pltpu.VMEM((2, layers, half, part), kind),
            pltpu.VMEM((2, layers - 1, half, part), kind),
            pltpu.SemaphoreType.DMA((64,)),
            pltpu.SemaphoreType.DMA((4 * peers,)),
            pltpu.SemaphoreType.DMA((2,)),
            pltpu.SemaphoreType.DMA((3,)),
            pltpu.SemaphoreType.DMA((9 + 2 * layers,)),
            pltpu.SemaphoreType.DMA((9 + 2 * layers,)),
            pltpu.SemaphoreType.DMA((peers,)),
            pltpu.SemaphoreType.DMA((peers,)),
        ],
        compiler_params=pltpu.CompilerParams(
            collective_id=number, has_side_effects=True, vmem_limit_bytes=VMEM_LIMIT
        ),
        name="route_and_sum",
    )(block, gate, up, down, order, select, back)


def ragged_attend(queries, cache, ids, bounds, base, factor):
    slots, heads, width = queries.shape
    blocks = cache.shape[1] // KEY_BLOCK
    cuts = list(zip(KEY_CUTS[:-1], KEY_CUTS[1:]))

    def kernel(ids_ref, bounds_ref, base_ref, q_ref, kv_ref, num_ref, den_ref):
        j = pl.program_id(0)

        @pl.when(j == 0)
        def _():
            num_ref[...] = jnp.zeros_like(num_ref)
            den_ref[...] = jnp.zeros_like(den_ref)

        found = []
        for i, (low, high) in enumerate(cuts):
            size = high - low
            kv = kv_ref[:, low:high]
            who = [ids_ref[(j * len(cuts) + i) * WINDOW + w] for w in range(WINDOW)]
            some = jnp.concatenate([q_ref[r] for r in who], axis=0)
            scores = factor * jnp.dot(some, kv, preferred_element_type=jnp.float32)
            places = (
                base_ref[0]
                + j * KEY_BLOCK
                + low
                + lax.broadcasted_iota(jnp.int32, (heads, size), 1)
            )
            lifted = jnp.exp(scores)
            weights = jnp.concatenate(
                [
                    jnp.where(
                        (places >= bounds_ref[r]) & (places < bounds_ref[slots + r]),
                        lifted[w * heads : (w + 1) * heads],
                        0.0,
                    )
                    for w, r in enumerate(who)
                ],
                axis=0,
            ).astype(jnp.bfloat16)
            num = lax.dot_general(
                weights,
                kv[:LATENT],
                (((1,), (1,)), ((), ())),
                preferred_element_type=jnp.float32,
            )
            wide = weights.astype(jnp.float32)
            den = sum(wide[:, k : k + 128] for k in range(0, size, 128))
            found.append((who, num, den))
        for who, num, den in found:
            for w, r in enumerate(who):
                rows = slice(w * heads, (w + 1) * heads)
                num_ref[r] += num[rows]
                den_ref[r] += den[rows]

    return pl.pallas_call(
        kernel,
        out_shape=[
            jax.ShapeDtypeStruct((slots, heads, LATENT), jnp.float32),
            jax.ShapeDtypeStruct((slots, heads, 128), jnp.float32),
        ],
        grid_spec=pltpu.PrefetchScalarGridSpec(
            num_scalar_prefetch=3,
            grid=(blocks,),
            in_specs=[
                pl.BlockSpec((slots, heads, width), lambda j, *_: (0, 0, 0)),
                pl.BlockSpec((width, KEY_BLOCK), lambda j, *_: (0, j)),
            ],
            out_specs=[
                pl.BlockSpec((slots, heads, LATENT), lambda j, *_: (0, 0, 0)),
                pl.BlockSpec((slots, heads, 128), lambda j, *_: (0, 0, 0)),
            ],
        ),
        compiler_params=pltpu.CompilerParams(vmem_limit_bytes=VMEM_LIMIT),
        name="ragged_attend",
    )(ids, bounds, base, queries, cache)


def pick_rows(chosen, values):
    return jnp.dot(
        chosen.astype(jnp.bfloat16), values, preferred_element_type=jnp.float32
    ).astype(values.dtype)


def direct_body(
    hidden,
    attn_gain,
    w_query,
    w_latent,
    w_key_up,
    w_value_up,
    w_out,
    latent_cache,
    cache_lengths,
    request_slot,
    ffn_gain,
    w_router,
    routes,
    expert_gate,
    expert_up,
    expert_down,
):
    f32, bf16 = jnp.float32, jnp.bfloat16
    rows, part = hidden.shape
    peers = lax.axis_size("tok")
    each = rows // peers
    local_heads = w_key_up.shape[0]
    expert_count = w_router.shape[1]
    head = lax.axis_index("head")
    tok = lax.axis_index("tok")
    ids = jnp.arange(rows, dtype=jnp.int32)

    owner = request_slot // rows
    earlier = (owner[None, :] == owner[:, None]) & (ids[None, :] < ids[:, None])
    send_place = owner * each + jnp.sum(earlier.astype(jnp.int32), axis=1)
    placed = ids[:, None] == send_place[None, :]
    route_mask = jnp.max(
        (routes[:, :, None] == jnp.arange(expert_count, dtype=jnp.int32)).astype(jnp.int32), axis=1
    )
    meta = jnp.concatenate(
        [
            (request_slot % rows)[:, None],
            (cache_lengths // 64)[:, None],
            (cache_lengths % 64)[:, None],
            route_mask,
        ],
        axis=1,
    ).astype(bf16)
    meta = jnp.pad(meta, ((0, 0), (0, 128 // each - meta.shape[1])))
    sent_meta = jnp.dot(placed.astype(bf16), meta, preferred_element_type=f32)
    blocks = pick_rows(placed, hidden).reshape(peers, each * part // 128, 128)
    wide, meta = to_owners(
        blocks, sent_meta.astype(jnp.int32).reshape(peers, 1, 128), 0
    )
    wide = wide.reshape(2, rows, part)
    meta = meta.reshape(rows, 128 // each)[:, : 3 + expert_count]
    slot, lengths = meta[:, 0], meta[:, 1] * 64 + meta[:, 2]
    mask = meta[:, 3:]
    starts = jnp.sum(jnp.where(slot[None, :] < slot[:, None], lengths[None, :], 0), axis=1)
    full = jnp.concatenate([wide[0], wide[1]], axis=1).astype(f32)
    mine = lax.dynamic_index_in_dim(wide, head, 0, keepdims=False)

    inv_attn = lax.rsqrt(jnp.mean(full * full, axis=1, keepdims=True) + NORM_EPS)
    normed = (full * inv_attn * attn_gain).astype(bf16)
    normed_part = lax.dynamic_slice_in_dim(normed, head * part, part, 1)
    compressed = jnp.dot(normed_part, w_latent, preferred_element_type=f32)
    queries = jnp.dot(normed, w_query, preferred_element_type=f32).astype(bf16)
    queries = queries.reshape(rows, local_heads, NOPE + ROPE)
    absorbed = jnp.einsum(
        "bhn,hnl->bhl", queries[:, :, :NOPE], w_key_up, preferred_element_type=f32
    ).astype(bf16)
    turned = rotate_pairs(queries[:, :, NOPE:].astype(f32), lengths).astype(bf16)
    probes = jnp.concatenate([absorbed, turned], axis=2)
    far_probes, far_compressed = swap_pair([probes, compressed], 1)
    compressed = compressed + far_compressed
    latent_new = compressed[:, :LATENT]
    latent_new = latent_new * lax.rsqrt(
        jnp.mean(latent_new * latent_new, axis=1, keepdims=True) + NORM_EPS
    )
    new_entry = jnp.concatenate(
        [latent_new, rotate_pairs(compressed[:, LATENT:], lengths)], axis=1
    ).astype(bf16)
    factor = (NOPE + ROPE) ** (-0.5)
    self_score = factor * jnp.einsum(
        "bhc,bc->bh", probes, new_entry, preferred_element_type=f32
    )
    self_weight = jnp.exp(self_score).astype(bf16).astype(f32)

    key_rows = latent_cache.shape[0]
    block_starts = (
        head * key_rows
        + jnp.arange(0, key_rows, KEY_BLOCK, dtype=jnp.int32)[:, None]
        + jnp.array(KEY_CUTS[:-1], jnp.int32)
    ).reshape(-1)
    ends = starts + lengths
    first = jnp.sum((ends[None, :] <= block_starts[:, None]).astype(jnp.int32), axis=1)
    first = jnp.minimum(first, rows - WINDOW)
    window = first[:, None] + jnp.arange(WINDOW, dtype=jnp.int32)
    window_ids = jnp.sum(
        jnp.where(window[:, :, None] == slot[None, None, :], ids[None, None, :], 0), axis=2
    )
    numerator, denominator = ragged_attend(
        jnp.concatenate([probes, far_probes], axis=1),
        latent_cache.T,
        window_ids.reshape(-1).astype(jnp.int32),
        jnp.concatenate([starts, ends]).astype(jnp.int32),
        (head * key_rows).reshape(1).astype(jnp.int32),
        factor,
    )
    denominator = jnp.sum(denominator, axis=2)
    far_num, far_den = swap_pair(
        [
            numerator[:, local_heads:].astype(bf16).reshape(rows * local_heads, LATENT),
            denominator[:, local_heads:].reshape(rows * local_heads // 128, 128),
        ],
        2,
    )
    total_num = (
        numerator[:, :local_heads]
        + far_num.reshape(rows, local_heads, LATENT).astype(f32)
        + self_weight[:, :, None] * new_entry[:, None, :LATENT].astype(f32)
    )
    total_den = denominator[:, :local_heads] + far_den.reshape(rows, local_heads) + self_weight
    mixed = (total_num / total_den[:, :, None]).astype(bf16)
    head_out = jnp.einsum("bhl,hld->bhd", mixed, w_value_up, preferred_element_type=f32)
    head_out = head_out.astype(bf16).reshape(rows, local_heads * NOPE)
    piece = jnp.dot(head_out, w_out, preferred_element_type=f32)
    kept = lax.dynamic_slice_in_dim(piece, head * part, part, 1)
    given = lax.dynamic_slice_in_dim(piece, (1 - head) * part, part, 1)
    (far_piece,) = swap_pair([given], 3)
    attended = (mine.astype(f32) + (kept + far_piece)).astype(bf16)

    attended_wide = attended.astype(f32)
    gained = (attended_wide * ffn_gain).astype(bf16)
    squares = jnp.sum(attended_wide * attended_wide, axis=1, keepdims=True)
    logit_part = jnp.dot(gained, w_router, preferred_element_type=f32)
    notes = jnp.concatenate([squares, logit_part], axis=1)
    high = notes.astype(bf16)
    low = (notes - high.astype(f32)).astype(bf16)
    notes = jnp.concatenate([high, low, mask.astype(bf16)], axis=1)
    notes = jnp.pad(notes, ((0, 0), (0, 128 - notes.shape[1])))
    half = rows // 2
    layers = peers // 4
    every = jnp.arange(half * peers, dtype=jnp.int32)
    c_, y_, z_ = (
        every // (half * peers // 2),
        every // (half * layers) % 2,
        every // half % layers,
    )
    inner = every % half
    source = inner // each * rows + (z_ * 4 + y_ * 2 + c_) * each + inner % each
    order = (source[:, None] == every[None, :]).astype(bf16)
    count = 1 + expert_count
    line = jnp.arange(128, dtype=jnp.int32)[:, None]
    lane = jnp.arange(128, dtype=jnp.int32)[None, :]
    held = lane < expert_count
    select = jnp.concatenate(
        [
            held & ((line == 1 + lane) | (line == count + 1 + lane)),
            held & (line == 2 * count + lane),
            ((line == 0) | (line == count)) & (lane >= 0),
        ],
        axis=1,
    ).astype(bf16)
    back = jnp.concatenate([attended, new_entry], axis=1)
    back = jnp.pad(back, ((0, 0), (0, 2 * part - back.shape[1])))
    summed, back = route_and_sum(
        jnp.concatenate([gained, notes], axis=1),
        expert_gate[0].T,
        expert_up[0].T,
        expert_down[0],
        order,
        select,
        back.reshape(peers, each * 2 * part // 128, 128),
        peers,
        4,
    )
    mixed_back = jnp.concatenate([back.reshape(rows, 2 * part), summed.reshape(rows, part)], axis=1)
    final = pick_rows(placed.T, mixed_back)
    return (
        final[:, part : part + LATENT + ROPE],
        final[:, :part],
        final[:, 2 * part :],
    )


def solution(mesh):
    in_specs = (
        P("tok", "head"),
        P(),
        P(None, "head"),
        P("head", None),
        P("head", None, None),
        P("head", None, None),
        P("head", None),
        P(("tok", "head"), None),
        P("tok"),
        P("tok"),
        P("head"),
        P("head", None),
        P("tok", None),
        P("tok", None, "head"),
        P("tok", None, "head"),
        P("tok", "head", None),
    )
    out_specs = (P("tok", None), P("tok", "head"), P("tok", "head"))
    chosen = direct_body if (mesh.shape["tok"], mesh.shape["head"]) == (16, 2) else body
    return jax.shard_map(chosen, mesh=mesh, in_specs=in_specs, out_specs=out_specs, check_vma=False)
```

```python
import jax
import jax.numpy as jnp
from jax import lax
from jax.experimental import pallas as pl
from jax.experimental.pallas import tpu as pltpu
from jax.sharding import PartitionSpec as P

D = 2048
NOPE = 128
ROPE = 64
LATENT = 512


NORM_EPS = 1e-06


def rotate_pairs(values, places):
    halfway = values.shape[-1] // 2
    freqs = 10000.0 ** (-jnp.arange(halfway, dtype=jnp.float32) / halfway)
    angles = places.astype(jnp.float32).reshape(places.shape + (1,) * (values.ndim - 1)) * freqs
    cosine = jnp.cos(angles)
    sine = jnp.sin(angles)
    first_half = values[..., :halfway]
    second_half = values[..., halfway:]
    return jnp.concatenate(
        [first_half * cosine - second_half * sine, first_half * sine + second_half * cosine],
        axis=-1,
    )


def owner_attend(all_heads, owner_lengths, latent_cache, head_index, factor):
    slot_rows = all_heads.shape[0]
    total_heads = all_heads.shape[1]
    probe_width = all_heads.shape[2]
    key_rows = latent_cache.shape[0]
    starts = jnp.cumsum(owner_lengths) - owner_lengths
    places = head_index * key_rows + jnp.arange(key_rows, dtype=jnp.int32)
    inside = (places[None, :] >= starts[:, None]) & (
        places[None, :] < (starts + owner_lengths)[:, None]
    )
    scores = factor * jnp.einsum(
        "qc,pc->qp",
        all_heads.reshape(slot_rows * total_heads, probe_width),
        latent_cache,
        preferred_element_type=jnp.float32,
    )
    scores = scores.reshape(slot_rows, total_heads, key_rows)
    weights = jnp.where(inside[:, None, :], jnp.exp(scores), 0.0).astype(jnp.bfloat16)
    numerator = jnp.einsum(
        "khp,pl->khl", weights, latent_cache[:, :LATENT], preferred_element_type=jnp.float32
    )
    denominator = jnp.sum(weights.astype(jnp.float32), axis=2)
    return (numerator, denominator)


def body(
    hidden,
    attn_gain,
    w_query,
    w_latent,
    w_key_up,
    w_value_up,
    w_out,
    latent_cache,
    cache_lengths,
    request_slot,
    ffn_gain,
    w_router,
    routes,
    expert_gate,
    expert_up,
    expert_down,
):
    local_rows = hidden.shape[0]
    quarter_width = hidden.shape[1]
    local_heads = w_key_up.shape[0]
    peer_count = lax.axis_size("tok")
    head_index = lax.axis_index("head")
    tok_index = lax.axis_index("tok")
    row_ids = jnp.arange(local_rows, dtype=jnp.int32)
    gathered = lax.all_gather(hidden, "head", axis=1, tiled=True)
    widened = gathered.astype(jnp.float32)
    inv_attn = lax.rsqrt(jnp.mean(widened * widened, axis=1, keepdims=True) + NORM_EPS)
    normed_attn = (widened * inv_attn * attn_gain).astype(jnp.bfloat16)
    normed_part = lax.dynamic_slice_in_dim(
        normed_attn, head_index * quarter_width, quarter_width, 1
    )
    compressed = lax.psum(
        jnp.dot(normed_part, w_latent, preferred_element_type=jnp.float32), "head"
    )
    latent_new = compressed[:, :LATENT]
    latent_new = latent_new * lax.rsqrt(
        jnp.mean(latent_new * latent_new, axis=1, keepdims=True) + NORM_EPS
    )
    new_entry = jnp.concatenate(
        [latent_new, rotate_pairs(compressed[:, LATENT:], cache_lengths)], axis=1
    ).astype(jnp.bfloat16)
    queries = jnp.dot(normed_attn, w_query, preferred_element_type=jnp.float32).astype(jnp.bfloat16)
    queries = queries.reshape(local_rows, local_heads, NOPE + ROPE)
    absorbed = jnp.einsum(
        "bhn,hnl->bhl", queries[:, :, :NOPE], w_key_up, preferred_element_type=jnp.float32
    ).astype(jnp.bfloat16)
    turned = rotate_pairs(queries[:, :, NOPE:].astype(jnp.float32), cache_lengths).astype(
        jnp.bfloat16
    )
    probes = jnp.concatenate([absorbed, turned], axis=2)
    factor = (NOPE + ROPE) ** (-0.5)
    self_score = factor * jnp.einsum(
        "bhc,bc->bh", probes, new_entry, preferred_element_type=jnp.float32
    )
    self_weight = jnp.exp(self_score).astype(jnp.bfloat16).astype(jnp.float32)
    per_owner = max(1, local_rows // peer_count)
    buffer_rows = peer_count * per_owner
    buffer_ids = jnp.arange(buffer_rows, dtype=jnp.int32)
    dest_owner = request_slot // local_rows
    earlier_same = (dest_owner[None, :] == dest_owner[:, None]) & (
        row_ids[None, :] < row_ids[:, None]
    )
    send_place = dest_owner * per_owner + jnp.sum(earlier_same.astype(jnp.int32), axis=1)
    all_probes, all_slots, all_lengths = (
        lax.all_gather(probes, "tok", axis=0, tiled=True),
        lax.all_gather(request_slot, "tok", axis=0, tiled=True),
        lax.all_gather(cache_lengths, "tok", axis=0, tiled=True),
    )
    total_rows = all_slots.shape[0]
    slot_hit = all_slots[None, :] == (tok_index * local_rows + row_ids)[:, None]
    request_at = jnp.sum(
        jnp.where(slot_hit, jnp.arange(total_rows, dtype=jnp.int32)[None, :], 0), axis=1
    )
    owner_probes = all_probes[request_at]
    owner_lengths = all_lengths[request_at]
    owned_here = (
        (all_slots // local_rows == tok_index).astype(jnp.int32).reshape(peer_count, local_rows)
    )
    prior_count = (jnp.cumsum(owned_here, axis=1) - owned_here).reshape(total_rows)
    back_index = request_at // local_rows * per_owner + prior_count[request_at]
    all_heads = lax.all_gather(owner_probes, "head", axis=1, tiled=True)
    numerator, denominator = owner_attend(
        all_heads, owner_lengths, latent_cache, head_index, factor
    )
    group_num, group_den = (
        lax.psum_scatter(numerator, "head", scatter_dimension=1, tiled=True),
        lax.psum_scatter(denominator, "head", scatter_dimension=1, tiled=True),
    )
    at_place = buffer_ids[:, None] == back_index[None, :]
    slot_of_place = jnp.sum(jnp.where(at_place, row_ids[None, :], 0), axis=1) + local_rows * (
        1 - jnp.max(at_place.astype(jnp.int32), axis=1)
    )
    padded_num = jnp.concatenate(
        [group_num, jnp.zeros((1, local_heads, LATENT), jnp.float32)], axis=0
    )
    padded_den = jnp.concatenate([group_den, jnp.zeros((1, local_heads), jnp.float32)], axis=0)
    got_num, got_den = (
        lax.all_to_all(
            padded_num[slot_of_place].reshape(peer_count, per_owner, local_heads, LATENT),
            "tok",
            split_axis=0,
            concat_axis=0,
            tiled=True,
        ),
        lax.all_to_all(
            padded_den[slot_of_place].reshape(peer_count, per_owner, local_heads),
            "tok",
            split_axis=0,
            concat_axis=0,
            tiled=True,
        ),
    )
    back_num = got_num.reshape(buffer_rows, local_heads, LATENT)
    back_den = got_den.reshape(buffer_rows, local_heads)
    total_num = back_num[send_place] + self_weight[:, :, None] * new_entry[:, None, :LATENT].astype(
        jnp.float32
    )
    total_den = back_den[send_place] + self_weight
    mixed_latent = (total_num / total_den[:, :, None]).astype(jnp.bfloat16)
    head_out = jnp.einsum(
        "bhl,hld->bhd", mixed_latent, w_value_up, preferred_element_type=jnp.float32
    ).astype(jnp.bfloat16)
    head_out = head_out.reshape(local_rows, local_heads * NOPE)
    attn_piece = lax.psum_scatter(
        jnp.dot(head_out, w_out, preferred_element_type=jnp.float32),
        "head",
        scatter_dimension=1,
        tiled=True,
    )
    attended = (hidden.astype(jnp.float32) + attn_piece).astype(jnp.bfloat16)
    attended_wide = attended.astype(jnp.float32)
    gained = (attended_wide * ffn_gain).astype(jnp.bfloat16)
    squares, logit_part = lax.psum(
        (
            jnp.sum(attended_wide * attended_wide, axis=1),
            jnp.dot(gained, w_router, preferred_element_type=jnp.float32),
        ),
        "head",
    )
    inv_ffn = lax.rsqrt(squares / D + NORM_EPS)
    logits = logit_part * inv_ffn[:, None]
    normed_ffn = (attended_wide * ffn_gain * inv_ffn[:, None]).astype(jnp.bfloat16)
    expert_count = w_router.shape[1]
    route_count = routes.shape[1]
    expert_ids = jnp.arange(expert_count, dtype=jnp.int32)
    named = routes[:, :, None] == expert_ids[None, None, :]
    picked = jnp.sum(jnp.where(named, logits[:, None, :], 0.0), axis=2)
    lifted = jnp.exp(picked)
    route_weight = lifted / jnp.sum(lifted, axis=1, keepdims=True)
    struck = jnp.max(named.astype(jnp.int32), axis=1)
    earlier_hits = jnp.cumsum(struck, axis=0) - struck
    capacity = min(local_rows, max(2, 2 * local_rows * route_count // expert_count))
    route_place = routes * capacity + jnp.take_along_axis(earlier_hits, routes, axis=1)
    slot_total = expert_count * capacity
    slot_ids = jnp.arange(slot_total, dtype=jnp.int32)
    filled = route_place[None, :, :] == slot_ids[:, None, None]
    source_token = jnp.sum(
        jnp.where(filled, row_ids[None, :, None], 0), axis=(1, 2)
    ) + local_rows * (1 - jnp.max(filled.astype(jnp.int32), axis=(1, 2)))
    full_rows = lax.all_gather(normed_ffn, "head", axis=1, tiled=True)
    padded_rows = jnp.concatenate(
        [full_rows, jnp.zeros((1, full_rows.shape[1]), jnp.bfloat16)], axis=0
    )
    arrived = lax.all_to_all(
        padded_rows[source_token].reshape(expert_count, capacity, full_rows.shape[1]),
        "tok",
        split_axis=0,
        concat_axis=0,
        tiled=True,
    )
    expert_in = arrived.reshape(peer_count * capacity, full_rows.shape[1])
    gate_value = jnp.dot(expert_in, expert_gate[0], preferred_element_type=jnp.float32)
    up_value = jnp.dot(expert_in, expert_up[0], preferred_element_type=jnp.float32)
    activity = (jax.nn.silu(gate_value) * up_value).astype(jnp.bfloat16)
    expert_share = lax.psum_scatter(
        jnp.dot(activity, expert_down[0], preferred_element_type=jnp.float32).astype(jnp.bfloat16),
        "head",
        scatter_dimension=1,
        tiled=True,
    )
    returned = lax.all_to_all(
        expert_share.reshape(peer_count, capacity, quarter_width),
        "tok",
        split_axis=0,
        concat_axis=0,
        tiled=True,
    )
    chosen_rows = returned.reshape(slot_total, quarter_width)[route_place]
    expert_mix = jnp.sum(route_weight[:, :, None] * chosen_rows.astype(jnp.float32), axis=1).astype(
        jnp.bfloat16
    )
    return (new_entry, attended, expert_mix)


MESH_ID = pl.DeviceIdType.MESH
KEY_BLOCK = 1664
KEY_CUTS = (0, 384, 768, 1152, 1536, 1664)
WINDOW = 4
VMEM_LIMIT = 48 * 1024 * 1024
ROUTE_VMEM_LIMIT = 60 * 1024 * 1024


def meet(partners):
    barrier = pltpu.get_barrier_semaphore()
    for partner in partners:
        pl.semaphore_signal(barrier, inc=1, device_id=partner, device_id_type=MESH_ID)
    pl.semaphore_wait(barrier, len(partners))


def in_vmem(count):
    return [pl.BlockSpec(memory_space=pltpu.VMEM)] * count


def swap_pair(arrays, number):
    count = len(arrays)

    def kernel(*refs):
        ins, outs = refs[:count], refs[count : 2 * count]
        send_sem, recv_sem = refs[2 * count :]
        partner = (lax.axis_index("tok"), 1 - lax.axis_index("head"))
        meet([partner])
        copies = []
        for i in range(count):
            copy = pltpu.make_async_remote_copy(
                src_ref=ins[i],
                dst_ref=outs[i],
                send_sem=send_sem.at[i],
                recv_sem=recv_sem.at[i],
                device_id=partner,
                device_id_type=MESH_ID,
            )
            copy.start()
            copies.append(copy)
        for copy in copies:
            copy.wait()

    return pl.pallas_call(
        kernel,
        out_shape=[jax.ShapeDtypeStruct(a.shape, a.dtype) for a in arrays],
        in_specs=in_vmem(count),
        out_specs=in_vmem(count),
        scratch_shapes=[pltpu.SemaphoreType.DMA((count,)), pltpu.SemaphoreType.DMA((count,))],
        compiler_params=pltpu.CompilerParams(
            collective_id=number, has_side_effects=True, vmem_limit_bytes=VMEM_LIMIT
        ),
        name=f"swap_pair_{number}",
    )(*arrays)


def to_owners(blocks, notes, number):
    peers = blocks.shape[0]

    def kernel(src, src_notes, out, out_notes, send_sem, recv_sem, pass_sem, note_sem, own_sem):
        tok, head = lax.axis_index("tok"), lax.axis_index("head")
        partner = (tok, 1 - head)
        others = [lax.rem(tok + d, peers) for d in range(1, peers)]
        meet([partner] + [(there, head) for there in others])

        def remote(source, dest, first, second, target):
            return pltpu.make_async_remote_copy(
                src_ref=source,
                dst_ref=dest,
                send_sem=first,
                recv_sem=second,
                device_id=target,
                device_id_type=MESH_ID,
            )

        sends = []
        for i, there in enumerate(others):
            sends.append(
                remote(
                    src.at[there],
                    out.at[head, tok],
                    send_sem.at[i],
                    recv_sem.at[head, tok],
                    (there, head),
                )
            )
            sends[-1].start()
        sends.append(
            remote(
                src.at[tok], out.at[head, tok], pass_sem.at[0], recv_sem.at[head, tok], partner
            )
        )
        sends[-1].start()
        for i, there in enumerate(others):
            sends.append(
                remote(
                    src_notes.at[there],
                    out_notes.at[tok],
                    send_sem.at[peers + i],
                    note_sem.at[tok],
                    (there, head),
                )
            )
            sends[-1].start()
        own = [
            pltpu.make_async_copy(src.at[tok], out.at[head, tok], own_sem.at[0]),
            pltpu.make_async_copy(src_notes.at[tok], out_notes.at[tok], own_sem.at[1]),
        ]
        for copy in own:
            copy.start()
        for i, there in enumerate(others):
            spot = out.at[head, there]
            remote(spot, spot, send_sem.at[0], recv_sem.at[head, there], partner).wait_recv()
            sends.append(
                remote(spot, spot, pass_sem.at[1 + i], recv_sem.at[head, there], partner)
            )
            sends[-1].start()
        for there in [tok] + others:
            spot = out.at[1 - head, there]
            remote(spot, spot, send_sem.at[0], recv_sem.at[1 - head, there], partner).wait_recv()
        for there in others:
            spot = out_notes.at[there]
            remote(spot, spot, send_sem.at[0], note_sem.at[there], partner).wait_recv()
        for copy in sends:
            copy.wait_send()
        for copy in own:
            copy.wait()

    return pl.pallas_call(
        kernel,
        out_shape=[
            jax.ShapeDtypeStruct((2,) + blocks.shape, blocks.dtype),
            jax.ShapeDtypeStruct(notes.shape, notes.dtype),
        ],
        in_specs=in_vmem(2),
        out_specs=in_vmem(2),
        scratch_shapes=[
            pltpu.SemaphoreType.DMA((2 * peers,)),
            pltpu.SemaphoreType.DMA((2, peers)),
            pltpu.SemaphoreType.DMA((peers,)),
            pltpu.SemaphoreType.DMA((peers,)),
            pltpu.SemaphoreType.DMA((2,)),
        ],
        compiler_params=pltpu.CompilerParams(
            collective_id=number, has_side_effects=True, vmem_limit_bytes=VMEM_LIMIT
        ),
        name="to_owners",
    )(blocks, notes)


def route_and_sum(block, gate, up, down, order, select, back, peers, number):
    rows, width = block.shape
    half = rows // 2
    layers = peers // 4
    part = width - 128
    units, full = gate.shape
    some = rows * peers // 2

    def kernel(
        src, gate_any, up_any, down_any, order_ref, select_ref, back_src, result, back_out,
        out, gate_ref, up_ref, down_ref, terms, got_core, kept, got_first, mid, got_second,
        last, got_z, send_sem, recv_sem, own_sem, weight_sem, sum_sends, sum_recvs,
        back_sends, back_recvs,
    ):
        tok, x = lax.axis_index("tok"), lax.axis_index("head")
        z, y, core = tok // 4, (tok // 2) % 2, tok % 2

        def place(z_, y_, core_):
            return z_ * 4 + y_ * 2 + core_

        across_x = (tok, 1 - x)
        across_y = (place(z, 1 - y, core), x)
        sibling = (place(z, y, 1 - core), x)
        along_z = [(place(lax.rem(z + d, layers), y, core), x) for d in range(1, layers)]
        others = [lax.rem(tok + d, peers) for d in range(1, peers)]
        meet([across_x] + [(there, x) for there in others])

        def spot(z_, y_, core_, x_, h):
            start = place(z_, y_, core_) * rows + (h or 0) * half
            size = rows if h is None else half
            return out.at[
                pl.ds(pl.multiple_of(start, half), size),
                pl.ds(pl.multiple_of(x_ * width, 128), width),
            ]

        def slot(z_, y_, core_, x_, h):
            return (place(z_, y_, core_) * 2 + x_) * 2 + (h or 0)

        sends = []

        def push(target, z_, y_, core_, x_, h, fresh=False):
            dst = spot(z_, y_, core_, x_, h)
            copy = pltpu.make_async_remote_copy(
                src_ref=src if fresh else dst,
                dst_ref=dst,
                send_sem=send_sem.at[len(sends)],
                recv_sem=recv_sem.at[slot(z_, y_, core_, x_, h)],
                device_id=target,
                device_id_type=MESH_ID,
            )
            copy.start()
            sends.append(copy)

        def land(z_, y_, core_, x_, h):
            dst = spot(z_, y_, core_, x_, h)
            pltpu.make_async_remote_copy(
                src_ref=dst,
                dst_ref=dst,
                send_sem=send_sem.at[0],
                recv_sem=recv_sem.at[slot(z_, y_, core_, x_, h)],
                device_id=sibling,
                device_id_type=MESH_ID,
            ).wait_recv()

        turns = [1, 3, 2][: layers - 1]
        for d in turns:
            push(along_z[d - 1], z, y, core, x, None, True)
        for target in (across_x, across_y, sibling):
            push(target, z, y, core, x, None, True)
        own = pltpu.make_async_copy(src, spot(z, y, core, x, None), own_sem.at[0])
        own.start()
        weights = [
            pltpu.make_async_copy(a, b, weight_sem.at[i])
            for i, (a, b) in enumerate(
                [(gate_any, gate_ref), (up_any, up_ref), (down_any, down_ref)]
            )
        ]
        for copy in weights:
            copy.start()

        def second(z_):
            land(z_, 1 - y, core, x, None)
            push(across_x, z_, 1 - y, core, x, 0)
            land(z_, y, core, 1 - x, None)
            push(across_y, z_, y, core, 1 - x, 1)
            push(sibling, z_, 1 - y, core, x, None)
            push(sibling, z_, y, core, 1 - x, None)

        def third(z_):
            land(z_, 1 - y, core, 1 - x, 0)
            land(z_, 1 - y, core, 1 - x, 1)
            push(sibling, z_, 1 - y, core, 1 - x, None)

        for d in turns:
            z_ = lax.rem(z + d, layers)
            land(z_, y, core, x, None)
            for target in (across_x, across_y, sibling):
                push(target, z_, y, core, x, None)
            if d == turns[0]:
                second(z)
        near = z + 1 - 2 * (z % 2)
        pairs = [(z, near), (lax.rem(z + 2, layers), lax.rem(near + 2, layers))]
        second(near)
        for z_ in pairs[1]:
            second(z_)

        def across(a, b):
            return lax.dot_general(
                a, b, (((1,), (1,)), ((), ())), preferred_element_type=jnp.float32
            )

        def product(a, b):
            return jnp.dot(a, b, preferred_element_type=jnp.float32)

        def expert(a, group):
            at = pl.ds(pl.multiple_of(group * some, some), some)
            left, right = out[at, part:width], out[at, width + part :]
            logits = product(left, select_ref[:, :128]) + product(right, select_ref[:, :128])
            named = product(left, select_ref[:, 128:256])
            squares = product(left, select_ref[:, 256:]) + product(right, select_ref[:, 256:])
            inv_ffn = lax.rsqrt(squares / full + NORM_EPS)
            lifted = jnp.where(named > 0.5, jnp.exp(logits * inv_ffn), 0.0)
            lane = lax.broadcasted_iota(jnp.int32, (some, 128), 1)
            mine = jnp.sum(jnp.where(lane == tok, lifted, 0.0), axis=1, keepdims=True)
            weight = mine / jnp.sum(lifted, axis=1, keepdims=True)
            inv_ffn = inv_ffn[:, :1]
            first, last = out[at, :part], out[at, width : width + part]
            gate_value = across(first, gate_ref[:, :part]) + across(last, gate_ref[:, part:])
            gate_value = gate_value * inv_ffn
            up_value = across(first, up_ref[:, :part]) + across(last, up_ref[:, part:])
            up_value = up_value * (inv_ffn * weight)
            activity = gate_value / (1.0 + jnp.exp(-gate_value)) * up_value
            moved = product(order_ref[...], activity.astype(out.dtype)).astype(out.dtype)
            for k in range(0, full, 512):
                piece = product(moved, down_ref[:, k : k + 512]).astype(terms.dtype)
                terms[a, :, :, k : k + 512] = piece.reshape(peers, half, 512)

        def copy_to(target, source, dest, index, landing=None):
            copy = pltpu.make_async_remote_copy(
                src_ref=source,
                dst_ref=dest,
                send_sem=sum_sends.at[index],
                recv_sem=sum_recvs.at[index if landing is None else landing],
                device_id=target,
                device_id_type=MESH_ID,
            )
            copy.start()
            return copy

        def columns(x_):
            return pl.ds(pl.multiple_of(x_ * part, 128), part)

        def total(first, second):
            return first.astype(jnp.float32) + second.astype(jnp.float32)

        def hand_over(a):
            return [
                copy_to(
                    sibling,
                    terms.at[a, pl.ds(((1 - core) * 2 + y_) * layers, layers)],
                    got_core.at[a, y_],
                    2 * a + g,
                )
                for g, y_ in enumerate((1 - y, y))
            ]

        def fold_core(a, y_):
            @pl.loop(0, layers)
            def _(z_):
                kept[a, y_, z_] = total(
                    terms[a, (core * 2 + y_) * layers + z_], got_core[a, y_, z_]
                ).astype(kept.dtype)

        def bring(pair):
            for z_ in pair:
                third(z_)
            for z_ in pair:
                for y_ in (y, 1 - y):
                    for x_ in (x, 1 - x):
                        land(z_, y_, 1 - core, x_, None)

        bring(pairs[0])
        own.wait()
        for copy in weights:
            copy.wait()
        expert(0, z // 2)
        cores = [hand_over(0)]
        bring(pairs[1])
        first_x = []
        for g, y_ in enumerate((1 - y, y)):
            cores[0][g].wait_recv()
            fold_core(0, y_)
            first_x.append(
                copy_to(
                    across_x,
                    kept.at[0, y_, slice(None), slice(None), columns(1 - x)],
                    got_first.at[0, slice(None), slice(None), pl.ds(g * part, part)],
                    5 + g,
                )
            )
        expert(1, 1 - z // 2)
        cores.append(hand_over(1))
        backs = []
        for i, there in enumerate(others):
            copy = pltpu.make_async_remote_copy(
                src_ref=back_src.at[there],
                dst_ref=back_out.at[tok],
                send_sem=back_sends.at[i],
                recv_sem=back_recvs.at[tok],
                device_id=(there, x),
                device_id_type=MESH_ID,
            )
            copy.start()
            backs.append(copy)
        own_back = pltpu.make_async_copy(back_src.at[tok], back_out.at[tok], own_sem.at[1])
        own_back.start()
        cores[1][0].wait_recv()
        fold_core(1, 1 - y)
        first_y = copy_to(across_y, kept.at[1, 1 - y], got_first.at[1], 4)
        first_x[0].wait_recv()

        @pl.loop(0, layers)
        def _(z_):
            mid[0, z_] = total(
                kept[0, 1 - y, z_, :, columns(x)], got_first[0, z_, :, :part]
            ).astype(mid.dtype)

        second_y = copy_to(across_y, mid.at[0], got_second.at[0], 7)
        cores[1][1].wait_recv()
        fold_core(1, y)
        first_x[1].wait_recv()
        zs = []

        def send_z(a):
            group = (z // 2) if a == 0 else (1 - z // 2)
            for d in range(1, layers):
                z_ = lax.rem(z + d, layers)
                zs.append(
                    copy_to(
                        along_z[d - 1],
                        last.at[a, z_],
                        got_z.at[group, d - 1],
                        9 + a * layers + d - 1,
                        9 + group * layers + d - 1,
                    )
                )

        first_y.wait_recv()

        @pl.loop(0, layers)
        def _(z_):
            mid[1, z_] = total(
                kept[1, y, z_, :, columns(1 - x)], got_first[1, z_, :, columns(1 - x)]
            ).astype(mid.dtype)

        second_x = copy_to(across_x, mid.at[1], got_second.at[1], 8)
        second_y.wait_recv()

        @pl.loop(0, layers)
        def _(z_):
            last[0, z_] = (
                total(kept[0, y, z_, :, columns(x)], got_first[0, z_, :, part:])
                + got_second[0, z_].astype(jnp.float32)
            ).astype(last.dtype)

        send_z(0)
        second_x.wait_recv()

        @pl.loop(0, layers)
        def _(z_):
            last[1, z_] = (
                total(kept[1, y, z_, :, columns(x)], got_first[1, z_, :, columns(x)])
                + got_second[1, z_].astype(jnp.float32)
            ).astype(last.dtype)

        send_z(1)
        for copy in zs:
            copy.wait_recv()
        for a in range(2):
            group = (z // 2) if a == 0 else (1 - z // 2)
            acc = last[a, z].astype(jnp.float32)
            for d in range(1, layers):
                acc = acc + got_z[group, d - 1].astype(jnp.float32)
            result[group] = acc.astype(result.dtype)
        for there in others:
            spot_back = back_out.at[there]
            pltpu.make_async_remote_copy(
                src_ref=spot_back,
                dst_ref=spot_back,
                send_sem=back_sends.at[0],
                recv_sem=back_recvs.at[there],
                device_id=sibling,
                device_id_type=MESH_ID,
            ).wait_recv()
        own_back.wait()
        for copy in (
            sends + backs + cores[0] + cores[1] + first_x + [first_y, second_y, second_x] + zs
        ):
            copy.wait_send()

    kind = block.dtype
    return pl.pallas_call(
        kernel,
        out_shape=[
            jax.ShapeDtypeStruct((2, half, part), kind),
            jax.ShapeDtypeStruct(back.shape, kind),
        ],
        in_specs=in_vmem(1) + [pl.BlockSpec(memory_space=pl.ANY)] * 3 + in_vmem(3),
        out_specs=in_vmem(2),
        scratch_shapes=[
            pltpu.VMEM((rows * peers, 2 * width), block.dtype),
            pltpu.VMEM((units, full), block.dtype),
            pltpu.VMEM((units, full), block.dtype),
            pltpu.VMEM((units, full), block.dtype),
            pltpu.VMEM((2, peers, half, full), kind),
            pltpu.VMEM((2, 2, layers, half, full), kind),
            pltpu.VMEM((2, 2, layers, half, full), kind),
            pltpu.VMEM((2, layers, half, full), kind),
            pltpu.VMEM((2, layers, half, part), kind),
            pltpu.VMEM((2, layers, half, part), kind),
            pltpu.VMEM((2, layers, half, part), kind),
            pltpu.VMEM((2, layers - 1, half, part), kind),
            pltpu.SemaphoreType.DMA((64,)),
            pltpu.SemaphoreType.DMA((4 * peers,)),
            pltpu.SemaphoreType.DMA((2,)),
            pltpu.SemaphoreType.DMA((3,)),
            pltpu.SemaphoreType.DMA((9 + 2 * layers,)),
            pltpu.SemaphoreType.DMA((9 + 2 * layers,)),
            pltpu.SemaphoreType.DMA((peers,)),
            pltpu.SemaphoreType.DMA((peers,)),
        ],
        compiler_params=pltpu.CompilerParams(
            collective_id=number, has_side_effects=True, vmem_limit_bytes=ROUTE_VMEM_LIMIT
        ),
        name="route_and_sum",
    )(block, gate, up, down, order, select, back)


def ragged_attend(queries, cache, ids, bounds, base, factor):
    slots, heads, width = queries.shape
    blocks = cache.shape[1] // KEY_BLOCK
    cuts = list(zip(KEY_CUTS[:-1], KEY_CUTS[1:]))

    def kernel(ids_ref, bounds_ref, base_ref, q_ref, kv_ref, num_ref, den_ref):
        j = pl.program_id(0)

        @pl.when(j == 0)
        def _():
            num_ref[...] = jnp.zeros_like(num_ref)
            den_ref[...] = jnp.zeros_like(den_ref)

        found = []
        for i, (low, high) in enumerate(cuts):
            size = high - low
            kv = kv_ref[:, low:high]
            who = [ids_ref[(j * len(cuts) + i) * WINDOW + w] for w in range(WINDOW)]
            some = jnp.concatenate([q_ref[r] for r in who], axis=0)
            scores = factor * jnp.dot(some, kv, preferred_element_type=jnp.float32)
            places = (
                base_ref[0]
                + j * KEY_BLOCK
                + low
                + lax.broadcasted_iota(jnp.int32, (heads, size), 1)
            )
            lifted = jnp.exp(scores)
            weights = jnp.concatenate(
                [
                    jnp.where(
                        (places >= bounds_ref[r]) & (places < bounds_ref[slots + r]),
                        lifted[w * heads : (w + 1) * heads],
                        0.0,
                    )
                    for w, r in enumerate(who)
                ],
                axis=0,
            ).astype(jnp.bfloat16)
            num = lax.dot_general(
                weights,
                kv[:LATENT],
                (((1,), (1,)), ((), ())),
                preferred_element_type=jnp.float32,
            )
            wide = weights.astype(jnp.float32)
            den = sum(wide[:, k : k + 128] for k in range(0, size, 128))
            found.append((who, num, den))
        for who, num, den in found:
            for w, r in enumerate(who):
                rows = slice(w * heads, (w + 1) * heads)
                num_ref[r] += num[rows]
                den_ref[r] += den[rows]

    return pl.pallas_call(
        kernel,
        out_shape=[
            jax.ShapeDtypeStruct((slots, heads, LATENT), jnp.float32),
            jax.ShapeDtypeStruct((slots, heads, 128), jnp.float32),
        ],
        grid_spec=pltpu.PrefetchScalarGridSpec(
            num_scalar_prefetch=3,
            grid=(blocks,),
            in_specs=[
                pl.BlockSpec((slots, heads, width), lambda j, *_: (0, 0, 0)),
                pl.BlockSpec((width, KEY_BLOCK), lambda j, *_: (0, j)),
            ],
            out_specs=[
                pl.BlockSpec((slots, heads, LATENT), lambda j, *_: (0, 0, 0)),
                pl.BlockSpec((slots, heads, 128), lambda j, *_: (0, 0, 0)),
            ],
        ),
        compiler_params=pltpu.CompilerParams(vmem_limit_bytes=VMEM_LIMIT),
        name="ragged_attend",
    )(ids, bounds, base, queries, cache)


def pick_rows(chosen, values):
    return jnp.dot(
        chosen.astype(jnp.bfloat16), values, preferred_element_type=jnp.float32
    ).astype(values.dtype)


def direct_body(
    hidden,
    attn_gain,
    w_query,
    w_latent,
    w_key_up,
    w_value_up,
    w_out,
    latent_cache,
    cache_lengths,
    request_slot,
    ffn_gain,
    w_router,
    routes,
    expert_gate,
    expert_up,
    expert_down,
):
    f32, bf16 = jnp.float32, jnp.bfloat16
    rows, part = hidden.shape
    peers = lax.axis_size("tok")
    each = rows // peers
    local_heads = w_key_up.shape[0]
    expert_count = w_router.shape[1]
    head = lax.axis_index("head")
    tok = lax.axis_index("tok")
    ids = jnp.arange(rows, dtype=jnp.int32)

    owner = request_slot // rows
    earlier = (owner[None, :] == owner[:, None]) & (ids[None, :] < ids[:, None])
    send_place = owner * each + jnp.sum(earlier.astype(jnp.int32), axis=1)
    placed = ids[:, None] == send_place[None, :]
    route_mask = jnp.max(
        (routes[:, :, None] == jnp.arange(expert_count, dtype=jnp.int32)).astype(jnp.int32), axis=1
    )
    meta = jnp.concatenate(
        [
            (request_slot % rows)[:, None],
            (cache_lengths // 64)[:, None],
            (cache_lengths % 64)[:, None],
            route_mask,
        ],
        axis=1,
    ).astype(bf16)
    meta = jnp.pad(meta, ((0, 0), (0, 128 // each - meta.shape[1])))
    sent_meta = jnp.dot(placed.astype(bf16), meta, preferred_element_type=f32)
    blocks = pick_rows(placed, hidden).reshape(peers, each * part // 128, 128)
    wide, meta = to_owners(
        blocks, sent_meta.astype(jnp.int32).reshape(peers, 1, 128), 0
    )
    wide = wide.reshape(2, rows, part)
    meta = meta.reshape(rows, 128 // each)[:, : 3 + expert_count]
    slot, lengths = meta[:, 0], meta[:, 1] * 64 + meta[:, 2]
    mask = meta[:, 3:]
    starts = jnp.sum(jnp.where(slot[None, :] < slot[:, None], lengths[None, :], 0), axis=1)
    full = jnp.concatenate([wide[0], wide[1]], axis=1).astype(f32)
    mine = lax.dynamic_index_in_dim(wide, head, 0, keepdims=False)

    inv_attn = lax.rsqrt(jnp.mean(full * full, axis=1, keepdims=True) + NORM_EPS)
    normed = (full * inv_attn * attn_gain).astype(bf16)
    normed_part = lax.dynamic_slice_in_dim(normed, head * part, part, 1)
    compressed = jnp.dot(normed_part, w_latent, preferred_element_type=f32)
    queries = jnp.dot(normed, w_query, preferred_element_type=f32).astype(bf16)
    queries = queries.reshape(rows, local_heads, NOPE + ROPE)
    absorbed = jnp.einsum(
        "bhn,hnl->bhl", queries[:, :, :NOPE], w_key_up, preferred_element_type=f32
    ).astype(bf16)
    turned = rotate_pairs(queries[:, :, NOPE:].astype(f32), lengths).astype(bf16)
    probes = jnp.concatenate([absorbed, turned], axis=2)
    far_probes, far_compressed = swap_pair([probes, compressed], 1)
    compressed = compressed + far_compressed
    latent_new = compressed[:, :LATENT]
    latent_new = latent_new * lax.rsqrt(
        jnp.mean(latent_new * latent_new, axis=1, keepdims=True) + NORM_EPS
    )
    new_entry = jnp.concatenate(
        [latent_new, rotate_pairs(compressed[:, LATENT:], lengths)], axis=1
    ).astype(bf16)
    factor = (NOPE + ROPE) ** (-0.5)
    self_score = factor * jnp.einsum(
        "bhc,bc->bh", probes, new_entry, preferred_element_type=f32
    )
    self_weight = jnp.exp(self_score).astype(bf16).astype(f32)

    key_rows = latent_cache.shape[0]
    block_starts = (
        head * key_rows
        + jnp.arange(0, key_rows, KEY_BLOCK, dtype=jnp.int32)[:, None]
        + jnp.array(KEY_CUTS[:-1], jnp.int32)
    ).reshape(-1)
    ends = starts + lengths
    first = jnp.sum((ends[None, :] <= block_starts[:, None]).astype(jnp.int32), axis=1)
    first = jnp.minimum(first, rows - WINDOW)
    window = first[:, None] + jnp.arange(WINDOW, dtype=jnp.int32)
    window_ids = jnp.sum(
        jnp.where(window[:, :, None] == slot[None, None, :], ids[None, None, :], 0), axis=2
    )
    numerator, denominator = ragged_attend(
        jnp.concatenate([probes, far_probes], axis=1),
        latent_cache.T,
        window_ids.reshape(-1).astype(jnp.int32),
        jnp.concatenate([starts, ends]).astype(jnp.int32),
        (head * key_rows).reshape(1).astype(jnp.int32),
        factor,
    )
    denominator = jnp.sum(denominator, axis=2)
    far_num, far_den = swap_pair(
        [
            numerator[:, local_heads:].astype(bf16).reshape(rows * local_heads, LATENT),
            denominator[:, local_heads:].reshape(rows * local_heads // 128, 128),
        ],
        2,
    )
    total_num = (
        numerator[:, :local_heads]
        + far_num.reshape(rows, local_heads, LATENT).astype(f32)
        + self_weight[:, :, None] * new_entry[:, None, :LATENT].astype(f32)
    )
    total_den = denominator[:, :local_heads] + far_den.reshape(rows, local_heads) + self_weight
    mixed = (total_num / total_den[:, :, None]).astype(bf16)
    head_out = jnp.einsum("bhl,hld->bhd", mixed, w_value_up, preferred_element_type=f32)
    head_out = head_out.astype(bf16).reshape(rows, local_heads * NOPE)
    piece = jnp.dot(head_out, w_out, preferred_element_type=f32)
    kept = lax.dynamic_slice_in_dim(piece, head * part, part, 1)
    given = lax.dynamic_slice_in_dim(piece, (1 - head) * part, part, 1)
    (far_piece,) = swap_pair([given], 3)
    attended = (mine.astype(f32) + (kept + far_piece)).astype(bf16)

    attended_wide = attended.astype(f32)
    gained = (attended_wide * ffn_gain).astype(bf16)
    squares = jnp.sum(attended_wide * attended_wide, axis=1, keepdims=True)
    logit_part = jnp.dot(gained, w_router, preferred_element_type=f32)
    notes = jnp.concatenate([squares, logit_part], axis=1)
    high = notes.astype(bf16)
    low = (notes - high.astype(f32)).astype(bf16)
    notes = jnp.concatenate([high, low, mask.astype(bf16)], axis=1)
    notes = jnp.pad(notes, ((0, 0), (0, 128 - notes.shape[1])))
    half = rows // 2
    layers = peers // 4
    every = jnp.arange(half * peers, dtype=jnp.int32)
    c_, y_, z_ = (
        every // (half * peers // 2),
        every // (half * layers) % 2,
        every // half % layers,
    )
    inner = every % half
    source = inner // each * rows + (z_ * 4 + y_ * 2 + c_) * each + inner % each
    order = (source[:, None] == every[None, :]).astype(bf16)
    count = 1 + expert_count
    line = jnp.arange(128, dtype=jnp.int32)[:, None]
    lane = jnp.arange(128, dtype=jnp.int32)[None, :]
    held = lane < expert_count
    select = jnp.concatenate(
        [
            held & ((line == 1 + lane) | (line == count + 1 + lane)),
            held & (line == 2 * count + lane),
            ((line == 0) | (line == count)) & (lane >= 0),
        ],
        axis=1,
    ).astype(bf16)
    back = jnp.concatenate([attended, new_entry], axis=1)
    back = jnp.pad(back, ((0, 0), (0, 2 * part - back.shape[1])))
    summed, back = route_and_sum(
        jnp.concatenate([gained, notes], axis=1),
        expert_gate[0].T,
        expert_up[0].T,
        expert_down[0],
        order,
        select,
        back.reshape(peers, each * 2 * part // 128, 128),
        peers,
        4,
    )
    back = back.reshape(rows, 2 * part)
    return (
        pick_rows(placed.T, back[:, part : part + LATENT + ROPE]),
        pick_rows(placed.T, back[:, :part]),
        pick_rows(placed.T, summed.reshape(rows, part)),
    )


def solution(mesh):
    in_specs = (
        P("tok", "head"),
        P(),
        P(None, "head"),
        P("head", None),
        P("head", None, None),
        P("head", None, None),
        P("head", None),
        P(("tok", "head"), None),
        P("tok"),
        P("tok"),
        P("head"),
        P("head", None),
        P("tok", None),
        P("tok", None, "head"),
        P("tok", None, "head"),
        P("tok", "head", None),
    )
    out_specs = (P("tok", None), P("tok", "head"), P("tok", "head"))
    chosen = direct_body if (mesh.shape["tok"], mesh.shape["head"]) == (16, 2) else body
    return jax.shard_map(chosen, mesh=mesh, in_specs=in_specs, out_specs=out_specs, check_vma=False)
```
